32 devices in a mesh: dp: 8 (over y, x, core), fsdp: 4 (over z).
Axes of the slice: x: 2, y: 2, z: 4, core: 2. Of those that a mesh axis runs over, the one named last changes fastest.
Arguments:
- layer_in: bfloat16 [32, 1024, 1024], P(('dp', 'fsdp')), may hold values from -16 to 16
- first_values: bfloat16 [32, 1024, 1024], P(('dp', 'fsdp')), may hold values from -16 to 16
- first_values_grad: float32 [32, 1024, 1024], P(('dp', 'fsdp')), may hold values from -6 to 6
- cotangent: bfloat16 [32, 1024, 1024], P(('dp', 'fsdp')), may hold values from -6 to 6
- doc_lengths: int32 [32, 8], P(('dp', 'fsdp')), may hold values from 1 to 512, 1024 in all within a row
- norm1_gain: bfloat16 [1024], P('fsdp'), may hold values from 0.5 to 1.5
- w_query: bfloat16 [1024, 1024], P('fsdp'), may hold values from -0.1875 to 0.1875
- w_key: bfloat16 [1024, 1024], P('fsdp'), may hold values from -0.1875 to 0.1875
- w_value: bfloat16 [1024, 1024], P('fsdp'), may hold values from -0.1875 to 0.1875
- w_out: bfloat16 [1024, 1024], P('fsdp'), may hold values from -0.75 to 0.75
- norm2_gain: bfloat16 [1024], P('fsdp'), may hold values from 0.5 to 1.5
- w_gate: bfloat16 [1024, 2816], P('fsdp'), may hold values from -0.1875 to 0.1875
- w_up: bfloat16 [1024, 2816], P('fsdp'), may hold values from -0.1875 to 0.1875
- w_down: bfloat16 [2816, 1024], P('fsdp'), may hold values from -0.109375 to 0.109375
Outputs:
- layer_out: bfloat16 [32, 1024, 1024], P(('dp', 'fsdp'))
- input_grad: float32 [32, 1024, 1024], P(('dp', 'fsdp'))
- first_values_grad_out: float32 [32, 1024, 1024], P(('dp', 'fsdp'))
- grad_norm1_gain: float32 [1024], P('fsdp')
- grad_w_query: float32 [1024, 1024], P('fsdp')
- grad_w_key: float32 [1024, 1024], P('fsdp')
- grad_w_value: float32 [1024, 1024], P('fsdp')
- grad_w_out: float32 [1024, 1024], P('fsdp')
- grad_norm2_gain: float32 [1024], P('fsdp')
- grad_w_gate: float32 [1024, 2816], P('fsdp')
- grad_w_up: float32 [1024, 2816], P('fsdp')
- grad_w_down: float32 [2816, 1024], P('fsdp')
- value_norms: float32 [2], replicated
The draws below stay inside these ranges and needn't reach their ends.
Inputs may be any that keep to these rules, and one draw needn't show every extreme that they name: `doc_lengths`: each row's entries sum to 1024; some entry of each row equals 512.
All inputs are finite; a program needn't handle non-finite values.
Results may differ from the reference program's by a relative error of at most 0.02.
Values may be sent and summed in bfloat16 or wider, within the bound.
No kernel may reach another device: no remote copies, remote signals or barrier semaphores. Data moves between devices by JAX's collectives and lax.ppermute only.
A program may use at most 384 MiB of HBM per device.

```python
import math
import jax
import jax.numpy as jnp
import numpy as np
from jax import lax

D = 1024
HEADS = 16
HEAD_DIM = 64
FF = 2816
ROW_LEN = 1024
DOCS = 8
BLOCK = 512
ROWS = 32


def draw_first_values(key, part):
    key = jax.random.fold_in(key, 11)
    scale_key, noise_key = jax.random.split(key)
    logs = jax.random.uniform(scale_key, (ROWS, 1, 1), jnp.float32, math.log(0.5), math.log(2.0))
    noise = jnp.clip(jax.random.normal(noise_key, (ROWS, ROW_LEN, D), jnp.float32), -6.0, 6.0)
    return (noise * jnp.exp(logs)).astype(jnp.bfloat16)


def channel_marks(pick_key, sign_key):
    chosen = jax.random.permutation(pick_key, D)[:4]
    marks = jnp.sum((jnp.arange(D)[None, :] == chosen[:, None]).astype(jnp.float32), 0)
    signs = (2 * jax.random.randint(sign_key, (D,), 0, 2) - 1).astype(jnp.float32)
    return (marks, signs)


def draw_layer_in(key, part):
    key = jax.random.fold_in(key, 5)
    pick_key, sign_key, size_key, noise_key = jax.random.split(key, 4)
    marks, signs = channel_marks(pick_key, sign_key)
    sizes = jax.random.uniform(size_key, (ROWS, ROW_LEN, 1), jnp.float32, 4.0, 8.0)
    noise = jnp.clip(jax.random.normal(noise_key, (ROWS, ROW_LEN, D), jnp.float32), -6.0, 6.0)
    outlier = signs[None, None, :] * sizes + 0.5 * noise
    values = marks[None, None, :] * outlier + (1.0 - marks[None, None, :]) * noise
    return values.astype(jnp.bfloat16)


def block_scale(own_key, extent, shards, smallest, high):
    level = 1.0
    for dim, shards_of in shards:
        draws = jax.random.uniform(jax.random.fold_in(jax.random.fold_in(own_key, 6), dim), (shards_of,), jnp.float32, smallest / len(shards), high / len(shards))
        level = level * jnp.repeat(jnp.exp(draws), extent[dim] // shards_of).reshape((-1,) + (1,) * (len(extent) - 1 - dim))
    return level


def split_up(amount, total, most, skew):
    weights = [(1 << 20) // math.isqrt(grade ** skew) + 1 for grade in range(2, amount + 1)]
    surplus, counts = total - most - (amount - 1), [1] * (amount - 1)
    while surplus > 0:
        movable = [i for i in range(amount - 1) if counts[i] < most]
        mass, remaining = sum([weights[i] for i in movable]), surplus
        for i in movable:
            more = min(most - counts[i], max(1, remaining * weights[i] // mass), surplus)
            counts[i] = counts[i] + more
            surplus = surplus - more
    return np.array([most] + counts)


def ragged(rng, count, total, bound, lean):
    if count == 2:
        one = jax.random.randint(rng, (), max(1, total - bound), min(bound, total - 1) + 1)
        return jnp.stack([one, total - one])
    tallies = jnp.asarray(split_up(count, total, bound, lean), jnp.int32)
    couples = (count - 1) // 2
    donor, taker = tallies[1:1 + 2 * couples:2], tallies[2:2 + 2 * couples:2]
    room = jnp.minimum(donor - 1, bound - taker)
    passed = jax.random.randint(jax.random.fold_in(rng, 1), (couples,), 0, 1 << 20) % (room + 1)
    tallies = tallies.at[1:1 + 2 * couples:2].set(donor - passed).at[2:2 + 2 * couples:2].set(taker + passed)
    return tallies[jax.random.permutation(jax.random.fold_in(rng, 2), count)]


def normal_values(key, shape, deviation, most, shards=(), held_as=jnp.bfloat16):
    values = jax.random.normal(key, shape, jnp.float32) * deviation
    if len(shards) > 0:
        values = block_scale(key, shape, shards, -0.22, 0.18) * values
    return jnp.clip(values, min=-most, max=most).astype(held_as)


def setup_inputs(seed: int = 0) -> dict:
    key_of = jax.random.split(jax.random.key(seed), 15)
    return {
        "layer_in": draw_layer_in(jax.random.fold_in(key_of[14], 71), 0),
        "first_values": draw_first_values(jax.random.fold_in(key_of[14], 71), 0),
        "first_values_grad": normal_values(key_of[2], (ROWS, ROW_LEN, D), 1.0, 6.0, ((0, 32),), jnp.float32),
        "cotangent": normal_values(key_of[3], (ROWS, ROW_LEN, D), 1.0, 6.0, ((0, 32),)),
        "doc_lengths": jax.vmap(lambda own: ragged(own, DOCS, ROW_LEN, ROW_LEN // 2, 2))(jax.random.split(key_of[4], ROWS)).reshape((ROWS, DOCS)).astype(jnp.int32),
        "norm1_gain": jnp.clip(1.0 + 0.1 * jax.random.normal(key_of[5], (D,), jnp.float32), 0.5, 1.5).astype(jnp.bfloat16),
        "w_query": normal_values(key_of[6], (D, D), D ** -0.5, 0.1875, ((0, 4),)),
        "w_key": normal_values(key_of[7], (D, D), D ** -0.5, 0.1875, ((0, 4),)),
        "w_value": normal_values(key_of[8], (D, D), D ** -0.5, 0.1875, ((0, 4),)),
        "w_out": normal_values(key_of[9], (D, D), (D // 16) ** -0.5, 0.75, ((0, 4),)),
        "norm2_gain": jnp.clip(1.0 + 0.1 * jax.random.normal(key_of[10], (D,), jnp.float32), 0.5, 1.5).astype(jnp.bfloat16),
        "w_gate": normal_values(key_of[11], (D, FF), D ** -0.5, 0.1875, ((0, 4),)),
        "w_up": normal_values(key_of[12], (D, FF), D ** -0.5, 0.1875, ((0, 4),)),
        "w_down": normal_values(key_of[13], (FF, D), FF ** -0.5, 0.109375, ((0, 4),)),
    }


EPS = 1e-06
HI = lax.Precision.HIGHEST

@jax.custom_vjp
def low(v):
    return lax.optimization_barrier(v.astype(jnp.bfloat16)).astype(jnp.float32)

@jax.custom_vjp
def low_back(v):
    return v

def low_keep(v):
    return (low(v), None)

def low_pass(kept, grad):
    return (grad,)

def back_keep(v):
    return (v, None)

def back_low(kept, grad):
    return (low(grad),)
low.defvjp(low_keep, low_pass)
low_back.defvjp(back_keep, back_low)

def layout(lengths):
    position = jnp.arange(ROW_LEN, dtype=jnp.int32)
    ends = jnp.cumsum(lengths).astype(jnp.int32)
    seg = lax.optimization_barrier(jnp.sum((position[:, None] >= ends[None, :]).astype(jnp.int32), 1)).astype(jnp.int32)
    starts = ends - lengths
    onehot = seg[:, None] == jnp.arange(DOCS, dtype=jnp.int32)[None, :]
    first = lax.optimization_barrier(jnp.sum(jnp.where(onehot, starts[None, :], 0), 1)).astype(jnp.int32)
    rel = (position - first).astype(jnp.float32)
    inverse = 10000.0 ** (-jnp.arange(HEAD_DIM // 2, dtype=jnp.float32) * 2.0 / HEAD_DIM)
    angle = rel[:, None] * inverse[None, :]
    keep = (seg < DOCS - 1).astype(jnp.float32)
    return (jnp.cos(angle), jnp.sin(angle), seg, position, keep)

def rotate(t, cosv, sinv):
    half = HEAD_DIM // 2
    first, second = (t[..., :half], t[..., half:])
    c = cosv[:, None, :]
    s = sinv[:, None, :]
    return jnp.concatenate([first * c - second * s, second * c + first * s], -1)

def attend(query, key, value, seg, position):
    blocks = ROW_LEN // BLOCK
    query_blocks = query.reshape(blocks, BLOCK, HEADS, HEAD_DIM)
    seg_blocks = seg.reshape(blocks, BLOCK)
    pos_blocks = position.reshape(blocks, BLOCK)

    @jax.checkpoint
    def one_block(item):
        qblock, sblock, pblock = item
        scores = jnp.einsum('qhd,khd->hqk', qblock, key, precision=HI) * 0.125
        allowed = (sblock[:, None] == seg[None, :]) & (pblock[:, None] >= position[None, :])
        scores = low_back(jnp.where(allowed[None], scores, -1e+30))
        top = lax.optimization_barrier(jnp.max(scores, -1, keepdims=True))
        expo = jnp.exp(scores - top)
        probs = expo / lax.optimization_barrier(jnp.sum(expo, -1, keepdims=True))
        return jnp.einsum('hqk,khd->qhd', low(probs), value, precision=HI)
    result = lax.map(one_block, (query_blocks, seg_blocks, pos_blocks))
    return result.reshape(ROW_LEN, HEADS, HEAD_DIM)

def layer(params, xrow, vrow, cosv, sinv, seg, position, keep):
    g1, wq, wk, wv, wo, g2, wg, wu, wd = params
    rinv1 = lax.rsqrt(lax.optimization_barrier(jnp.mean(xrow * xrow, -1, keepdims=True)) + EPS)
    h1 = low(xrow * rinv1 * g1)
    query = low_back(jnp.dot(h1, wq, precision=HI)).reshape(ROW_LEN, HEADS, HEAD_DIM)
    key = low_back(jnp.dot(h1, wk, precision=HI)).reshape(ROW_LEN, HEADS, HEAD_DIM)
    query = low(rotate(query, cosv, sinv))
    key = low(rotate(key, cosv, sinv))
    own = jnp.dot(h1, wv, precision=HI)
    mixed_flat = low(low_back(0.5 * own + 0.5 * vrow))
    mixed = mixed_flat.reshape(ROW_LEN, HEADS, HEAD_DIM)
    attn = attend(query, key, mixed, seg, position).reshape(ROW_LEN, D)
    attn = low(low_back(attn * keep[:, None]))
    r1 = xrow + low_back(jnp.dot(attn, wo, precision=HI))
    rinv2 = lax.rsqrt(lax.optimization_barrier(jnp.mean(r1 * r1, -1, keepdims=True)) + EPS)
    h2 = low(r1 * rinv2 * g2)
    gate = low_back(jnp.dot(h2, wg, precision=HI))
    up = low_back(jnp.dot(h2, wu, precision=HI))
    hidden = low(jax.nn.silu(gate) * up)
    out = r1 + low_back(jnp.dot(hidden, wd, precision=HI))
    return (out, jnp.sum(mixed_flat * mixed_flat))

def reference(layer_in, first_values, first_values_grad, cotangent, doc_lengths, norm1_gain, w_query, w_key, w_value, w_out, norm2_gain, w_gate, w_up, w_down):
    params = tuple((w.astype(jnp.float32) for w in (norm1_gain, w_query, w_key, w_value, w_out, norm2_gain, w_gate, w_up, w_down)))

    def step(carry, item):
        grads, sums = carry
        xrow, vrow, grow, dyrow, lrow = item
        cosv, sinv, seg, position, keep = layout(lrow)
        xf = xrow.astype(jnp.float32)
        vf = vrow.astype(jnp.float32)

        def forward(prm, xin, vin):
            return layer(prm, xin, vin, cosv, sinv, seg, position, keep)
        out, pull, mixed_sq = jax.vjp(forward, params, xf, vf, has_aux=True)
        dparams, dx, dv = pull(dyrow.astype(jnp.float32))
        grads = jax.tree.map(lambda a, b: a + b, grads, dparams)
        sums = sums + jnp.stack([jnp.sum(vf * vf), mixed_sq])
        return ((grads, sums), (out.astype(jnp.bfloat16), dx, grow + dv))
    start = (tuple((jnp.zeros_like(p) for p in params)), jnp.zeros((2,), jnp.float32))
    (grads, sums), (outs, dxs, dvs) = lax.scan(step, start, (layer_in, first_values, first_values_grad, cotangent, doc_lengths))
    norms = sums / (ROWS * ROW_LEN * D)
    return (outs, dxs, dvs, grads[0], grads[1], grads[2], grads[3], grads[4], grads[5], grads[6], grads[7], grads[8], norms)
```

```python
import jax
import jax.numpy as jnp
from jax import lax
from jax.experimental import pallas as pl
from jax.experimental.pallas import tpu as pltpu
from jax.sharding import PartitionSpec as P

HEADS = 16
HEAD_DIM = 64
EPS = 1e-06
NEG = -1e30
QB = 256
G = 32
L = 128
bf16 = jnp.bfloat16
f32 = jnp.float32
ANY = pl.BlockSpec(memory_space=pl.ANY)
SMEM = pl.BlockSpec(memory_space=pltpu.SMEM)


def params(mib=58):
    return pltpu.CompilerParams(vmem_limit_bytes=mib * 2**20)


def cost(flops, moved):
    return pl.CostEstimate(flops=int(flops), bytes_accessed=int(moved), transcendentals=0)


def shape(dims, dtype=bf16):
    return jax.ShapeDtypeStruct(dims, dtype)


def nt(a, b):
    return lax.dot_general(a, b, (((1,), (1,)), ((), ())), preferred_element_type=f32)


def nn(a, b):
    return lax.dot_general(a, b, (((1,), (0,)), ((), ())), preferred_element_type=f32)


def tn(a, b):
    return lax.dot_general(a, b, (((0,), (0,)), ((), ())), preferred_element_type=f32)


def fast_mesh(dp, fsdp, shard_rows):
    return dp == 8 and fsdp == 4 and shard_rows == 8 * G


def row_pieces(w, count):
    return w.reshape(count, G, w.shape[1] // L, L).transpose(0, 2, 1, 3)


def column_pieces(w, count):
    return w.reshape(w.shape[0] // G, G, count, L).transpose(2, 0, 1, 3)


def dp_swap(x, bit):
    return lax.ppermute(x, "dp", [(i, i ^ bit) for i in range(lax.axis_size("dp"))])


def after(x, *first):
    return lax.optimization_barrier((x, first))[0]


def fsdp_shift(x, step):
    size = lax.axis_size("fsdp")
    return lax.ppermute(x, "fsdp", [(i, (i + step) % size) for i in range(size)])


class Gather:
    def __init__(self, mine, extra=None):
        self.count = mine.shape[0]
        self.extras = None
        sent = mine if extra is None else jnp.concatenate([mine, extra[None]])
        far = [fsdp_shift(sent, s) for s in (1, 2, 3)]
        if extra is not None:
            self.extras = [extra] + [x[self.count] for x in far]
        self.start = jnp.stack([x[: self.count] for x in far])

    def near(self, *gate):
        self.start = after(self.start, *gate)
        self.x, self.y = dp_swap(self.start, 2), dp_swap(self.start, 4)

    def corner(self, *gate):
        cut = self.count // 2
        self.c1 = dp_swap(after(self.x[:, :cut], *gate), 4)
        self.c2 = dp_swap(after(self.y[:, cut:], *gate), 2)

    def core(self, *gate):
        self.other = [dp_swap(after(a, *gate), 1) for a in (self.start, self.x, self.y)]

    def core_corner(self, *gate):
        self.other += [dp_swap(after(a, *gate), 1) for a in (self.c1, self.c2)]

    def arrays(self):
        return [self.start, self.x, self.y, self.c1, self.c2] + self.other


def piece_sources(count):
    cut = count // 2
    found = []
    for core in range(2):
        for i, (mask, low, size) in enumerate(
            ((0, 0, count), (2, 0, count), (4, 0, count), (6, 0, cut), (6, cut, count - cut))
        ):
            found.append((5 * core + i, mask | core, low, size))
    return found


class Group:
    def __init__(self, tensors, arrays, whole):
        self.tensors, self.arrays, self.whole = tensors, list(arrays), whole

    def specs(self):
        return [ANY] * len(self.arrays)

    def fetch(self, index, refs, pos, scratch, sem):
        if self.whole:
            pltpu.make_async_copy(refs[index], scratch, sem).start()
            return
        z, d = pos[0], pos[1]
        at = sum(t[0] for t in self.tensors[:index])
        blocks, by_rows = self.tensors[index]

        def target(shard, piece, low, size):
            if by_rows:
                return scratch.at[pl.ds(low, size), shard * 8 + piece]
            return scratch.at[piece, pl.ds(shard * blocks + low, size)]

        for piece in range(8):
            pltpu.make_async_copy(
                refs[0].at[piece, pl.ds(at, blocks)], target(z, piece, 0, blocks), sem
            ).start()
        for array, mask, low, size in piece_sources(sum(t[0] for t in self.tensors)):
            begin, end = max(at, low), min(at + blocks, low + size)
            if end <= begin:
                continue
            for s in range(3):
                pltpu.make_async_copy(
                    refs[1 + array].at[s, pl.ds(begin - low, end - begin)],
                    target(lax.rem(z + 3 - s, 4), d ^ mask, begin - at, end - begin),
                    sem,
                ).start()


def wait_all(scratch, sem):
    pltpu.make_async_copy(scratch, scratch, sem).wait()


def two(w, i):
    rows = w.shape[1] * w.shape[2]
    return jnp.concatenate([w[2 * i].reshape(rows, L), w[2 * i + 1].reshape(rows, L)], 1)


def swap_halves(t):
    lane = lax.broadcasted_iota(jnp.int32, t.shape, 1) % 64
    return jnp.where(lane < 32, pltpu.roll(t, 96, 1), pltpu.roll(t, 32, 1))


def qkv_body(group, pos, x_ref, v1_ref, gain_ref, cos_ref, sin_ref, *rest):
    count = len(group.arrays)
    w_refs = rest[:count]
    q_ref, k_ref, v_ref, h_ref, ht_ref, sums_ref, *rest = rest[count:]
    outs, (wq, wk, wv, sem) = rest[:3], rest[3:]
    step = pl.program_id(0)
    length = x_ref.shape[0]

    @pl.when(step == 0)
    def _():
        for i, w in enumerate((wq, wk, wv)):
            group.fetch(i, w_refs, pos, w, sem.at[i])
        sums_ref[...] = jnp.zeros_like(sums_ref)
        for i in range(length // QB):
            rows = slice(i * QB, (i + 1) * QB)
            x = x_ref[rows, :].astype(f32)
            n1 = x * lax.rsqrt(jnp.mean(x * x, -1, keepdims=True) + EPS)
            h = n1 * gain_ref[...]
            h_ref[rows, :] = h.astype(bf16)
            ht_ref[:, :, :, rows] = h.T.astype(bf16).reshape(ht_ref.shape[:3] + (QB,))
        wait_all(wq, sem.at[0])
        wait_all(wk, sem.at[1])
        wait_all(wv, sem.at[2])
        for i, w in enumerate((wq, wk, wv)):
            pltpu.make_async_copy(w, outs[i], sem.at[3 + i]).start()

    cos, sin = cos_ref[...], sin_ref[...]
    h = h_ref[...]

    def rope(t):
        return jnp.concatenate(
            [t[:, i * L : (i + 1) * L] * cos + swap_halves(t[:, i * L : (i + 1) * L]) * sin for i in range(2)], 1
        )

    def pair(w):
        rows = w.shape[1] * G
        return jnp.concatenate([w[2 * step].reshape(rows, L), w[2 * step + 1].reshape(rows, L)], 1)

    q_ref[...] = (rope(nn(h, pair(wq))).astype(bf16).astype(f32) * 0.125).astype(bf16)
    k_ref[...] = rope(nn(h, pair(wk))).astype(bf16)
    v1 = v1_ref[...].astype(f32)
    vm = (0.5 * nn(h, pair(wv)) + 0.5 * v1).astype(bf16)
    v_ref[...] = vm
    vm = vm.astype(f32)
    total_1 = jnp.sum((v1 * v1).reshape(length // 8, 8, 2 * L), 0)
    total_2 = jnp.sum((vm * vm).reshape(length // 8, 8, 2 * L), 0)
    sums_ref[0] += total_1
    sums_ref[1] += total_2

    @pl.when(step == pl.num_programs(0) - 1)
    def _():
        for i, w in enumerate((wq, wk, wv)):
            pltpu.make_async_copy(w, outs[i], sem.at[3 + i]).wait()


def qkv(pos, x, v1, gain, cos_w, sin_w, group):
    length, width = x.shape
    blocks = width // L
    col = pl.BlockSpec((length, 2 * L), lambda i: (0, i))

    def fixed(*dims):
        return pl.BlockSpec(dims, lambda i: (0,) * len(dims))

    weight = pltpu.VMEM((blocks, width // G, G, L), bf16)
    return pl.pallas_call(
        lambda *refs: qkv_body(group, *refs),
        grid=(blocks // 2,),
        in_specs=[SMEM, fixed(length, width), col, fixed(1, width), fixed(length, L), fixed(length, L)]
        + group.specs(),
        out_specs=[col, col, col, fixed(length, width), fixed(width // G // 2, 2, G, length), fixed(2, 8, 2 * L)] + [ANY] * 3,
        out_shape=[
            shape((length, width)),
            shape((length, width)),
            shape((length, width)),
            shape((length, width)),
            shape((width // G // 2, 2, G, length)),
            shape((2, 8, 2 * L), f32),
        ]
        + [shape((blocks, width // G, G, L))] * 3,
        scratch_shapes=[weight, weight, weight, pltpu.SemaphoreType.DMA((6,))],
        compiler_params=params(),
        cost_estimate=cost(6 * length * width * width, 24 * length * width),
        name="qkv",
    )(pos, x, v1, gain, cos_w, sin_w, *group.arrays)
def half_mask(rows, which):
    lane = lax.broadcasted_iota(jnp.int32, (rows, 128), 1)
    return (lane < 64) if which == 0 else (lane >= 64)


def pick(x, which):
    return jnp.where(half_mask(x.shape[0], which), x, jnp.zeros_like(x))


def attend_fwd_body(q_ref, k_ref, v_ref, end_ref, keep_ref, *rest):
    o_ref, lse_ref, bias = rest[-3:]
    pair = pl.program_id(0)
    length = q_ref.shape[0]
    blocks = length // QB

    @pl.when(pair == 0)
    def _():
        for i in range(blocks):
            size = (i + 1) * QB
            q_at = lax.broadcasted_iota(jnp.int32, (QB, size), 0) + i * QB
            k_at = lax.broadcasted_iota(jnp.int32, (QB, size), 1)
            ok = (q_at >= k_at) & (q_at < end_ref[:, :size])
            bias[i * QB : (i + 1) * QB, :size] = jnp.where(ok, 0.0, NEG)

    lane = lax.broadcasted_iota(jnp.int32, (QB, 128), 1)
    for i in range(blocks):
        rows = slice(i * QB, (i + 1) * QB)
        size = (i + 1) * QB
        outs = []
        old = lse_ref[rows, :]
        for h in range(2):
            s = nt(pick(q_ref[rows, :], h), k_ref[:size, :]) + bias[rows, :size]
            top = jnp.max(s, -1, keepdims=True)
            expo = jnp.exp(s - top)
            total = jnp.sum(expo, -1, keepdims=True)
            outs.append(nn(expo.astype(bf16), v_ref[:size, :]) / total)
            old = jnp.where(lane == 2 * pair + h, top + jnp.log(total), old)
        lse_ref[rows, :] = old
        o = jnp.where(lane < 64, outs[0], outs[1]) * keep_ref[rows, :]
        o_ref[rows, :] = o.astype(bf16)


def attend_fwd(q, k, v, end_row, keep_col, first, pairs, before=None):
    length, width = q.shape
    col = pl.BlockSpec((length, 128), lambda p: (0, p + first))
    return pl.pallas_call(
        attend_fwd_body,
        grid=(pairs,),
        in_specs=[
            col,
            col,
            col,
            pl.BlockSpec((1, length), lambda p: (0, 0)),
            pl.BlockSpec((length, 1), lambda p: (0, 0)),
        ]
        + ([] if before is None else [ANY]),
        out_specs=[col, pl.BlockSpec((length, 128), lambda p: (0, 0))],
        out_shape=[
            jax.ShapeDtypeStruct((length, width), bf16),
            jax.ShapeDtypeStruct((length, 128), f32),
        ],
        scratch_shapes=[pltpu.VMEM((length, length), f32)],
        compiler_params=params(),
        cost_estimate=cost(5 * length * length * width, 16 * length * width),
        input_output_aliases={} if before is None else {5: 0},
        name="attend_fwd",
    )(q, k, v, end_row, keep_col, *([] if before is None else [before]))


def attend_bwd_body(
    q_ref, k_ref, v_ref, do_ref, lse_ref, first_ref, cos_ref, sin_ref, fg_ref, *rest,
):
    dq_ref, dk_ref, dv_ref, fo_ref, bias, dk_acc, dv_acc = rest[-7:]
    pair = pl.program_id(0)
    length = q_ref.shape[0]
    blocks = length // QB

    @pl.when(pair == 0)
    def _():
        for i in range(blocks):
            size = (i + 1) * QB
            k_at = lax.broadcasted_iota(jnp.int32, (size, QB), 0)
            q_at = lax.broadcasted_iota(jnp.int32, (size, QB), 1) + i * QB
            ok = (q_at >= k_at) & (k_at >= first_ref[:, i * QB : (i + 1) * QB])
            bias[:size, i * QB : (i + 1) * QB] = jnp.where(ok, 0.0, NEG)

    k_t = k_ref[...].astype(f32).T.astype(bf16)
    for i in reversed(range(blocks)):
        rows = slice(i * QB, (i + 1) * QB)
        size = (i + 1) * QB
        part_k = None
        part_v = None
        part_q = []
        for h in range(2):
            qh = pick(q_ref[rows, :], h)
            dh = pick(do_ref[rows, :], h)
            lse = lse_ref[pl.ds(2 * pair + h, 1), rows]
            p = jnp.exp(nt(k_ref[:size, :], qh) + bias[:size, rows] - lse)
            dp = nt(v_ref[:size, :], dh)
            delta = jnp.sum(p * dp, 0, keepdims=True)
            ds = (p * (dp - delta)).astype(bf16)
            av = nn(p.astype(bf16), dh)
            ak = nn(ds, qh)
            part_v = av if part_v is None else part_v + av
            part_k = ak if part_k is None else part_k + ak
            part_q.append(nn(k_t[h * 64 : (h + 1) * 64, :size], ds))
        if i == blocks - 1:
            dk_acc[...] = part_k
            dv_acc[...] = part_v
        else:
            dk_acc[:size, :] += part_k
            dv_acc[:size, :] += part_v
        dq = jnp.concatenate(part_q, 0).T * 0.125
        dq = dq * cos_ref[rows, :] + swap_halves(dq) * sin_ref[rows, :]
        dq_ref[rows, :] = dq.astype(bf16)
    dk = dk_acc[...]
    dk_ref[...] = (dk * cos_ref[...] + swap_halves(dk) * sin_ref[...]).astype(bf16)
    dv = dv_acc[...].astype(bf16).astype(f32) * 0.5
    dv_ref[...] = dv.astype(bf16)
    fo_ref[...] = fg_ref[...] + dv


def attend_bwd(q, k, v, do, lse_t, first_row, cos_w, sin_back, fgrad, first, pairs, before=None):
    length, width = q.shape
    col = pl.BlockSpec((length, 128), lambda p: (0, p + first))
    before = [] if before is None else list(before)

    def whole(a):
        return pl.BlockSpec(a.shape, lambda p: (0, 0))

    wide = jax.ShapeDtypeStruct((length, width), bf16)
    return pl.pallas_call(
        attend_bwd_body,
        grid=(pairs,),
        in_specs=[col] * 4 + [whole(lse_t), whole(first_row), whole(cos_w), whole(sin_back), col]
        + [ANY] * len(before),
        out_specs=[col] * 4,
        out_shape=[wide, wide, wide, jax.ShapeDtypeStruct((length, width), f32)],
        scratch_shapes=[
            pltpu.VMEM((length, length), f32),
            pltpu.VMEM((length, 128), f32),
            pltpu.VMEM((length, 128), f32),
        ],
        compiler_params=params(),
        cost_estimate=cost(12 * length * length * width, 24 * length * width),
        input_output_aliases={9 + i: i for i in range(len(before))},
        name="attend_bwd",
    )(q, k, v, do, lse_t, first_row, cos_w, sin_back, fgrad, *before)


def chosen_columns(ref, parity):
    blocks = ref.shape[1] // L
    return jnp.concatenate(
        [ref[:, pl.ds(pl.multiple_of((2 * p + parity) * L, L), L)] for p in range(blocks // 2)], 1
    )


def chosen_rows(ref, parity):
    return ref[:, parity].reshape(ref.shape[0] * G, ref.shape[3])


def wd_rows(wd, t):
    return jnp.concatenate([wd[c, pl.ds(8 * t, 8)].reshape(8 * G, L) for c in range(wd.shape[0])], 1)


def pair_at(w, t):
    rows = w.shape[1] * G
    return jnp.concatenate([w[2 * t].reshape(rows, L), w[2 * t + 1].reshape(rows, L)], 1)


def ffn_up_body(groups, pos, x_ref, o_ref, gain_ref, *rest):
    count = [len(g.arrays) for g in groups]
    refs_1, refs_2 = rest[: count[0]], rest[count[0] : sum(count)]
    (r1_ref, h_ref, ht_ref, hid_ref, ga_ref, ua_ref, wo_ref, wg_ref, wu_ref,
     wo, wg, wu, sem) = rest[sum(count):]
    step = pl.program_id(0)
    length = x_ref.shape[0]

    @pl.when(step == 0)
    def _():
        groups[0].fetch(0, refs_1, pos, wo, sem.at[0])
        groups[0].fetch(1, refs_1, pos, wg, sem.at[1])
        groups[1].fetch(0, refs_2, pos, wu, sem.at[2])
        wait_all(wo, sem.at[0])
        for i in range(length // QB):
            rows = slice(i * QB, (i + 1) * QB)
            r1 = x_ref[rows, :].astype(f32) + jnp.concatenate(
                [nn(o_ref[rows, :], two(wo, c)) for c in range(wo.shape[0] // 2)], 1
            )
            r1_ref[rows, :] = r1
            n2 = r1 * lax.rsqrt(jnp.mean(r1 * r1, -1, keepdims=True) + EPS)
            h = n2 * gain_ref[...]
            h_ref[rows, :] = h.astype(bf16)
            ht_ref[:, :, :, rows] = h.T.astype(bf16).reshape(ht_ref.shape[:3] + (QB,))
        wait_all(wg, sem.at[1])
        wait_all(wu, sem.at[2])
        pltpu.make_async_copy(wo, wo_ref, sem.at[3]).start()
        pltpu.make_async_copy(wg, wg_ref, sem.at[4]).start()
        pltpu.make_async_copy(wu, wu_ref, sem.at[5]).start()

    @pl.when(step > 0)
    def _():
        t = step - 1
        wgt, wut = pair_at(wg, t), pair_at(wu, t)
        for i in range(2):
            rows = slice(i * (length // 2), (i + 1) * (length // 2))
            gate = nn(h_ref[rows, :], wgt)
            up = nn(h_ref[rows, :], wut)
            sigma = 1.0 / (1.0 + jnp.exp(-gate))
            silu = gate * sigma
            hid_ref[rows, :] = (silu * up).astype(bf16)
            ga_ref[rows, :] = (up * (sigma + silu * (1.0 - sigma))).astype(bf16)
            ua_ref[rows, :] = silu.astype(bf16)

    @pl.when(step == pl.num_programs(0) - 1)
    def _():
        pltpu.make_async_copy(wo, wo_ref, sem.at[3]).wait()
        pltpu.make_async_copy(wg, wg_ref, sem.at[4]).wait()
        pltpu.make_async_copy(wu, wu_ref, sem.at[5]).wait()


def once(*dims):
    return pl.BlockSpec(dims, lambda i: (0,) * len(dims), pipeline_mode=pl.Buffered(1))


def ffn_up(pos, x, o, gain, groups, hidden):
    length, width = x.shape
    tiles = hidden // (2 * L)
    col = pl.BlockSpec((length, 2 * L), lambda i: (0, jnp.maximum(i - 1, 0)))
    ht_dims = (width // G // 2, 2, G, length)
    square = (width // L, width // G, G, L)
    wide = (hidden // L, width // G, G, L)
    return pl.pallas_call(
        lambda *refs: ffn_up_body(groups, *refs),
        grid=(1 + tiles,),
        in_specs=[SMEM, once(length, width), once(length, width), once(1, width)]
        + groups[0].specs()
        + groups[1].specs(),
        out_specs=[once(length, width), once(length, width), once(*ht_dims), col, col, col, ANY, ANY, ANY],
        out_shape=[
            shape((length, width), f32),
            shape((length, width)),
            shape(ht_dims),
            shape((length, hidden)),
            shape((length, hidden)),
            shape((length, hidden)),
            shape(square),
            shape(wide),
            shape(wide),
        ],
        scratch_shapes=[
            pltpu.VMEM(square, bf16),
            pltpu.VMEM(wide, bf16),
            pltpu.VMEM(wide, bf16),
            pltpu.SemaphoreType.DMA((6,)),
        ],
        compiler_params=params(),
        cost_estimate=cost(4 * length * width * hidden, 40 * length * width),
        name="ffn_up",
    )(pos, x, o, gain, *groups[0].arrays, *groups[1].arrays)


def ffn_down_body(group, pos, ht_ref, df_ref, hid_ref, ga_ref, ua_ref, *rest):
    count = len(group.arrays)
    dg_ref, du_ref, sg_ref, su_ref, sd_ref, wd_ref, wd, dfs, hts, sem = rest[count:]
    step = pl.program_id(0)
    length = df_ref.shape[0]

    @pl.when(step == 0)
    def _():
        group.fetch(0, rest[:count], pos, wd, sem.at[0])
        other = 1 - lax.rem(pos[1], 2)
        dfs[...] = chosen_columns(df_ref, other)
        hts[...] = chosen_rows(ht_ref, other)
        wait_all(wd, sem.at[0])
        pltpu.make_async_copy(wd, wd_ref, sem.at[1]).start()

    wdt = wd_rows(wd, step)
    for i in range(2):
        rows = slice(i * (length // 2), (i + 1) * (length // 2))
        dhid = nt(df_ref[rows, :], wdt)
        dg_ref[rows, :] = (dhid * ga_ref[rows, :].astype(f32)).astype(bf16)
        du_ref[rows, :] = (dhid * ua_ref[rows, :].astype(f32)).astype(bf16)
    gd = tn(hid_ref[...], dfs[...]).astype(bf16)
    for p in range(4):
        sd_ref[:, p] = gd[:, p * L : (p + 1) * L].reshape(8, G, L)
    for ref, grad in ((sg_ref, dg_ref), (su_ref, du_ref)):
        g = nn(hts[...], grad[...]).astype(bf16)
        for c in range(2):
            ref[:, :, c] = g[:, c * L : (c + 1) * L].reshape(4, 4, G, L)

    @pl.when(step == pl.num_programs(0) - 1)
    def _():
        pltpu.make_async_copy(wd, wd_ref, sem.at[1]).wait()


def ffn_down(pos, ht, df, hid, ga, ua, group):
    length, width = df.shape
    hidden = hid.shape[1]
    col = pl.BlockSpec((length, 2 * L), lambda i: (0, i))
    grad_cols = pl.BlockSpec((4, 4, 2, G, L), lambda i: (0, 0, i, 0, 0))
    grad_rows = pl.BlockSpec((8, 4, G, L), lambda i: (i, 0, 0, 0))
    tall = (width // L, hidden // G, G, L)
    return pl.pallas_call(
        lambda *refs: ffn_down_body(group, *refs),
        grid=(hidden // (2 * L),),
        in_specs=[SMEM, once(*ht.shape), once(length, width), col, col, col] + group.specs(),
        out_specs=[col, col, grad_cols, grad_cols, grad_rows, ANY],
        out_shape=[
            shape((length, hidden)),
            shape((length, hidden)),
            shape((4, 4, hidden // L, G, L)),
            shape((4, 4, hidden // L, G, L)),
            shape((hidden // G, 4, G, L)),
            shape(tall),
        ],
        scratch_shapes=[
            pltpu.VMEM(tall, bf16),
            pltpu.VMEM((length, width // 2), bf16),
            pltpu.VMEM((width // 2, length), bf16),
            pltpu.SemaphoreType.DMA((2,)),
        ],
        compiler_params=params(),
        cost_estimate=cost(5 * length * width * hidden, 60 * length * width),
        name="ffn_down",
    )(pos, ht, df, hid, ga, ua, *group.arrays)


def ffn_back_body(pos, r1_ref, df_ref, keep_ref, gain_ref, wo, dg_ref, du_ref, wg, wu, dr_ref, da_ref, do_ref, acc):
    step = pl.program_id(0)
    length = r1_ref.shape[0]
    both = jnp.concatenate([dg_ref[...], du_ref[...]], 1)
    part = nt(both, jnp.concatenate([two(wg, 0), two(wu, 0)], 1))

    @pl.when(step == 0)
    def _():
        acc[...] = part

    @pl.when(step > 0)
    def _():
        acc[...] += part

    @pl.when(step == pl.num_programs(0) - 1)
    def _():
        for i in range(length // QB):
            rows = slice(i * QB, (i + 1) * QB)
            r1 = r1_ref[rows, :]
            rinv = lax.rsqrt(jnp.mean(r1 * r1, -1, keepdims=True) + EPS)
            n2 = r1 * rinv
            dn = acc[rows, :] * gain_ref[...]
            dr = df_ref[rows, :].astype(f32) + rinv * (dn - n2 * jnp.mean(dn * n2, -1, keepdims=True))
            dr_ref[rows, :] = dr
            da = dr.astype(bf16)
            da_ref[rows, :] = da
            do = nt(da, jnp.concatenate([two(wo, c) for c in range(wo.shape[0] // 2)], 1))
            do_ref[rows, :] = (do * keep_ref[rows, :]).astype(bf16)


def ffn_back(pos, r1, df, keep_col, gain, dgate, dup, wo, wg, wu):
    length, width = r1.shape
    hidden = dgate.shape[1]
    col = pl.BlockSpec((length, 2 * L), lambda i: (0, i))
    weight = pl.BlockSpec((2, width // G, G, L), lambda i: (i, 0, 0, 0))
    return pl.pallas_call(
        ffn_back_body,
        grid=(hidden // (2 * L),),
        in_specs=[SMEM, once(length, width), once(length, width), once(length, 1), once(1, width)]
        + [once(*wo.shape), col, col, weight, weight],
        out_specs=[once(length, width)] * 3,
        out_shape=[shape((length, width), f32), shape((length, width)), shape((length, width))],
        scratch_shapes=[pltpu.VMEM((length, width), f32)],
        compiler_params=params(),
        cost_estimate=cost(4 * length * width * hidden, 40 * length * width),
        name="ffn_back",
    )(pos, r1, df, keep_col, gain, wo, dgate, dup, wg, wu)


def bits(pos):
    d = pos[1]
    return lax.rem(d, 2), lax.rem(d // 2, 2), lax.rem(d // 4, 2)


def ffn_grads_body(pos, ht_ref, df_ref, hid_ref, dg_ref, du_ref, rg_ref, ru_ref, rd_ref,
                   sg, kg, su, ku, sa, ka, sb, kb, dfk, htk, tile, tiled):
    step = pl.program_id(0)
    core, b1, b2 = bits(pos)

    @pl.when(step == 0)
    def _():
        dfk[...] = chosen_columns(df_ref, core)
        htk[...] = chosen_rows(ht_ref, core)

    for send, keep, grad, got, by_x in ((sg, kg, dg_ref, rg_ref, True), (su, ku, du_ref, ru_ref, False)):
        g = nn(htk[...], grad[...])
        for c in range(2):
            tile[:, :, c] = (
                g[:, c * L : (c + 1) * L].reshape(4, 4, G, L) + got[:, :, c].astype(f32)
            ).astype(bf16)
        for i in range(2):
            if by_x:
                send[:, i] = tile[:, 2 * i + 1 - b1]
                keep[:, i] = tile[:, 2 * i + b1]
            else:
                send[:, i] = tile[:, 2 * (1 - b2) + i]
                keep[:, i] = tile[:, 2 * b2 + i]
    gd = tn(hid_ref[...], dfk[...])
    for p in range(4):
        tiled[:, p] = (gd[:, p * L : (p + 1) * L].reshape(8, G, L) + rd_ref[:, p].astype(f32)).astype(bf16)
    middle = pl.num_programs(0) // 2

    @pl.when(step <= middle)
    def _():
        for i in range(2):
            sa[:, i] = tiled[:, 2 * i + 1 - b1]
            ka[:, i] = tiled[:, 2 * i + b1]

    @pl.when(step >= middle)
    def _():
        for i in range(2):
            sb[:, i] = tiled[:, 2 * (1 - b2) + i]
            kb[:, i] = tiled[:, 2 * b2 + i]


def ffn_grads(pos, ht, df, hid, dgate, dup, got):
    length, width = df.shape
    hidden = hid.shape[1]
    tiles = hidden // (2 * L)
    middle = tiles // 2
    col = pl.BlockSpec((length, 2 * L), lambda i: (0, i))
    half = pl.BlockSpec((4, 2, 2, G, L), lambda i: (0, 0, i, 0, 0))
    rows_a = pl.BlockSpec((8, 2, G, L), lambda i: (jnp.minimum(i, middle), 0, 0, 0))
    rows_b = pl.BlockSpec((8, 2, G, L), lambda i: (jnp.maximum(i - middle, 0), 0, 0, 0))
    cols = shape((4, 2, hidden // L, G, L))
    rows = shape((8 * (middle + 1), 2, G, L))
    return pl.pallas_call(
        ffn_grads_body,
        grid=(tiles,),
        in_specs=[
            SMEM,
            once(*ht.shape),
            once(length, width),
            col,
            col,
            col,
            pl.BlockSpec((4, 4, 2, G, L), lambda i: (0, 0, i, 0, 0)),
            pl.BlockSpec((4, 4, 2, G, L), lambda i: (0, 0, i, 0, 0)),
            pl.BlockSpec((8, 4, G, L), lambda i: (i, 0, 0, 0)),
        ],
        out_specs=[half] * 4 + [rows_a, rows_a, rows_b, rows_b],
        out_shape=[cols] * 4 + [rows] * 4,
        scratch_shapes=[
            pltpu.VMEM((length, width // 2), bf16),
            pltpu.VMEM((width // 2, length), bf16),
            pltpu.VMEM((4, 4, 2, G, L), bf16),
            pltpu.VMEM((8, 4, G, L), bf16),
        ],
        compiler_params=params(),
        cost_estimate=cost(3 * length * width * hidden, 40 * length * width),
        name="ffn_grads",
    )(pos, ht, df, hid, dgate, dup, *got)


def ffn_out_body(r1_ref, hid_ref, wd, out_ref):
    out_ref[...] = (r1_ref[...] + nn(hid_ref[...], two(wd, 0))).astype(bf16)


def ffn_out(r1, hid, wd):
    length, width = r1.shape
    hidden = hid.shape[1]
    col = pl.BlockSpec((length, 2 * L), lambda i: (0, i))
    return pl.pallas_call(
        ffn_out_body,
        grid=(width // (2 * L),),
        in_specs=[col, once(length, hidden), pl.BlockSpec((2, hidden // G, G, L), lambda i: (i, 0, 0, 0))],
        out_specs=col,
        out_shape=shape((length, width)),
        compiler_params=params(),
        cost_estimate=cost(2 * length * width * hidden, 20 * length * width),
        name="ffn_out",
    )(r1, hid, wd)


def square_send_body(pos, o_ref, ht_ref, da_ref, dq_ref, dk_ref, dv_ref, out_ref, ot, left):
    step = pl.program_id(0)
    length = o_ref.shape[0]
    per = pl.num_programs(0) // 4

    @pl.when(step == 0)
    def _():
        other = 1 - lax.rem(pos[1], 2)
        for i in range(length // QB):
            rows = slice(i * QB, (i + 1) * QB)
            ot[:, :, :, rows] = o_ref[rows, :].astype(f32).T.astype(bf16).reshape(ot.shape[:3] + (QB,))
        left[0] = chosen_rows(ot, other)
        left[1] = chosen_rows(ht_ref, other)

    for i, ref in enumerate((da_ref, dq_ref, dk_ref, dv_ref)):

        @pl.when(step // per == i)
        def _():
            g = nn(left[min(i, 1)], ref[...]).astype(bf16)
            for c in range(2):
                out_ref[:, :, c] = g[:, c * L : (c + 1) * L].reshape(4, 4, G, L)


def square_keep_body(pos, o_ref, ht_ref, da_ref, dq_ref, dk_ref, dv_ref, got, sa, ka, sb, kb, ot, left, tile):
    step = pl.program_id(0)
    length = o_ref.shape[0]
    per = pl.num_programs(0) // 4
    core, b1, b2 = bits(pos)

    @pl.when(step == 0)
    def _():
        for i in range(length // QB):
            rows = slice(i * QB, (i + 1) * QB)
            ot[:, :, :, rows] = o_ref[rows, :].astype(f32).T.astype(bf16).reshape(ot.shape[:3] + (QB,))
        left[0] = chosen_rows(ot, core)
        left[1] = chosen_rows(ht_ref, core)

    for i, ref in enumerate((da_ref, dq_ref, dk_ref, dv_ref)):

        @pl.when(step // per == i)
        def _():
            g = nn(left[min(i, 1)], ref[...])
            for c in range(2):
                tile[:, :, c] = (
                    g[:, c * L : (c + 1) * L].reshape(4, 4, G, L) + got[:, :, c].astype(f32)
                ).astype(bf16)
            for j in range(2):
                if i < 2:
                    sa[:, j] = tile[:, 2 * j + 1 - b1]
                    ka[:, j] = tile[:, 2 * j + b1]
                else:
                    sb[:, j] = tile[:, 2 * (1 - b2) + j]
                    kb[:, j] = tile[:, 2 * b2 + j]


def square_grads(pos, o, ht, grads, got):
    length, width = o.shape
    per = width // (2 * L)
    tiles = 4 * per

    def quarter(which):
        return pl.BlockSpec((length, 2 * L), lambda i: (0, jnp.clip(i - which * per, 0, per - 1)))

    common = [SMEM, once(length, width), once(*ht.shape)] + [quarter(i) for i in range(4)]
    whole = pl.BlockSpec((4, 4, 2, G, L), lambda i: (0, 0, i, 0, 0))
    scratch = [pltpu.VMEM(ht.shape, bf16), pltpu.VMEM((2, width // 2, length), bf16)]
    estimate = cost(4 * length * width * width, 24 * length * width)
    if got is None:
        return pl.pallas_call(
            square_send_body,
            grid=(tiles,),
            in_specs=common,
            out_specs=whole,
            out_shape=shape((4, 4, 4 * width // L, G, L)),
            scratch_shapes=scratch,
            compiler_params=params(),
            cost_estimate=estimate,
            name="square_send",
        )(pos, o, ht, *grads)
    first = pl.BlockSpec((4, 2, 2, G, L), lambda i: (0, 0, jnp.minimum(i, 2 * per - 1), 0, 0))
    second = pl.BlockSpec((4, 2, 2, G, L), lambda i: (0, 0, jnp.maximum(i - 2 * per, 0), 0, 0))
    half = shape((4, 2, 2 * width // L, G, L))
    return pl.pallas_call(
        square_keep_body,
        grid=(tiles,),
        in_specs=common + [whole],
        out_specs=[first, first, second, second],
        out_shape=[half] * 4,
        scratch_shapes=scratch + [pltpu.VMEM((4, 4, 2, G, L), bf16)],
        compiler_params=params(),
        cost_estimate=estimate,
        name="square_keep",
    )(pos, o, ht, *grads, got)


def input_grad_body(x_ref, gain_ref, dr_ref, dq_ref, dk_ref, dv_ref, wq, wk, wv, out_ref, acc):
    step = pl.program_id(0)
    length = x_ref.shape[0]
    both = jnp.concatenate([dq_ref[...], dk_ref[...], dv_ref[...]], 1)
    part = nt(both, jnp.concatenate([two(w, 0) for w in (wq, wk, wv)], 1))

    @pl.when(step == 0)
    def _():
        acc[...] = part

    @pl.when(step > 0)
    def _():
        acc[...] += part

    @pl.when(step == pl.num_programs(0) - 1)
    def _():
        for i in range(length // QB):
            rows = slice(i * QB, (i + 1) * QB)
            x = x_ref[rows, :].astype(f32)
            rinv = lax.rsqrt(jnp.mean(x * x, -1, keepdims=True) + EPS)
            n1 = x * rinv
            dn = acc[rows, :] * gain_ref[...]
            out_ref[rows, :] = dr_ref[rows, :] + rinv * (dn - n1 * jnp.mean(dn * n1, -1, keepdims=True))


def input_grad(x, gain, dr1, dq, dk, dv, weights):
    length, width = x.shape
    col = pl.BlockSpec((length, 2 * L), lambda i: (0, i))
    weight = pl.BlockSpec((2, width // G, G, L), lambda i: (i, 0, 0, 0))
    return pl.pallas_call(
        input_grad_body,
        grid=(width // (2 * L),),
        in_specs=[once(length, width), once(1, width), once(length, width), col, col, col] + [weight] * 3,
        out_specs=once(length, width),
        out_shape=shape((length, width), f32),
        scratch_shapes=[pltpu.VMEM((length, width), f32)],
        compiler_params=params(),
        cost_estimate=cost(6 * length * width * width, 24 * length * width),
        name="input_grad",
    )(x, gain, dr1, dq, dk, dv, *weights)


def place_body(pos, *refs):
    pieces, outs = refs[:10], refs[10:]
    d = pos[1]
    for array, mask, low, size in piece_sources(pieces[0].shape[1]):
        rows = pl.ds(pl.multiple_of((d ^ mask) * G, G), G)
        for c in range(size):
            which, at = 0, low + c
            while at >= outs[which].shape[1] // L:
                at -= outs[which].shape[1] // L
                which += 1
            outs[which][rows, at * L : (at + 1) * L] = pieces[array][0, c].astype(f32)


def place(pos, arrays, widths, rows):
    vmem = pl.BlockSpec(memory_space=pltpu.VMEM)
    return pl.pallas_call(
        place_body,
        in_specs=[SMEM] + [vmem] * 10,
        out_specs=[vmem] * len(widths),
        out_shape=[shape((rows, w), f32) for w in widths],
        compiler_params=params(),
        name="place",
    )(pos, *arrays)


def layout(lengths, length):
    position = jnp.arange(length, dtype=jnp.int32)
    ends = jnp.cumsum(lengths).astype(jnp.int32)
    seg = jnp.sum((position[:, None] >= ends[None, :]).astype(jnp.int32), 1)
    onehot = seg[:, None] == jnp.arange(lengths.shape[0], dtype=jnp.int32)[None, :]
    first = jnp.sum(jnp.where(onehot, (ends - lengths)[None, :], 0), 1)
    last = jnp.sum(jnp.where(onehot, ends[None, :], 0), 1)
    rel = (position - first).astype(f32)
    inverse = 10000.0 ** (-jnp.arange(HEAD_DIM // 2, dtype=f32) * 2.0 / HEAD_DIM)
    angle = rel[:, None] * inverse[None, :]
    keep = (seg < lengths.shape[0] - 1).astype(f32)
    cos, sin = jnp.cos(angle), jnp.sin(angle)
    cos_w = jnp.concatenate([cos] * 4, 1)
    sin_w = jnp.concatenate([-sin, sin] * 2, 1)
    return cos_w, sin_w, first[None, :], last[None, :], keep[:, None]


def add(*terms):
    total = terms[0].astype(f32)
    for t in terms[1:]:
        total = total + t.astype(f32)
    return total


def halve(kept, got, bit):
    picked = []
    for at in (1 - bit, bit):
        parts = [lax.dynamic_index_in_dim(x, at, 1, keepdims=False) for x in (kept, got)]
        picked.append(add(*parts).astype(bf16))
    return picked


def in_parts(sums):
    parts = []
    for _ in range(3):
        part = lax.reduce_precision(sums, 8, 7)
        parts.append(part)
        sums = sums - part
    return jnp.pad(jnp.stack(parts).astype(bf16), ((0, G - 3), (0, L - 2)))


def from_parts(block):
    parts = block[..., :3, :2].astype(f32)
    return parts[..., 0, :] + parts[..., 1, :] + parts[..., 2, :]


def over_fsdp(total, z, extra=None):
    terms = [lax.dynamic_index_in_dim(total, z, 0, keepdims=False)]
    extras = [extra]
    for s in (1, 2, 3):
        away = lax.dynamic_index_in_dim(total, lax.rem(z + s, 4), 0, keepdims=False)
        if extra is not None:
            away = jnp.concatenate([away, extra[None]])
        came = fsdp_shift(away, s)
        if extra is not None:
            extras.append(came[-1])
            came = came[:-1]
        terms.append(came)
    sums = None
    if extra is not None:
        numbers = jnp.stack([from_parts(e) for e in extras])
        for shard in range(4):
            term = lax.dynamic_index_in_dim(numbers, lax.rem(z + 4 - shard, 4), 0, keepdims=False)
            sums = term if sums is None else sums + term
    return add(*terms).astype(bf16), sums


def unfold_rows(w):
    return w.transpose(0, 2, 1, 3).reshape(w.shape[0] * G, w.shape[1] * L)


def sum_whole(grad):
    part = lax.psum_scatter(grad.astype(bf16), "fsdp", scatter_dimension=0, tiled=True)
    return lax.psum(part, "dp").astype(f32)


def local(
    layer_in, first_values, first_values_grad, cotangent, doc_lengths, norm1_gain,
    w_query, w_key, w_value, w_out, norm2_gain, w_gate, w_up, w_down,
):
    rows, length, width = layer_in.shape
    hidden = w_gate.shape[1]
    dp, fsdp = lax.axis_size("dp"), lax.axis_size("fsdp")
    fast = fast_mesh(dp, fsdp, w_query.shape[0])
    z, d = lax.axis_index("fsdp"), lax.axis_index("dp")
    b1, b2 = lax.rem(d // 2, 2), lax.rem(d // 4, 2)
    x, v1 = layer_in[0], first_values[0]
    df = cotangent[0]
    gains = jnp.stack([norm1_gain, norm2_gain])
    c, h = width // L, hidden // L
    members = (
        ((w_query, w_key, w_value), ((c, True),) * 3),
        ((w_out, w_gate), ((c, True), (h, True))),
        ((w_up,), ((h, True),)),
        ((w_down,), ((w_down.shape[0] // G, False),)),
    )
    if fast:
        pos = jnp.stack([z, d]).astype(jnp.int32)
        extra = jnp.pad(gains.reshape(-1, L), ((0, G - gains.size // L), (0, 0)))
        mines, owns = [], []
        for weights, tensors in members:
            pieces, owned = [], []
            for w, (_, by_rows) in zip(weights, tensors):
                if by_rows:
                    pieces.append(row_pieces(lax.dynamic_slice_in_dim(w, d * G, G, 0), 1)[0])
                    owned.append(row_pieces(w, 8))
                else:
                    pieces.append(column_pieces(lax.dynamic_slice_in_dim(w, d * L, L, 1), 1)[0])
                    owned.append(column_pieces(w, 8))
            mines.append(jnp.concatenate(pieces) if len(pieces) > 1 else pieces[0])
            owns.append(jnp.concatenate(owned, 1) if len(owned) > 1 else owned[0])
        g1 = Gather(mines[0], extra)
        far = jnp.stack([e[: gains.size // L].reshape(gains.shape) for e in g1.extras])
        g1.near()
        g2 = Gather(after(mines[1], g1.start))
        g1.corner()
        g1.core()
        g1.core_corner()
        g2.near()
        g3 = Gather(after(mines[2], g2.start))
        groups = [Group(members[0][1], [owns[0]] + g1.arrays(), False)]
        whole_gains = jnp.concatenate(
            [lax.dynamic_index_in_dim(far, lax.rem(z + 4 - j, 4), 0, keepdims=False) for j in range(4)], 1
        )
    else:
        pos = jnp.zeros((2,), jnp.int32)

        def blocks(w, by_rows):
            full = lax.all_gather(w, "fsdp", axis=0, tiled=True)
            return row_pieces(full, full.shape[0] // G).transpose(1, 0, 2, 3) if by_rows else column_pieces(full, c)

        whole_gains = lax.all_gather(gains, "fsdp", axis=1, tiled=True)
        groups = [
            Group(tensors, [blocks(w, t[1]) for w, t in zip(weights, tensors)], True)
            for weights, tensors in members
        ]
    whole_gains = whole_gains.astype(f32)
    gain_1, gain_2 = whole_gains[:1], whole_gains[1:]
    cos_w, sin_w, first_row, last_row, keep_col = layout(doc_lengths[0], length)

    q, k, vm, h1, h1t, sums, wq, wk, wv = qkv(pos, x, v1, gain_1, cos_w, sin_w, groups[0])
    squares = jnp.sum(sums, (1, 2))
    entries = rows * length * width * dp * fsdp
    if fast:
        g2.corner(q)
        g3.near(q)
        g4 = Gather(after(mines[3], g3.start, q))
    o, lse_1 = attend_fwd(q, k, vm, last_row, keep_col, 0, 3)
    if fast:
        g2.core(o)
        g2.core_corner(o)
        g3.corner(o)
    o, lse_2 = attend_fwd(q, k, vm, last_row, keep_col, 3, 3, o)
    if fast:
        g3.core(o)
        g4.near(o)
    o, lse_3 = attend_fwd(q, k, vm, last_row, keep_col, 6, 2, o)
    if fast:
        g3.core_corner(o)
        g4.corner(o)
        g4.core(o)
        groups += [Group(members[i][1], [owns[i]] + g.arrays(), False) for i, g in ((1, g2), (2, g3))]
    r1, h2, h2t, hid, ga, ua, wo, wg, wu = ffn_up(pos, x, o, gain_2, groups[1:3], hidden)
    if fast:
        g4.core_corner(r1)
        groups.append(Group(members[3][1], [owns[3]] + g4.arrays(), False))
    dgate, dup, sg, su, sd, wd = ffn_down(pos, h2t, df, hid, ga, ua, groups[3])
    if fast:
        got = [dp_swap(g, 1) for g in (sg, su, sd)]
    else:
        got = [jnp.zeros_like(g) for g in (sg, su, sd)]
    dr1, da, do = ffn_back(pos, r1, df, keep_col, gain_2, dgate, dup, wo, wg, wu)
    tg, kg, tu, ku, ta, ka, tb, kb = ffn_grads(pos, h2t, df, hid, dgate, dup, after(got, da))
    if fast:
        ng, na, nu, nb = dp_swap(tg, 2), dp_swap(ta, 2), dp_swap(tu, 4), dp_swap(tb, 4)
    back = (first_row, cos_w, -sin_w, first_values_grad[0])
    results = attend_bwd(q, k, vm, after(do, tg), lse_1.T, *back, 0, 3)
    results = attend_bwd(q, k, vm, do, lse_2.T, *back, 3, 3, results)
    dq, dk, dv, first_out = attend_bwd(q, k, vm, do, lse_3.T, *back, 6, 2, results)
    grads = (da, dq, dk, dv)
    if fast:
        ng, na, nu, nb = after((ng, na, nu, nb), dq)
        tg, kg = halve(kg, ng, b2)
        ta, ka = halve(ka, na, b2)
        tu, ku = halve(ku, nu, b1)
        tb, kb = halve(kb, nb, b1)
        mg, ma, mu, mb = dp_swap(tg, 4), dp_swap(ta, 4), dp_swap(tu, 2), dp_swap(tb, 2)
    send = square_grads(pos, o, h1t, grads, None)
    swapped = dp_swap(send, 1) if fast else jnp.zeros_like(send)
    d_x = input_grad(after(x, send), gain_1, dr1, dq, dk, dv, (wq, wk, wv))
    swapped = after(swapped, d_x)
    if fast:
        mg, ma, mu, mb = after((mg, ma, mu, mb), d_x)
        total_g = add(kg, mg).astype(bf16)
        total_a = add(ka, ma).astype(bf16)
        total_u = add(ku, mu).astype(bf16)
        total_b = add(kb, mb).astype(bf16)
        count = hidden // G
        edge = count // 2
        skip = count - total_b.shape[0]
        total_d = jnp.concatenate([total_a[:edge], total_b[edge - skip :]]).reshape(4, count // 4, G, L)
        reduced, sums_z = over_fsdp(jnp.concatenate([total_g, total_u, total_d], 1), z, in_parts(squares))
        wide = lax.all_gather(jnp.concatenate([reduced, in_parts(sums_z)[None]]), "dp")
        squares = jnp.sum(from_parts(wide[:, -1]), 0)
        wide = wide[:, :-1].astype(f32)
        n = hidden // L
        grad_wg, grad_wu = unfold_rows(wide[:, :n]), unfold_rows(wide[:, n : 2 * n])
        grad_wd = wide[:, 2 * n :].transpose(1, 2, 0, 3).reshape(hidden // 4, width)

    ts, ks, tt, kt = square_grads(pos, o, h1t, grads, swapped)
    if fast:
        ns, n_t = dp_swap(ts, 2), dp_swap(tt, 4)
    out = ffn_out(r1, after(hid, ts), wd)
    if fast:
        ns, n_t = after((ns, n_t), out)
        ts, ks = halve(ks, ns, b2)
        tt, kt = halve(kt, n_t, b1)
        total_s = add(ks, dp_swap(ts, 4)).astype(bf16)
        total_t = add(kt, dp_swap(tt, 2)).astype(bf16)
        reduced, _ = over_fsdp(jnp.concatenate([total_s, total_t], 1), z)
        last = Gather.__new__(Gather)
        last.count, last.start = reduced.shape[0], reduced[None]
        last.near()
        last.corner()
        last.core()
        last.core_corner()
        grad_wo, grad_wq, grad_wk, grad_wv = place(pos, last.arrays(), [width] * 4, w_query.shape[0])
    else:
        grad_wg = join(kg, tg, sg, True)
        grad_wu = join(ku, tu, su, False)
        squares = lax.psum(squares, ("dp", "fsdp"))
        count = hidden // G
        edge = count // 2
        skip = count - kb.shape[0]
        even = jnp.concatenate(
            [jnp.stack([ka, ta], 2)[:edge].reshape(edge, 4, G, L), jnp.stack([kb, tb], 1)[edge - skip :].reshape(edge, 4, G, L)]
        )
        grad_wd = jnp.stack([even, sd], 2).reshape(count, 8, G, L).transpose(0, 2, 1, 3).reshape(hidden, width)
        n = width // L
        firsts = join(ks, ts, send[:, :, : 2 * n], True)
        seconds = join(kt, tt, send[:, :, 2 * n :], False)
        grad_wo, grad_wq = firsts[:, :width], firsts[:, width:]
        grad_wk, grad_wv = seconds[:, :width], seconds[:, width:]
        grad_wo, grad_wq, grad_wk, grad_wv, grad_wg, grad_wu, grad_wd = [
            sum_whole(g) for g in (grad_wo, grad_wq, grad_wk, grad_wv, grad_wg, grad_wu, grad_wd)
        ]
    def along(*pairs):
        return sum(jnp.sum(w.astype(f32) * g, 1) for w, g in pairs)

    grad_g1 = along((w_query, grad_wq), (w_key, grad_wk), (w_value, grad_wv)) / norm1_gain.astype(f32)
    grad_g2 = along((w_gate, grad_wg), (w_up, grad_wu)) / norm2_gain.astype(f32)
    return (
        out[None], d_x[None], first_out[None], grad_g1, grad_wq, grad_wk, grad_wv, grad_wo, grad_g2,
        grad_wg, grad_wu, grad_wd, squares / entries,
    )


def join(kept, sent, odd, by_x):
    even = jnp.stack([kept, sent], 2 if by_x else 1)
    even = even.reshape(odd.shape)
    both = jnp.stack([even, odd], 2)
    return unfold_rows(both.reshape((32,) + odd.shape[2:]))


def solution(mesh):
    by_row = P(("dp", "fsdp"), None, None)
    shard = P("fsdp", None)
    return jax.shard_map(
        local,
        mesh=mesh,
        in_specs=(by_row,) * 4
        + (P(("dp", "fsdp"), None), P("fsdp"), shard, shard, shard, shard, P("fsdp"), shard, shard, shard),
        out_specs=(by_row,) * 3
        + (P("fsdp"), shard, shard, shard, shard, P("fsdp"), shard, shard, shard, P()),
        check_vma=False,
    )
```

```python
import jax
import jax.numpy as jnp
from jax import lax
from jax.experimental import pallas as pl
from jax.experimental.pallas import tpu as pltpu
from jax.sharding import PartitionSpec as P

HEADS = 16
HEAD_DIM = 64
EPS = 1e-06
NEG = -1e30
COST = 4e9
QB = 256
G = 32
L = 128
bf16 = jnp.bfloat16
f32 = jnp.float32
ANY = pl.BlockSpec(memory_space=pl.ANY)
SMEM = pl.BlockSpec(memory_space=pltpu.SMEM)


def params(mib=58):
    return pltpu.CompilerParams(vmem_limit_bytes=mib * 2**20)


def cost(us):
    return pl.CostEstimate(flops=int(us * COST), bytes_accessed=0, transcendentals=0)


def shape(dims, dtype=bf16):
    return jax.ShapeDtypeStruct(dims, dtype)


def nt(a, b):
    return lax.dot_general(a, b, (((1,), (1,)), ((), ())), preferred_element_type=f32)


def nn(a, b):
    return lax.dot_general(a, b, (((1,), (0,)), ((), ())), preferred_element_type=f32)


def tn(a, b):
    return lax.dot_general(a, b, (((0,), (0,)), ((), ())), preferred_element_type=f32)


def fast_mesh(dp, fsdp, shard_rows):
    return dp == 8 and fsdp == 4 and shard_rows == 8 * G


def row_pieces(w, count):
    return w.reshape(count, G, w.shape[1] // L, L).transpose(0, 2, 1, 3)


def column_pieces(w, count):
    return w.reshape(w.shape[0] // G, G, count, L).transpose(2, 0, 1, 3)


def dp_swap(x, bit):
    return lax.ppermute(x, "dp", [(i, i ^ bit) for i in range(lax.axis_size("dp"))])


def after(x, *first):
    return lax.optimization_barrier((x, first))[0]


def fsdp_shift(x, step):
    size = lax.axis_size("fsdp")
    return lax.ppermute(x, "fsdp", [(i, (i + step) % size) for i in range(size)])


class Gather:
    def __init__(self, sent, extra=False):
        self.count = sent.shape[0] - extra
        self.far = [fsdp_shift(sent, s) for s in (1, 2, 3)]
        self.extras = [x[self.count] for x in [sent] + self.far] if extra else None

    def near(self, *gate):
        self.start = jnp.stack([x[: self.count] for x in after(self.far, *gate)])
        self.x, self.y = dp_swap(self.start, 2), dp_swap(self.start, 4)

    def corner(self, *gate):
        cut = self.count // 2
        self.c1 = dp_swap(after(self.x[:, :cut], *gate), 4)
        self.c2 = dp_swap(after(self.y[:, cut:], *gate), 2)

    def core(self, *gate):
        self.other = [dp_swap(after(a, *gate), 1) for a in (self.start, self.x, self.y)]

    def core_corner(self, *gate):
        self.other += [dp_swap(after(a, *gate), 1) for a in (self.c1, self.c2)]

    def arrays(self):
        return [self.start, self.x, self.y, self.c1, self.c2] + self.other


def piece_sources(count):
    cut = count // 2
    found = []
    for core in range(2):
        for i, (mask, low, size) in enumerate(
            ((0, 0, count), (2, 0, count), (4, 0, count), (6, 0, cut), (6, cut, count - cut))
        ):
            found.append((5 * core + i, mask | core, low, size))
    return found


class Group:
    def __init__(self, tensors, owned, arrays, whole):
        self.tensors, self.whole, self.owned = tensors, whole, len(owned)
        self.arrays = list(owned) + list(arrays)

    def specs(self):
        return [ANY] * len(self.arrays)

    def fetch(self, index, refs, pos, scratch, sem):
        if self.whole:
            pltpu.make_async_copy(refs[index], scratch, sem).start()
            return
        z, d = pos[0], pos[1]
        at = sum(t[0] for t in self.tensors[:index])
        blocks, by_rows = self.tensors[index]

        def target(shard, piece, low, size):
            if by_rows:
                return scratch.at[pl.ds(low, size), shard * 8 + piece]
            return scratch.at[piece, pl.ds(shard * blocks + low, size)]

        own = refs[index]
        rows = own.shape[0]
        flat = scratch.reshape(scratch.shape[0], scratch.shape[1] * G, L)
        for c in range(scratch.shape[0]):
            pltpu.make_async_copy(
                own.at[:, pl.ds(c * L, L)], flat.at[c, pl.ds(pl.multiple_of(z * rows, G), rows)], sem
            ).start()
        for array, mask, low, size in piece_sources(sum(t[0] for t in self.tensors)):
            begin, end = max(at, low), min(at + blocks, low + size)
            if end <= begin:
                continue
            for s in range(3):
                pltpu.make_async_copy(
                    refs[self.owned + array].at[s, pl.ds(begin - low, end - begin)],
                    target(lax.rem(z + 3 - s, 4), d ^ mask, begin - at, end - begin),
                    sem,
                ).start()


def cut_body(tensors, gains, pos, *refs):
    count = len(tensors)
    weights, refs = refs[:count], refs[count:]
    if gains:
        gain_ref, refs = refs[0], refs[1:]
    out, stages, sem = refs[0], refs[1:-1], refs[-1]
    d = pos[1]
    copies = []
    for i, (blocks, by_rows) in enumerate(tensors):
        rows = pl.ds(pl.multiple_of(d * G, G), G)
        cols = pl.ds(pl.multiple_of(d * L, L), L)
        part = weights[i].at[rows] if by_rows else weights[i].at[:, cols]
        copies.append(pltpu.make_async_copy(part, stages[i], sem.at[i]))
    for c in copies:
        c.start()
    at = 0
    for i, (blocks, by_rows) in enumerate(tensors):
        copies[i].wait()
        if by_rows:
            for c in range(blocks):
                out[at + c] = stages[i][:, c * L : (c + 1) * L]
        else:
            out[at : at + blocks] = stages[i][...].reshape(blocks, G, L)
        at += blocks
    if gains:
        out[at] = gain_ref[...]


def cut(pos, weights, tensors, gains=None):
    vmem = pl.BlockSpec(memory_space=pltpu.VMEM)
    total = sum(t[0] for t in tensors) + (gains is not None)
    stages = [
        pltpu.VMEM((G, w.shape[1]) if by_rows else (w.shape[0], L), bf16) for w, (_, by_rows) in zip(weights, tensors)
    ]
    return pl.pallas_call(
        lambda *refs: cut_body(tensors, gains is not None, *refs),
        in_specs=[SMEM] + [ANY] * len(weights) + ([] if gains is None else [vmem]),
        out_specs=vmem,
        out_shape=shape((total, G, L)),
        scratch_shapes=stages + [pltpu.SemaphoreType.DMA((len(weights),))],
        compiler_params=params(),
        name="cut",
    )(pos, *weights, *([] if gains is None else [gains]))


def wait_all(scratch, sem):
    pltpu.make_async_copy(scratch, scratch, sem).wait()


def two(w, i):
    rows = w.shape[1] * w.shape[2]
    return jnp.concatenate([w[2 * i].reshape(rows, L), w[2 * i + 1].reshape(rows, L)], 1)


def swap_halves(t):
    lane = lax.broadcasted_iota(jnp.int32, t.shape, 1) % 64
    return jnp.where(lane < 32, pltpu.roll(t, 96, 1), pltpu.roll(t, 32, 1))


def chunked(blocks, size):
    return [(low, min(size, blocks - low)) for low in range(0, blocks, size)]


def beside(w, low, size):
    rows = w.shape[1] * G
    return jnp.concatenate([w[low + c].reshape(rows, L) for c in range(size)], 1)


def like(a):
    return pltpu.VMEM(a.shape, a.dtype)


def qkv_body(group, pos, gain_ref, cos_ref, sin_ref, x_ref, v1_hbm, *rest):
    count = len(group.arrays)
    w_refs = rest[:count]
    (q_out, k_out, v_out, ht_out, sums_ref, wq_out, wk_out, wv_out,
     v1, wq, wk, wv, h, ht, q, k, v, sem) = rest[count:]
    length, width = x_ref.shape
    blocks = width // L
    for i, w in enumerate((wq, wk, wv)):
        group.fetch(i, w_refs, pos, w, sem.at[i])
    get_v1 = pltpu.make_async_copy(v1_hbm, v1, sem.at[3])
    get_v1.start()
    for i in range(length // QB):
        rows = slice(i * QB, (i + 1) * QB)
        x = x_ref[rows, :].astype(f32)
        n = x * lax.rsqrt(jnp.mean(x * x, -1, keepdims=True) + EPS) * gain_ref[...]
        h[rows, :] = n.astype(bf16)
        ht[:, :, :, rows] = n.T.astype(bf16).reshape(ht.shape[:3] + (QB,))
    out = [pltpu.make_async_copy(ht, ht_out, sem.at[4])]
    out[0].start()
    cos, sin = cos_ref[...], sin_ref[...]
    at = 5

    def send(a, b):
        out.append(pltpu.make_async_copy(a, b, sem.at[at + len(out) - 1]))
        out[-1].start()

    sums_ref[...] = jnp.zeros_like(sums_ref)
    for i, (w, w_out, t, t_out) in enumerate(((wq, wq_out, q, q_out), (wk, wk_out, k, k_out), (wv, wv_out, v, v_out))):
        wait_all(w, sem.at[i])
        send(w, w_out)
        if i == 2:
            get_v1.wait()
        for low, size in chunked(blocks, 2):
            cols = slice(low * L, (low + size) * L)
            got = nn(h[...], beside(w, low, size))
            if i == 2:
                first = v1[:, cols].astype(f32)
                mixed = (0.5 * got + 0.5 * first).astype(bf16)
                v[:, cols] = mixed
                mixed = mixed.astype(f32)
                sums_ref[0] += jnp.sum((first * first).reshape(length // 8, 8, size * L), 0)
                sums_ref[1] += jnp.sum((mixed * mixed).reshape(length // 8, 8, size * L), 0)
                continue
            for c in range(size):
                part = got[:, c * L : (c + 1) * L]
                part = (part * cos + swap_halves(part) * sin).astype(bf16)
                if i == 0:
                    part = (part.astype(f32) * 0.125).astype(bf16)
                t[:, (low + c) * L : (low + c + 1) * L] = part
        send(t, t_out)
    for c in out:
        c.wait()


def qkv(pos, x, v1, gain, cos_w, sin_w, group):
    length, width = x.shape
    blocks = width // L
    vmem = pl.BlockSpec(memory_space=pltpu.VMEM)
    weight = shape((blocks, width // G, G, L))
    ht = shape((width // G // 2, 2, G, length))
    return pl.pallas_call(
        lambda *refs: qkv_body(group, *refs),
        in_specs=[SMEM, vmem, vmem, vmem, vmem, ANY] + group.specs(),
        out_specs=[ANY] * 4 + [vmem] + [ANY] * 3,
        out_shape=[shape((length, width))] * 3 + [ht, shape((2, 8, 2 * L), f32)] + [weight] * 3,
        scratch_shapes=[like(a) for a in (v1, weight, weight, weight, x, ht, x, x, x)]
        + [pltpu.SemaphoreType.DMA((12,))],
        compiler_params=params(),
        cost_estimate=cost(15),
        name="qkv",
    )(pos, gain, cos_w, sin_w, x, v1, *group.arrays)


def half_mask(rows, which):
    lane = lax.broadcasted_iota(jnp.int32, (rows, 128), 1)
    return (lane < 64) if which == 0 else (lane >= 64)


def pick(x, which):
    return jnp.where(half_mask(x.shape[0], which), x, jnp.zeros_like(x))


def attend_fwd_body(q_ref, k_ref, v_ref, end_ref, keep_ref, *rest):
    o_ref, lse_ref, bias = rest[-3:]
    pair = pl.program_id(0)
    length = q_ref.shape[0]
    blocks = length // QB

    @pl.when(pair == 0)
    def _():
        for i in range(blocks):
            size = (i + 1) * QB
            q_at = lax.broadcasted_iota(jnp.int32, (QB, size), 0) + i * QB
            k_at = lax.broadcasted_iota(jnp.int32, (QB, size), 1)
            ok = (q_at >= k_at) & (q_at < end_ref[:, :size])
            bias[i * QB : (i + 1) * QB, :size] = jnp.where(ok, 0.0, NEG)

    lane = lax.broadcasted_iota(jnp.int32, (QB, 128), 1)
    for i in range(blocks):
        rows = slice(i * QB, (i + 1) * QB)
        size = (i + 1) * QB
        outs = []
        old = lse_ref[rows, :]
        for h in range(2):
            s = nt(pick(q_ref[rows, :], h), k_ref[:size, :]) + bias[rows, :size]
            top = jnp.max(s, -1, keepdims=True)
            expo = jnp.exp(s - top)
            total = jnp.sum(expo, -1, keepdims=True)
            outs.append(nn(expo.astype(bf16), v_ref[:size, :]) / total)
            old = jnp.where(lane == 2 * pair + h, top + jnp.log(total), old)
        lse_ref[rows, :] = old
        o = jnp.where(lane < 64, outs[0], outs[1]) * keep_ref[rows, :]
        o_ref[rows, :] = o.astype(bf16)


def attend_fwd(q, k, v, end_row, keep_col, first, pairs, before=None):
    length, width = q.shape
    col = pl.BlockSpec((length, 128), lambda p: (0, p + first))
    return pl.pallas_call(
        attend_fwd_body,
        grid=(pairs,),
        in_specs=[
            col,
            col,
            col,
            pl.BlockSpec((1, length), lambda p: (0, 0)),
            pl.BlockSpec((length, 1), lambda p: (0, 0)),
        ]
        + ([] if before is None else [ANY]),
        out_specs=[col, pl.BlockSpec((length, 128), lambda p: (0, 0))],
        out_shape=[
            jax.ShapeDtypeStruct((length, width), bf16),
            jax.ShapeDtypeStruct((length, 128), f32),
        ],
        scratch_shapes=[pltpu.VMEM((length, length), f32)],
        compiler_params=params(),
        cost_estimate=cost(4.2 * pairs),
        input_output_aliases={} if before is None else {5: 0},
        name="attend_fwd",
    )(q, k, v, end_row, keep_col, *([] if before is None else [before]))


def attend_bwd_body(
    q_ref, k_ref, v_ref, do_ref, lse_ref, first_ref, cos_ref, sin_ref, fg_ref, *rest,
):
    dq_ref, dk_ref, dv_ref, fo_ref, bias, dk_acc, dv_acc = rest[-7:]
    pair = pl.program_id(0)
    length = q_ref.shape[0]
    blocks = length // QB

    @pl.when(pair == 0)
    def _():
        for i in range(blocks):
            size = (i + 1) * QB
            k_at = lax.broadcasted_iota(jnp.int32, (size, QB), 0)
            q_at = lax.broadcasted_iota(jnp.int32, (size, QB), 1) + i * QB
            ok = (q_at >= k_at) & (k_at >= first_ref[:, i * QB : (i + 1) * QB])
            bias[:size, i * QB : (i + 1) * QB] = jnp.where(ok, 0.0, NEG)

    k_t = k_ref[...].astype(f32).T.astype(bf16)
    for i in reversed(range(blocks)):
        rows = slice(i * QB, (i + 1) * QB)
        size = (i + 1) * QB
        part_k = None
        part_v = None
        part_q = []
        for h in range(2):
            qh = pick(q_ref[rows, :], h)
            dh = pick(do_ref[rows, :], h)
            lse = lse_ref[pl.ds(2 * pair + h, 1), rows]
            p = jnp.exp(nt(k_ref[:size, :], qh) + bias[:size, rows] - lse)
            dp = nt(v_ref[:size, :], dh)
            delta = jnp.sum(p * dp, 0, keepdims=True)
            ds = (p * (dp - delta)).astype(bf16)
            av = nn(p.astype(bf16), dh)
            ak = nn(ds, qh)
            part_v = av if part_v is None else part_v + av
            part_k = ak if part_k is None else part_k + ak
            part_q.append(nn(k_t[h * 64 : (h + 1) * 64, :size], ds))
        if i == blocks - 1:
            dk_acc[...] = part_k
            dv_acc[...] = part_v
        else:
            dk_acc[:size, :] += part_k
            dv_acc[:size, :] += part_v
        dq = jnp.concatenate(part_q, 0).T * 0.125
        dq = dq * cos_ref[rows, :] + swap_halves(dq) * sin_ref[rows, :]
        dq_ref[rows, :] = dq.astype(bf16)
    dk = dk_acc[...]
    dk_ref[...] = (dk * cos_ref[...] + swap_halves(dk) * sin_ref[...]).astype(bf16)
    dv = dv_acc[...].astype(bf16).astype(f32) * 0.5
    dv_ref[...] = dv.astype(bf16)
    fo_ref[...] = fg_ref[...] + dv


def attend_bwd(q, k, v, do, lse_t, first_row, cos_w, sin_back, fgrad, first, pairs, before=None):
    length, width = q.shape
    col = pl.BlockSpec((length, 128), lambda p: (0, p + first))
    before = [] if before is None else list(before)

    def whole(a):
        return pl.BlockSpec(a.shape, lambda p: (0, 0))

    wide = jax.ShapeDtypeStruct((length, width), bf16)
    return pl.pallas_call(
        attend_bwd_body,
        grid=(pairs,),
        in_specs=[col] * 4 + [whole(lse_t), whole(first_row), whole(cos_w), whole(sin_back), col]
        + [ANY] * len(before),
        out_specs=[col] * 4,
        out_shape=[wide, wide, wide, jax.ShapeDtypeStruct((length, width), f32)],
        scratch_shapes=[
            pltpu.VMEM((length, length), f32),
            pltpu.VMEM((length, 128), f32),
            pltpu.VMEM((length, 128), f32),
        ],
        compiler_params=params(),
        cost_estimate=cost(5.5 * pairs),
        input_output_aliases={9 + i: i for i in range(len(before))},
        name="attend_bwd",
    )(q, k, v, do, lse_t, first_row, cos_w, sin_back, fgrad, *before)


def chosen_columns(ref, parity):
    blocks = ref.shape[1] // L
    return jnp.concatenate(
        [ref[:, pl.ds(pl.multiple_of((2 * p + parity) * L, L), L)] for p in range(blocks // 2)], 1
    )


def chosen_rows(ref, parity):
    return ref[:, parity].reshape(ref.shape[0] * G, ref.shape[3])


def wd_rows(wd, t):
    return jnp.concatenate([wd[c, pl.ds(8 * t, 8)].reshape(8 * G, L) for c in range(wd.shape[0])], 1)


def pair_at(w, t):
    rows = w.shape[1] * G
    return jnp.concatenate([w[2 * t].reshape(rows, L), w[2 * t + 1].reshape(rows, L)], 1)


def once(*dims):
    return pl.BlockSpec(dims, lambda i: (0,) * len(dims), pipeline_mode=pl.Buffered(1))


def ffn_body(groups, pos, x_ref, o_ref, gain_ref, df_hbm, *rest):
    count = [len(g.arrays) for g in groups]
    refs, rest = rest[: sum(count)], rest[sum(count) :]
    of = [refs[: count[0]], refs[count[0] :]]
    (hid_ref, dg_ref, du_ref, sg_ref, su_ref, sd_ref, r1_out, ht_out, ot_out,
     wo_out, wg_out, wu_out, wd_out,
     wo, wg, wu, wd, r1, h2, ht, ot, df, dfs, hts, sem) = rest
    step = pl.program_id(0)
    length = x_ref.shape[0]
    outs = ((r1, r1_out), (ht, ht_out), (ot, ot_out), (wo, wo_out), (wg, wg_out), (wu, wu_out), (wd, wd_out))

    @pl.when(step == 0)
    def _():
        groups[0].fetch(0, of[0], pos, wo, sem.at[0])
        groups[0].fetch(1, of[0], pos, wg, sem.at[1])
        groups[1].fetch(0, of[1], pos, wu, sem.at[2])
        pltpu.make_async_copy(df_hbm, df, sem.at[4]).start()
        groups[1].fetch(1, of[1], pos, wd, sem.at[3])
        other = 1 - lax.rem(pos[1], 2)
        wait_all(wo, sem.at[0])
        w = jnp.concatenate([two(wo, c) for c in range(wo.shape[0] // 2)], 1)
        for i in range(length // QB):
            rows = slice(i * QB, (i + 1) * QB)
            r = x_ref[rows, :].astype(f32) + nn(o_ref[rows, :], w)
            r1[rows, :] = r
            h = r * lax.rsqrt(jnp.mean(r * r, -1, keepdims=True) + EPS) * gain_ref[...]
            h2[rows, :] = h.astype(bf16)
            ht[:, :, :, rows] = h.T.astype(bf16).reshape(ht.shape[:3] + (QB,))
            ot[:, :, :, rows] = o_ref[rows, :].astype(f32).T.astype(bf16).reshape(ht.shape[:3] + (QB,))
        hts[...] = chosen_rows(ht, other)
        wait_all(df, sem.at[4])
        dfs[...] = chosen_columns(df, other)
        wait_all(wg, sem.at[1])
        wait_all(wu, sem.at[2])
        wait_all(wd, sem.at[3])
        for i, (a, b) in enumerate(outs):
            pltpu.make_async_copy(a, b, sem.at[5 + i]).start()

    @pl.when(step > 0)
    def _():
        t = step - 1
        wgt, wut, wdt = pair_at(wg, t), pair_at(wu, t), wd_rows(wd, t)
        for i in range(length // QB):
            rows = slice(i * QB, (i + 1) * QB)
            gate = nn(h2[rows, :], wgt)
            up = nn(h2[rows, :], wut)
            dhid = nt(df[rows, :], wdt)
            sigma = 0.5 + 0.5 * jnp.tanh(0.5 * gate)
            silu = gate * sigma
            hid_ref[rows, :] = (silu * up).astype(bf16)
            dg_ref[rows, :] = (dhid * up * (sigma + silu * (1.0 - sigma))).astype(bf16)
            du_ref[rows, :] = (dhid * silu).astype(bf16)
        gd = tn(hid_ref[...], dfs[...]).astype(bf16)
        for p in range(4):
            sd_ref[:, p] = gd[:, p * L : (p + 1) * L].reshape(8, G, L)
        for ref, grad in ((sg_ref, dg_ref), (su_ref, du_ref)):
            g = nn(hts[...], grad[...]).astype(bf16)
            for c in range(2):
                ref[:, :, c] = g[:, c * L : (c + 1) * L].reshape(4, 4, G, L)

    @pl.when(step == pl.num_programs(0) - 1)
    def _():
        for i, (a, b) in enumerate(outs):
            pltpu.make_async_copy(a, b, sem.at[5 + i]).wait()


def ffn(pos, x, o, df, gain, groups, hidden):
    length, width = x.shape
    tiles = hidden // (2 * L)

    def late(i):
        return jnp.maximum(i - 1, 0)

    col = pl.BlockSpec((length, 2 * L), lambda i: (0, late(i)))
    grad_cols = pl.BlockSpec((4, 4, 2, G, L), lambda i: (0, 0, late(i), 0, 0))
    grad_rows = pl.BlockSpec((8, 4, G, L), lambda i: (late(i), 0, 0, 0))
    ht_dims = (width // G // 2, 2, G, length)
    square, wide = (width // L, width // G, G, L), (hidden // L, width // G, G, L)
    tall = (width // L, hidden // G, G, L)
    kept = [((length, width), f32), (ht_dims, bf16), (ht_dims, bf16)]
    kept += [(square, bf16), (wide, bf16), (wide, bf16), (tall, bf16)]
    vmem = [pltpu.VMEM(*a) for a in kept]
    return pl.pallas_call(
        lambda *refs: ffn_body(groups, *refs),
        grid=(1 + tiles,),
        in_specs=[SMEM, once(length, width), once(length, width), once(1, width), ANY]
        + [s for g in groups for s in g.specs()],
        out_specs=[col, col, col, grad_cols, grad_cols, grad_rows] + [ANY] * 7,
        out_shape=[
            shape((length, hidden)),
            shape((length, hidden)),
            shape((length, hidden)),
            shape((4, 4, hidden // L, G, L)),
            shape((4, 4, hidden // L, G, L)),
            shape((hidden // G, 4, G, L)),
        ]
        + [shape(*a) for a in kept],
        scratch_shapes=vmem[3:]
        + [
            vmem[0],
            pltpu.VMEM((length, width), bf16),
            vmem[1],
            vmem[2],
            pltpu.VMEM((length, width), bf16),
            pltpu.VMEM((length, width // 2), bf16),
            pltpu.VMEM((width // 2, length), bf16),
            pltpu.SemaphoreType.DMA((12,)),
        ],
        compiler_params=params(),
        cost_estimate=cost(46),
        name="ffn",
    )(pos, x, o, gain, df, *[a for g in groups for a in g.arrays])


def ffn_back_body(gain_ref, keep_ref, r1_hbm, df_hbm, wo_hbm, dg_hbm, du_hbm, wg_hbm, wu_hbm,
                  dr_out, da_out, do_out, r1, df, wo, dg, du, wg, wu, acc, da, do, sem):
    length, width = r1.shape
    chunks = chunked(wg.shape[0], 6)
    loads = []
    for i, (low, size) in enumerate(chunks):
        cols = pl.ds(low * L, size * L)
        loads.append(
            [
                pltpu.make_async_copy(a.at[:, cols] if flat else a.at[pl.ds(low, size)],
                                      b.at[:, cols] if flat else b.at[pl.ds(low, size)], sem.at[i])
                for a, b, flat in ((dg_hbm, dg, 1), (wg_hbm, wg, 0), (du_hbm, du, 1), (wu_hbm, wu, 0))
            ]
        )
    last = [pltpu.make_async_copy(a, b, sem.at[len(chunks) + i]) for i, (a, b) in
            enumerate(((r1_hbm, r1), (df_hbm, df), (wo_hbm, wo)))]
    for copies in loads + [last]:
        for c in copies:
            c.start()
    for (low, size), copies in zip(chunks, loads):
        for c in copies:
            c.wait()
        both = jnp.concatenate([a[:, low * L : (low + size) * L] for a in (dg, du)], 1)
        for n in range(width // QB):
            rows = slice(n * QB // G, (n + 1) * QB // G)
            w = jnp.concatenate(
                [a[low + c, rows].reshape(QB, L) for a in (wg, wu) for c in range(size)], 1
            )
            part = nt(both, w)
            if low == 0:
                acc[:, n * QB : (n + 1) * QB] = part
            else:
                acc[:, n * QB : (n + 1) * QB] += part
    for c in last:
        c.wait()
    w = jnp.concatenate([two(wo, c) for c in range(wo.shape[0] // 2)], 1)
    out = []
    for i in range(length // QB):
        rows = slice(i * QB, (i + 1) * QB)
        r = r1[rows, :]
        rinv = lax.rsqrt(jnp.mean(r * r, -1, keepdims=True) + EPS)
        n2 = r * rinv
        dn = acc[rows, :] * gain_ref[...]
        dr = df[rows, :].astype(f32) + rinv * (dn - n2 * jnp.mean(dn * n2, -1, keepdims=True))
        acc[rows, :] = dr
        da[rows, :] = dr.astype(bf16)
        do[rows, :] = (nt(da[rows, :], w) * keep_ref[rows, :]).astype(bf16)
        for k, (a, b) in enumerate(((acc, dr_out), (da, da_out), (do, do_out))):
            c = pltpu.make_async_copy(
                a.at[pl.ds(i * QB, QB)], b.at[pl.ds(i * QB, QB)], sem.at[len(chunks) + 3 + 3 * i + k]
            )
            c.start()
            out.append(c)
    for c in out:
        c.wait()


def ffn_back(r1, df, keep_col, gain, dgate, dup, wo, wg, wu):
    length, width = r1.shape
    hidden = dgate.shape[1]
    vmem = pl.BlockSpec(memory_space=pltpu.VMEM)

    return pl.pallas_call(
        ffn_back_body,
        in_specs=[vmem, vmem] + [ANY] * 7,
        out_specs=[ANY] * 3,
        out_shape=[shape((length, width), f32), shape((length, width)), shape((length, width))],
        scratch_shapes=[like(a) for a in (r1, df, wo, dgate, dup, wg, wu, r1, df, df)]
        + [pltpu.SemaphoreType.DMA((7 + 3 * (length // QB),))],
        compiler_params=params(),
        cost_estimate=cost(22),
        name="ffn_back",
    )(gain, keep_col, r1, df, wo, dgate, dup, wg, wu)


def bits(pos):
    d = pos[1]
    return lax.rem(d, 2), lax.rem(d // 2, 2), lax.rem(d // 4, 2)


def sort_out(out, by_x, value, at, own):
    n = value.shape[1]
    for p in range(4):
        bit, other = (p % 2, p // 2) if by_x else (p // 2, p % 2)
        which = jnp.where(own == bit, 0, 1)
        out[which, other, pl.ds(at, n)] = value[p]


def ffn_grads_body(pos, ht_hbm, df_hbm, hid_hbm, dg_hbm, du_hbm, rg_hbm, ru_hbm, rd_hbm,
                   ka_out, ta_out, kb_out, tb_out,
                   ht, df, hid, dg, du, rg, ru, rd, out_a, out_b, sem):
    core, b1, b2 = bits(pos)
    blocks = rg.shape[2]
    chunks = chunked(blocks, 4)
    first = [pltpu.make_async_copy(ht_hbm.at[:, core], ht, sem.at[0])]
    for p in range(4):
        cols = pl.ds(pl.multiple_of((2 * p + core) * L, L), L)
        first.append(pltpu.make_async_copy(df_hbm.at[:, cols], df.at[:, pl.ds(p * L, L)], sem.at[1 + p]))
    at = 5
    loads = {}
    for name, a, b, ra, rb in (("g", dg_hbm, dg, rg_hbm, rg), ("u", du_hbm, du, ru_hbm, ru), ("d", hid_hbm, hid, rd_hbm, rd)):
        for low, size in chunks:
            cols = pl.ds(low * L, size * L)
            if name == "d":
                some = pl.ds(4 * low, 4 * size)
                pair = (ra.at[some], rb.at[some])
            else:
                some = pl.ds(low, size)
                pair = (ra.at[:, :, some], rb.at[:, :, some])
            loads[name, low] = [
                pltpu.make_async_copy(a.at[:, cols], b.at[:, cols], sem.at[at]),
                pltpu.make_async_copy(*pair, sem.at[at + 1]),
            ]
            at += 2
    for c in first:
        c.start()
    for copies in loads.values():
        for c in copies:
            c.start()
    for c in first:
        c.wait()
    left = ht[...].reshape(ht.shape[0] * G, ht.shape[2])
    targets = ((out_a, ka_out, ta_out), (out_b, kb_out, tb_out))
    sent = []

    def send(which, low, size):
        o, *refs = targets[which]
        some = pl.ds(low, size)
        for i, ref in enumerate(refs):
            sent.append(pltpu.make_async_copy(o.at[i, :, some], ref.at[:, some], sem.at[56 + len(sent)]))
            sent[-1].start()

    for name, grad, got, out, by_x, own in (("g", dg, rg, out_a, True, b1), ("u", du, ru, out_b, False, b2)):
        for low, size in chunks:
            for c in loads[name, low]:
                c.wait()
            g = nn(left, grad[:, low * L : (low + size) * L])
            for s in range(4):
                rows = g[s * 4 * G : (s + 1) * 4 * G].reshape(4, G, size * L)
                value = jnp.stack([rows[:, :, c * L : (c + 1) * L] for c in range(size)], 1)
                value = (value + got[s, :, low : low + size].astype(f32)).astype(bf16)
                sort_out(out, by_x, value, s * blocks + low, own)
        send(0 if by_x else 1, 0, 4 * blocks)
    right = df[...]
    for low, size in chunks:
        for c in loads["d", low]:
            c.wait()
        g = tn(hid[:, low * L : (low + size) * L], right)
        n = 4 * size
        value = jnp.stack([g[:, p * L : (p + 1) * L].reshape(n, G, L) for p in range(4)], 0)
        value = value + jnp.stack([rd[4 * low : 4 * low + n, p].astype(f32) for p in range(4)], 0)
        value = value.astype(bf16)
        edge = min(max(2 * blocks - 4 * low, 0), n)
        if edge:
            sort_out(out_a, True, value[:, :edge], 4 * blocks + 4 * low, b1)
        if edge < n:
            sort_out(out_b, False, value[:, edge:], 4 * blocks + 4 * low + edge - 2 * blocks, b2)
    send(0, 4 * blocks, 2 * blocks)
    send(1, 4 * blocks, 2 * blocks)
    for c in sent:
        c.wait()


def ffn_grads(pos, ht, df, hid, dgate, dup, got):
    length, width = df.shape
    hidden = hid.shape[1]
    half = shape((2, 6 * hidden // L, G, L))
    return pl.pallas_call(
        ffn_grads_body,
        in_specs=[SMEM] + [ANY] * 8,
        out_specs=[ANY] * 4,
        out_shape=[half] * 4,
        scratch_shapes=[
            pltpu.VMEM((ht.shape[0], G, length), bf16),
            pltpu.VMEM((length, width // 2), bf16),
        ]
        + [like(a) for a in (hid, dgate, dup, *got)]
        + [pltpu.VMEM((2,) + half.shape, bf16)] * 2
        + [pltpu.SemaphoreType.DMA((64,))],
        compiler_params=params(),
        cost_estimate=cost(17),
        name="ffn_grads",
    )(pos, ht, df, hid, dgate, dup, *got)


def ffn_out_body(r1_ref, hid_ref, wd, out_ref):
    out_ref[...] = (r1_ref[...] + nn(hid_ref[...], two(wd, 0))).astype(bf16)


def ffn_out(r1, hid, wd):
    length, width = r1.shape
    hidden = hid.shape[1]
    col = pl.BlockSpec((length, 2 * L), lambda i: (0, i))
    return pl.pallas_call(
        ffn_out_body,
        grid=(width // (2 * L),),
        in_specs=[col, once(length, hidden), pl.BlockSpec((2, hidden // G, G, L), lambda i: (i, 0, 0, 0))],
        out_specs=col,
        out_shape=shape((length, width)),
        compiler_params=params(),
        cost_estimate=cost(11),
        name="ffn_out",
    )(r1, hid, wd)


def square_body(keep, pos, ot_hbm, ht_hbm, *rest):
    grads_hbm, rest = rest[:4], rest[4:]
    if keep:
        got_hbm, ka_out, ta_out, kb_out, tb_out, ot, ht, da, dq, dk, dv, got, out_a, out_b, sem = rest
    else:
        out_hbm, ot, ht, da, dq, dk, dv, out, sem = rest
    core, b1, b2 = bits(pos)
    grads = (da, dq, dk, dv)
    mine = core if keep else 1 - core
    blocks = da.shape[1] // L
    loads = [pltpu.make_async_copy(a, b, sem.at[i]) for i, (a, b) in enumerate(zip(grads_hbm, grads))]
    lefts = [pltpu.make_async_copy(a.at[:, mine], b, sem.at[4 + i]) for i, (a, b) in enumerate(((ot_hbm, ot), (ht_hbm, ht)))]
    recv = []
    if keep:
        for i in range(4):
            some = pl.ds(i * blocks, blocks)
            recv.append(pltpu.make_async_copy(got_hbm.at[:, :, some], got.at[:, :, some], sem.at[6 + i]))
            recv[i].start()
    lefts[0].start()
    loads[0].start()
    lefts[1].start()
    for c in loads[1:]:
        c.start()
    sent = []

    def send(a, b):
        sent.append(pltpu.make_async_copy(a, b, sem.at[10 + len(sent)]))
        sent[-1].start()

    for i in range(4):
        if i < 2:
            lefts[i].wait()
        loads[i].wait()
        if keep:
            recv[i].wait()
        ref = (ot, ht, ht, ht)[i]
        left = ref[...].reshape(ref.shape[0] * G, ref.shape[2])
        for low, size in chunked(blocks, 4):
            g = nn(left, grads[i][:, low * L : (low + size) * L])
            for s in range(4):
                rows = g[s * 4 * G : (s + 1) * 4 * G].reshape(4, G, size * L)
                value = jnp.stack([rows[:, :, c * L : (c + 1) * L] for c in range(size)], 1)
                at = i * blocks + low
                if not keep:
                    out[s, :, at : at + size] = value.astype(bf16)
                    continue
                value = (value + got[s, :, at : at + size].astype(f32)).astype(bf16)
                at = s * 2 * blocks + (i % 2) * blocks + low
                sort_out(out_a if i < 2 else out_b, i < 2, value, at, b1 if i < 2 else b2)
        if not keep:
            some = pl.ds(i * blocks, blocks)
            send(out.at[:, :, some], out_hbm.at[:, :, some])
        elif i == 1:
            send(out_a.at[0], ka_out)
            send(out_a.at[1], ta_out)
        elif i == 3:
            send(out_b.at[0], kb_out)
            send(out_b.at[1], tb_out)
    for c in sent:
        c.wait()


def square_grads(pos, ot, ht, grads, got):
    length, width = grads[0].shape
    whole = shape((4, 4, 4 * width // L, G, L))
    half = shape((2, 8 * width // L, G, L))
    keep = got is not None
    left = pltpu.VMEM((ht.shape[0], G, length), bf16)
    return pl.pallas_call(
        lambda *refs: square_body(keep, *refs),
        in_specs=[SMEM] + [ANY] * (7 if keep else 6),
        out_specs=[ANY] * 4 if keep else ANY,
        out_shape=[half] * 4 if keep else whole,
        scratch_shapes=[left, left]
        + [like(a) for a in grads]
        + ([like(whole)] + [pltpu.VMEM((2,) + half.shape, bf16)] * 2 if keep else [like(whole)])
        + [pltpu.SemaphoreType.DMA((14,))],
        compiler_params=params(),
        cost_estimate=cost(10),
        name="square_keep" if keep else "square_send",
    )(pos, ot, ht, *grads, *([got] if keep else []))


def input_grad_body(x_ref, gain_ref, dq_hbm, dk_hbm, dv_hbm, wq_hbm, wk_hbm, wv_hbm, dr_hbm, out_hbm,
                    dq, dk, dv, wq, wk, wv, dr, acc, sem):
    length, width = x_ref.shape
    blocks = width // L
    pairs = ((dq_hbm, dq, wq_hbm, wq), (dk_hbm, dk, wk_hbm, wk), (dv_hbm, dv, wv_hbm, wv))
    loads = [
        (pltpu.make_async_copy(a, b, sem.at[2 * i]), pltpu.make_async_copy(c, d, sem.at[2 * i + 1]))
        for i, (a, b, c, d) in enumerate(pairs)
    ]
    get_dr = pltpu.make_async_copy(dr_hbm, dr, sem.at[6])
    for pair in loads:
        for c in pair:
            c.start()
    get_dr.start()
    for i, (_, grad, _, w) in enumerate(pairs):
        for c in loads[i]:
            c.wait()
        for n in range(width // QB):
            rows = slice(n * QB // G, (n + 1) * QB // G)
            part = nt(grad[...], jnp.concatenate([w[c, rows].reshape(QB, L) for c in range(blocks)], 1))
            if i == 0:
                acc[:, n * QB : (n + 1) * QB] = part
            else:
                acc[:, n * QB : (n + 1) * QB] += part
    get_dr.wait()
    out = []
    for i in range(length // QB):
        rows = slice(i * QB, (i + 1) * QB)
        x = x_ref[rows, :].astype(f32)
        rinv = lax.rsqrt(jnp.mean(x * x, -1, keepdims=True) + EPS)
        n1 = x * rinv
        dn = acc[rows, :] * gain_ref[...]
        acc[rows, :] = dr[rows, :] + rinv * (dn - n1 * jnp.mean(dn * n1, -1, keepdims=True))
        out.append(pltpu.make_async_copy(acc.at[pl.ds(i * QB, QB)], out_hbm.at[pl.ds(i * QB, QB)], sem.at[7 + i]))
        out[-1].start()
    for c in out:
        c.wait()


def input_grad(x, gain, dr1, dq, dk, dv, weights):
    length, width = x.shape
    vmem = pl.BlockSpec(memory_space=pltpu.VMEM)
    return pl.pallas_call(
        input_grad_body,
        in_specs=[vmem, vmem] + [ANY] * 7,
        out_specs=ANY,
        out_shape=shape((length, width), f32),
        scratch_shapes=[like(a) for a in (dq, dk, dv, *weights, dr1, dr1)]
        + [pltpu.SemaphoreType.DMA((7 + length // QB,))],
        compiler_params=params(),
        cost_estimate=cost(14),
        name="input_grad",
    )(x, gain, dq, dk, dv, *weights, dr1)


def place_body(tall, pos, *refs):
    pieces, outs = refs[:10], refs[10:]
    blocks = []
    for which, out in enumerate(outs[:-3] if tall else outs):
        blocks += [(which, c) for c in range(out.shape[1] // L)]
    if tall:
        blocks += [(len(outs) - 3, j) for j in range(outs[-3].shape[0] // G)] + [(None, 0)]
    d = pos[1]
    for array, mask, low, size in piece_sources(pieces[0].shape[1]):
        piece = d ^ mask
        rows = pl.ds(pl.multiple_of(piece * G, G), G)
        cols = pl.ds(pl.multiple_of(piece * L, L), L)
        for c in range(size):
            which, at = blocks[low + c]
            value = pieces[array][0, c].astype(f32)
            if which is None:
                outs[-1][piece] = value
            elif tall and which == len(outs) - 3:
                outs[which][at * G : (at + 1) * G, cols] = value
            else:
                outs[which][rows, at * L : (at + 1) * L] = value
    if tall:
        total = outs[-1][0]
        for piece in range(1, 8):
            total = total + outs[-1][piece]
        outs[-2][...] = total


def place(pos, arrays, widths, rows, tall=None):
    vmem = pl.BlockSpec(memory_space=pltpu.VMEM)
    outs = [shape((rows, w), f32) for w in widths]
    if tall is not None:
        outs += [shape(tall, f32), shape((G, L), f32)]
    return pl.pallas_call(
        lambda *refs: place_body(tall is not None, *refs),
        in_specs=[SMEM] + [vmem] * 10,
        out_specs=[vmem] * len(outs),
        out_shape=outs,
        scratch_shapes=[] if tall is None else [pltpu.VMEM((8, G, L), f32)],
        compiler_params=params(),
        name="place",
    )(pos, *arrays)


def layout(lengths, length):
    position = jnp.arange(length, dtype=jnp.int32)
    ends = jnp.cumsum(lengths).astype(jnp.int32)
    seg = jnp.sum((position[:, None] >= ends[None, :]).astype(jnp.int32), 1)
    onehot = seg[:, None] == jnp.arange(lengths.shape[0], dtype=jnp.int32)[None, :]
    first = jnp.sum(jnp.where(onehot, (ends - lengths)[None, :], 0), 1)
    last = jnp.sum(jnp.where(onehot, ends[None, :], 0), 1)
    rel = (position - first).astype(f32)
    inverse = 10000.0 ** (-jnp.arange(HEAD_DIM // 2, dtype=f32) * 2.0 / HEAD_DIM)
    angle = rel[:, None] * inverse[None, :]
    keep = (seg < lengths.shape[0] - 1).astype(f32)
    cos, sin = jnp.cos(angle), jnp.sin(angle)
    cos_w = jnp.concatenate([cos] * 4, 1)
    sin_w = jnp.concatenate([-sin, sin] * 2, 1)
    return cos_w, sin_w, first[None, :], last[None, :], keep[:, None]


def add(*terms):
    total = terms[0].astype(f32)
    for t in terms[1:]:
        total = total + t.astype(f32)
    return total


def halve(kept, got, bit):
    picked = []
    for at in (1 - bit, bit):
        parts = [lax.dynamic_index_in_dim(x, at, 0, keepdims=False) for x in (kept, got)]
        picked.append(add(*parts).astype(bf16))
    return picked


def in_parts(sums):
    parts = []
    for _ in range(3):
        part = lax.reduce_precision(sums, 8, 7)
        parts.append(part)
        sums = sums - part
    return jnp.pad(jnp.stack(parts).astype(bf16), ((0, G - 3), (0, L - 2)))


def from_parts(block):
    parts = block[..., :3, :2].astype(f32)
    return parts[..., 0, :] + parts[..., 1, :] + parts[..., 2, :]


def to_shards(total, z, extra=None):
    terms = [lax.dynamic_index_in_dim(total, z, 0, keepdims=False)]
    if extra is not None:
        terms[0] = jnp.concatenate([terms[0], extra[None]])
    for s in (1, 2, 3):
        away = lax.dynamic_index_in_dim(total, lax.rem(z + s, 4), 0, keepdims=False)
        if extra is not None:
            away = jnp.concatenate([away, extra[None]])
        terms.append(fsdp_shift(away, s))
    return terms


def sums_over_fsdp(terms, z):
    numbers = jnp.stack([from_parts(t[-1]) for t in terms])
    sums = jnp.zeros_like(numbers[0])
    for shard in range(4):
        sums = sums + lax.dynamic_index_in_dim(numbers, lax.rem(z + 4 - shard, 4), 0, keepdims=False)
    return sums


def back_over_dp(reduced):
    g = Gather.__new__(Gather)
    g.count, g.start = reduced.shape[0], reduced[None]
    g.x, g.y = dp_swap(g.start, 2), dp_swap(g.start, 4)
    return g


def unfold_rows(w):
    return w.transpose(0, 2, 1, 3).reshape(w.shape[0] * G, w.shape[1] * L)


def sum_whole(grad):
    part = lax.psum_scatter(grad.astype(bf16), "fsdp", scatter_dimension=0, tiled=True)
    return lax.psum(part, "dp").astype(f32)


def local(
    layer_in, first_values, first_values_grad, cotangent, doc_lengths, norm1_gain,
    w_query, w_key, w_value, w_out, norm2_gain, w_gate, w_up, w_down,
):
    rows, length, width = layer_in.shape
    hidden = w_gate.shape[1]
    dp, fsdp = lax.axis_size("dp"), lax.axis_size("fsdp")
    fast = fast_mesh(dp, fsdp, w_query.shape[0])
    z, d = lax.axis_index("fsdp"), lax.axis_index("dp")
    b1, b2 = lax.rem(d // 2, 2), lax.rem(d // 4, 2)
    x, v1 = layer_in[0], first_values[0]
    df = cotangent[0]
    gains = jnp.stack([norm1_gain, norm2_gain])
    c, h = width // L, hidden // L
    members = (
        ((w_query, w_key, w_value), ((c, True),) * 3),
        ((w_out, w_gate), ((c, True), (h, True))),
        ((w_up, w_down), ((h, True), (w_down.shape[0] // G, False))),
    )
    if fast:
        pos = jnp.stack([z, d]).astype(jnp.int32)
        extra = jnp.pad(gains.reshape(-1, L), ((0, G - gains.size // L), (0, 0)))
        g1 = Gather(cut(pos, *members[0], extra), True)
        far = jnp.stack([e[: gains.size // L].reshape(gains.shape) for e in g1.extras])
        mines = [cut(after(pos, g1.extras[0]), *m) for m in members[1:]]
        g1.near()
        g2 = Gather(after(mines[0], g1.start))
        g1.corner(*g2.far)
        g2.near()
        g3 = Gather(after(mines[1], g2.start))
        g1.core()
        g1.core_corner()
        groups = [Group(members[0][1], members[0][0], g1.arrays(), False)]
        whole_gains = jnp.concatenate(
            [lax.dynamic_index_in_dim(far, lax.rem(z + 4 - j, 4), 0, keepdims=False) for j in range(4)], 1
        )
    else:
        pos = jnp.zeros((2,), jnp.int32)

        def blocks(w, by_rows):
            full = lax.all_gather(w, "fsdp", axis=0, tiled=True)
            return row_pieces(full, full.shape[0] // G).transpose(1, 0, 2, 3) if by_rows else column_pieces(full, c)

        whole_gains = lax.all_gather(gains, "fsdp", axis=1, tiled=True)
        groups = [
            Group(tensors, [], [blocks(w, t[1]) for w, t in zip(weights, tensors)], True)
            for weights, tensors in members
        ]
    whole_gains = whole_gains.astype(f32)
    gain_1, gain_2 = whole_gains[:1], whole_gains[1:]
    cos_w, sin_w, first_row, last_row, keep_col = layout(doc_lengths[0], length)

    q, k, vm, h1t, sums, wq, wk, wv = qkv(pos, x, v1, gain_1, cos_w, sin_w, groups[0])
    squares = jnp.sum(sums, (1, 2))
    entries = rows * length * width * dp * fsdp
    if fast:
        g2.corner(q)
        q = after(q, g2.x, g2.y)
    o, lse_1 = attend_fwd(q, k, vm, last_row, keep_col, 0, 3)
    if fast:
        g3.near(o)
        g2.core(o)
        o = after(o, g2.c1, g2.c2, g3.start)
    o, lse_2 = attend_fwd(q, k, vm, last_row, keep_col, 3, 5, o)
    if fast:
        g3.corner(o)
        g2.core_corner(o)
        g3.core(o)
        g3.core_corner()
        groups += [Group(members[i][1], members[i][0], g.arrays(), False) for i, g in ((1, g2), (2, g3))]
    hid, dgate, dup, sg, su, sd, r1, h2t, ot, wo, wg, wu, wd = ffn(pos, x, o, df, gain_2, groups[1:], hidden)
    got = [dp_swap(g, 1) if fast else jnp.zeros_like(g) for g in (sg, su, sd)]
    dr1, da, do = ffn_back(r1, df, keep_col, gain_2, dgate, dup, wo, wg, wu)
    ka, ta, kb, tb = ffn_grads(pos, h2t, df, hid, dgate, dup, after(got, da))
    if fast:
        na, nb = dp_swap(ta, 2), dp_swap(tb, 4)
    back = (first_row, cos_w, -sin_w, first_values_grad[0])
    results = attend_bwd(q, k, vm, after(do, ta), lse_1.T, *back, 0, 3)
    dq, dk, dv, first_out = attend_bwd(q, k, vm, do, lse_2.T, *back, 3, 5, results)
    grads = (da, dq, dk, dv)
    if fast:
        na, nb = after((na, nb), dq)
        ta, ka = halve(ka, na, b2)
        tb, kb = halve(kb, nb, b1)
        ma, mb = dp_swap(ta, 4), dp_swap(tb, 2)
        grads = after(grads, ta, tb)
    send = square_grads(pos, ot, h1t, grads, None)
    swapped = dp_swap(send, 1) if fast else jnp.zeros_like(send)
    d_x = input_grad(after(x, send), gain_1, dr1, dq, dk, dv, (wq, wk, wv))
    swapped = after(swapped, d_x)
    if fast:
        ma, mb = after((ma, mb), d_x)
        total_a, total_b = add(ka, ma).astype(bf16), add(kb, mb).astype(bf16)
        n = 4 * hidden // L
        cols_a, cols_b = [t[:n].reshape(4, n // 4, G, L) for t in (total_a, total_b)]
        cols_d = jnp.concatenate([total_a[n:], total_b[n:]]).reshape(4, n // 4, G, L)
        wide_terms = to_shards(jnp.concatenate([cols_a, cols_b, cols_d], 1), z, in_parts(squares))
    ks, ts, kt, tt = square_grads(pos, ot, h1t, grads, swapped)
    if fast:
        ns, n_t = dp_swap(ts, 2), dp_swap(tt, 4)
    out = ffn_out(r1, after(hid, ts), wd)
    if fast:
        ns, n_t = after((ns, n_t), out)
        ts, ks = halve(ks, ns, b2)
        tt, kt = halve(kt, n_t, b1)
        ms, mt = dp_swap(ts, 4), dp_swap(tt, 2)
        wide_terms = after(wide_terms, ts, tt)
        reduced = add(*[t[:-1] for t in wide_terms]).astype(bf16)
        wide = back_over_dp(jnp.concatenate([reduced, in_parts(sums_over_fsdp(wide_terms, z))[None]]))
        total_s, total_t = add(ks, ms).astype(bf16), add(kt, mt).astype(bf16)
        both = [t.reshape((4, -1) + t.shape[1:]) for t in (total_s, total_t)]
        last_terms = to_shards(jnp.concatenate(both, 1), z)
        wide.corner(*both)
        wide.core()
        wide.core_corner()
        grad_wg, grad_wu, grad_wd, squares = place(
            pos, wide.arrays(), [hidden] * 2, w_query.shape[0], (w_down.shape[0], width)
        )
        squares = from_parts(squares)
        last = back_over_dp(add(*last_terms).astype(bf16))
        last.corner()
        last.core()
        last.core_corner()
        grad_wo, grad_wq, grad_wk, grad_wv = place(pos, last.arrays(), [width] * 4, w_query.shape[0])
    else:
        squares = lax.psum(squares, ("dp", "fsdp"))
        n = 4 * hidden // L
        even_a, even_b = jnp.stack([ka, ta], 1), jnp.stack([kb, tb], 0)
        even_a, even_b = [e.reshape((4,) + ka.shape[1:]) for e in (even_a, even_b)]
        grad_wg, grad_wu = join(even_a[:, :n], sg), join(even_b[:, :n], su)
        even_d = jnp.concatenate([even_a[:, n:], even_b[:, n:]], 1).transpose(1, 0, 2, 3)
        grad_wd = jnp.stack([even_d, sd], 2).reshape(n, 8, G, L).transpose(0, 2, 1, 3).reshape(hidden, width)
        n = 2 * width // L
        even_s, even_t = jnp.stack([ks, ts], 1), jnp.stack([kt, tt], 0)
        firsts = join(even_s.reshape((4,) + ks.shape[1:]), send[:, :, :n])
        seconds = join(even_t.reshape((4,) + ks.shape[1:]), send[:, :, n:])
        grad_wo, grad_wq = firsts[:, :width], firsts[:, width:]
        grad_wk, grad_wv = seconds[:, :width], seconds[:, width:]
        grad_wo, grad_wq, grad_wk, grad_wv, grad_wg, grad_wu, grad_wd = [
            sum_whole(g) for g in (grad_wo, grad_wq, grad_wk, grad_wv, grad_wg, grad_wu, grad_wd)
        ]
    def along(*pairs):
        return sum(jnp.sum(w.astype(f32) * g, 1) for w, g in pairs)

    grad_g1 = along((w_query, grad_wq), (w_key, grad_wk), (w_value, grad_wv)) / norm1_gain.astype(f32)
    grad_g2 = along((w_gate, grad_wg), (w_up, grad_wu)) / norm2_gain.astype(f32)
    return (
        out[None], d_x[None], first_out[None], grad_g1, grad_wq, grad_wk, grad_wv, grad_wo, grad_g2,
        grad_wg, grad_wu, grad_wd, squares / entries,
    )


def join(even, odd):
    even = even.reshape((4, 4, -1) + even.shape[2:]).transpose(1, 0, 2, 3, 4)
    both = jnp.stack([even, odd], 2)
    return unfold_rows(both.reshape((32,) + odd.shape[2:]))


def solution(mesh):
    by_row = P(("dp", "fsdp"), None, None)
    shard = P("fsdp", None)
    return jax.shard_map(
        local,
        mesh=mesh,
        in_specs=(by_row,) * 4
        + (P(("dp", "fsdp"), None), P("fsdp"), shard, shard, shard, shard, P("fsdp"), shard, shard, shard),
        out_specs=(by_row,) * 3
        + (P("fsdp"), shard, shard, shard, shard, P("fsdp"), shard, shard, shard, P()),
        check_vma=False,
    )
```

```python
import jax
import jax.numpy as jnp
from jax import lax
from jax.experimental import pallas as pl
from jax.experimental.pallas import tpu as pltpu
from jax.sharding import PartitionSpec as P

HEADS = 16
HEAD_DIM = 64
EPS = 1e-06
NEG = -1e30
COST = 4e9
QB = 256
G = 32
L = 128
bf16 = jnp.bfloat16
f32 = jnp.float32
ANY = pl.BlockSpec(memory_space=pl.ANY)
SMEM = pl.BlockSpec(memory_space=pltpu.SMEM)


def params(mib=58):
    return pltpu.CompilerParams(vmem_limit_bytes=mib * 2**20)


def cost(us):
    return pl.CostEstimate(flops=int(us * COST), bytes_accessed=0, transcendentals=0)


def shape(dims, dtype=bf16):
    return jax.ShapeDtypeStruct(dims, dtype)


def nt(a, b):
    return lax.dot_general(a, b, (((1,), (1,)), ((), ())), preferred_element_type=f32)


def nn(a, b):
    return lax.dot_general(a, b, (((1,), (0,)), ((), ())), preferred_element_type=f32)


def tn(a, b):
    return lax.dot_general(a, b, (((0,), (0,)), ((), ())), preferred_element_type=f32)


def fast_mesh(dp, fsdp, shard_rows):
    return dp == 8 and fsdp == 4 and shard_rows == 8 * G


def row_pieces(w, count):
    return w.reshape(count, G, w.shape[1] // L, L).transpose(0, 2, 1, 3)


def column_pieces(w, count):
    return w.reshape(w.shape[0] // G, G, count, L).transpose(2, 0, 1, 3)


def dp_swap(x, bit):
    return lax.ppermute(x, "dp", [(i, i ^ bit) for i in range(lax.axis_size("dp"))])


def after(x, *first):
    return lax.optimization_barrier((x, first))[0]


def fsdp_shift(x, step):
    size = lax.axis_size("fsdp")
    return lax.ppermute(x, "fsdp", [(i, (i + step) % size) for i in range(size)])


class Gather:
    def __init__(self, sent, extra=False):
        self.count = sent.shape[0] - extra
        self.far = [fsdp_shift(sent, s) for s in (1, 2, 3)]
        self.extras = [x[self.count] for x in [sent] + self.far] if extra else None

    def near(self, *gate):
        self.start = jnp.stack([x[: self.count] for x in after(self.far, *gate)])
        self.x, self.y = dp_swap(self.start, 2), dp_swap(self.start, 4)

    def corner(self, *gate):
        cut = self.count // 2
        self.c1 = dp_swap(after(self.x[:, :cut], *gate), 4)
        self.c2 = dp_swap(after(self.y[:, cut:], *gate), 2)

    def core(self, *gate):
        self.other = [dp_swap(after(a, *gate), 1) for a in (self.start, self.x, self.y)]

    def core_corner(self, *gate):
        self.other += [dp_swap(after(a, *gate), 1) for a in (self.c1, self.c2)]

    def arrays(self):
        return [self.start, self.x, self.y, self.c1, self.c2] + self.other


def piece_sources(count):
    cut = count // 2
    found = []
    for core in range(2):
        for i, (mask, low, size) in enumerate(
            ((0, 0, count), (2, 0, count), (4, 0, count), (6, 0, cut), (6, cut, count - cut))
        ):
            found.append((5 * core + i, mask | core, low, size))
    return found


class Group:
    def __init__(self, tensors, owned, arrays, whole):
        self.tensors, self.whole, self.owned = tensors, whole, len(owned)
        self.arrays = list(owned) + list(arrays)

    def specs(self):
        return [ANY] * len(self.arrays)

    def fetch(self, index, refs, pos, scratch, sem):
        if self.whole:
            pltpu.make_async_copy(refs[index], scratch, sem).start()
            return
        z, d = pos[0], pos[1]
        at = sum(t[0] for t in self.tensors[:index])
        blocks, by_rows = self.tensors[index]

        def target(shard, piece, low, size):
            if by_rows:
                return scratch.at[pl.ds(low, size), shard * 8 + piece]
            return scratch.at[piece, pl.ds(shard * blocks + low, size)]

        own = refs[index]
        rows = own.shape[0]
        flat = scratch.reshape(scratch.shape[0], scratch.shape[1] * G, L)
        for c in range(scratch.shape[0]):
            pltpu.make_async_copy(
                own.at[:, pl.ds(c * L, L)], flat.at[c, pl.ds(pl.multiple_of(z * rows, G), rows)], sem
            ).start()
        for array, mask, low, size in piece_sources(sum(t[0] for t in self.tensors)):
            begin, end = max(at, low), min(at + blocks, low + size)
            if end <= begin:
                continue
            for s in range(3):
                pltpu.make_async_copy(
                    refs[self.owned + array].at[s, pl.ds(begin - low, end - begin)],
                    target(lax.rem(z + 3 - s, 4), d ^ mask, begin - at, end - begin),
                    sem,
                ).start()


def cut_body(tensors, gains, pos, *refs):
    count = len(tensors)
    weights, refs = refs[:count], refs[count:]
    if gains:
        gain_ref, refs = refs[0], refs[1:]
    out, stages, sem = refs[0], refs[1:-1], refs[-1]
    d = pos[1]
    copies = []
    for i, (blocks, by_rows) in enumerate(tensors):
        rows = pl.ds(pl.multiple_of(d * G, G), G)
        cols = pl.ds(pl.multiple_of(d * L, L), L)
        part = weights[i].at[rows] if by_rows else weights[i].at[:, cols]
        copies.append(pltpu.make_async_copy(part, stages[i], sem.at[i]))
    for c in copies:
        c.start()
    at = 0
    for i, (blocks, by_rows) in enumerate(tensors):
        copies[i].wait()
        if by_rows:
            for c in range(blocks):
                out[at + c] = stages[i][:, c * L : (c + 1) * L]
        else:
            out[at : at + blocks] = stages[i][...].reshape(blocks, G, L)
        at += blocks
    if gains:
        out[at] = gain_ref[...]


def cut(pos, weights, tensors, gains=None):
    vmem = pl.BlockSpec(memory_space=pltpu.VMEM)
    total = sum(t[0] for t in tensors) + (gains is not None)
    stages = [
        pltpu.VMEM((G, w.shape[1]) if by_rows else (w.shape[0], L), bf16) for w, (_, by_rows) in zip(weights, tensors)
    ]
    return pl.pallas_call(
        lambda *refs: cut_body(tensors, gains is not None, *refs),
        in_specs=[SMEM] + [ANY] * len(weights) + ([] if gains is None else [vmem]),
        out_specs=vmem,
        out_shape=shape((total, G, L)),
        scratch_shapes=stages + [pltpu.SemaphoreType.DMA((len(weights),))],
        compiler_params=params(),
        name="cut",
    )(pos, *weights, *([] if gains is None else [gains]))


def wait_all(scratch, sem):
    pltpu.make_async_copy(scratch, scratch, sem).wait()


def two(w, i):
    rows = w.shape[1] * w.shape[2]
    return jnp.concatenate([w[2 * i].reshape(rows, L), w[2 * i + 1].reshape(rows, L)], 1)


def swap_halves(t):
    lane = lax.broadcasted_iota(jnp.int32, t.shape, 1) % 64
    return jnp.where(lane < 32, pltpu.roll(t, 96, 1), pltpu.roll(t, 32, 1))


def chunked(blocks, size):
    return [(low, min(size, blocks - low)) for low in range(0, blocks, size)]


def beside(w, low, size):
    rows = w.shape[1] * G
    return jnp.concatenate([w[low + c].reshape(rows, L) for c in range(size)], 1)


def like(a):
    return pltpu.VMEM(a.shape, a.dtype)


def qkv_body(group, pos, gain_ref, cos_ref, sin_ref, x_ref, v1_hbm, *rest):
    count = len(group.arrays)
    w_refs = rest[:count]
    (q_out, k_out, v_out, ht_out, sums_ref, wq_out, wk_out, wv_out,
     v1, wq, wk, wv, h, ht, q, k, v, sem) = rest[count:]
    length, width = x_ref.shape
    blocks = width // L
    for i, w in enumerate((wq, wk, wv)):
        group.fetch(i, w_refs, pos, w, sem.at[i])
    get_v1 = pltpu.make_async_copy(v1_hbm, v1, sem.at[3])
    get_v1.start()
    for i in range(length // QB):
        rows = slice(i * QB, (i + 1) * QB)
        x = x_ref[rows, :].astype(f32)
        n = x * lax.rsqrt(jnp.mean(x * x, -1, keepdims=True) + EPS) * gain_ref[...]
        h[rows, :] = n.astype(bf16)
        ht[:, :, :, rows] = n.T.astype(bf16).reshape(ht.shape[:3] + (QB,))
    out = [pltpu.make_async_copy(ht, ht_out, sem.at[4])]
    out[0].start()
    cos, sin = cos_ref[...], sin_ref[...]
    at = 5

    def send(a, b):
        out.append(pltpu.make_async_copy(a, b, sem.at[at + len(out) - 1]))
        out[-1].start()

    sums_ref[...] = jnp.zeros_like(sums_ref)
    for i, (w, w_out, t, t_out) in enumerate(((wq, wq_out, q, q_out), (wk, wk_out, k, k_out), (wv, wv_out, v, v_out))):
        wait_all(w, sem.at[i])
        send(w, w_out)
        if i == 2:
            get_v1.wait()
        for low, size in chunked(blocks, 2):
            cols = slice(low * L, (low + size) * L)
            got = nn(h[...], beside(w, low, size))
            if i == 2:
                first = v1[:, cols].astype(f32)
                mixed = (0.5 * got + 0.5 * first).astype(bf16)
                v[:, cols] = mixed
                mixed = mixed.astype(f32)
                sums_ref[0] += jnp.sum((first * first).reshape(length // 8, 8, size * L), 0)
                sums_ref[1] += jnp.sum((mixed * mixed).reshape(length // 8, 8, size * L), 0)
                continue
            for c in range(size):
                part = got[:, c * L : (c + 1) * L]
                part = (part * cos + swap_halves(part) * sin).astype(bf16)
                if i == 0:
                    part = (part.astype(f32) * 0.125).astype(bf16)
                t[:, (low + c) * L : (low + c + 1) * L] = part
        send(t, t_out)
    for c in out:
        c.wait()


def qkv(pos, x, v1, gain, cos_w, sin_w, group):
    length, width = x.shape
    blocks = width // L
    vmem = pl.BlockSpec(memory_space=pltpu.VMEM)
    weight = shape((blocks, width // G, G, L))
    ht = shape((width // G // 2, 2, G, length))
    return pl.pallas_call(
        lambda *refs: qkv_body(group, *refs),
        in_specs=[SMEM, vmem, vmem, vmem, vmem, ANY] + group.specs(),
        out_specs=[ANY] * 4 + [vmem] + [ANY] * 3,
        out_shape=[shape((length, width))] * 3 + [ht, shape((2, 8, 2 * L), f32)] + [weight] * 3,
        scratch_shapes=[like(a) for a in (v1, weight, weight, weight, x, ht, x, x, x)]
        + [pltpu.SemaphoreType.DMA((12,))],
        compiler_params=params(),
        cost_estimate=cost(15),
        name="qkv",
    )(pos, gain, cos_w, sin_w, x, v1, *group.arrays)


def half_mask(rows, which):
    lane = lax.broadcasted_iota(jnp.int32, (rows, 128), 1)
    return (lane < 64) if which == 0 else (lane >= 64)


def pick(x, which, other=None):
    return jnp.where(half_mask(x.shape[0], which), x, jnp.zeros_like(x) if other is None else other)


def marks(seg, docs):
    lane = jnp.arange(128, dtype=jnp.int32)[None, :] % 64
    same = lane == seg[:, None]
    return jnp.where((lane < docs) & ~same, NEG, 0.0).astype(bf16), same.astype(bf16)


def key_blocks(length):
    return length // 2 // QB + 1


def attend_fwd_body(q_ref, k_ref, v_ref, qm_ref, km_ref, keep_ref, *rest):
    o_ref, lse_ref = rest[-2:]
    pair = pl.program_id(0)
    length = q_ref.shape[0]
    blocks = length // QB
    most = key_blocks(length)
    row, col = [lax.broadcasted_iota(jnp.int32, (QB, QB), a) for a in (0, 1)]
    causal = jnp.where(row >= col, 0.0, NEG)
    keys = [pick(k_ref[...], h, km_ref[...]) for h in range(2)]
    lane = lax.broadcasted_iota(jnp.int32, (QB, 128), 1)

    work = [(i, h) for i in range(blocks) for h in range(2)]

    def span(i):
        return slice(max(0, i + 1 - most) * QB, (i + 1) * QB)

    def scores(i, h):
        rows = slice(i * QB, (i + 1) * QB)
        return nt(pick(q_ref[rows, :], h, qm_ref[rows, :]), keys[h][span(i), :])

    ahead = scores(*work[0])
    outs, stats = {}, {}
    for at, (i, h) in enumerate(work):
        rows = slice(i * QB, (i + 1) * QB)
        s = ahead + causal if i == 0 else jnp.concatenate([ahead[:, :-QB], ahead[:, -QB:] + causal], 1)
        if at + 1 < len(work):
            ahead = scores(*work[at + 1])
        top = jnp.max(s, -1, keepdims=True)
        expo = jnp.exp(s - top)
        total = jnp.sum(expo, -1, keepdims=True)
        outs[h] = nn(expo.astype(bf16), v_ref[span(i), :]) / total
        stats[h] = top + jnp.log(total)
        if h == 1:
            old = jnp.where(lane == 2 * pair, stats[0], lse_ref[rows, :])
            lse_ref[rows, :] = jnp.where(lane == 2 * pair + 1, stats[1], old)
            o = jnp.where(lane < 64, outs[0], outs[1]) * keep_ref[rows, :]
            o_ref[rows, :] = o.astype(bf16)


def attend_fwd(q, k, v, q_mark, k_mark, keep_col, first, pairs, before=None):
    length, width = q.shape
    col = pl.BlockSpec((length, 128), lambda p: (0, p + first))
    return pl.pallas_call(
        attend_fwd_body,
        grid=(pairs,),
        in_specs=[
            col,
            col,
            col,
            pl.BlockSpec((length, 128), lambda p: (0, 0)),
            pl.BlockSpec((length, 128), lambda p: (0, 0)),
            pl.BlockSpec((length, 1), lambda p: (0, 0)),
        ]
        + ([] if before is None else [ANY]),
        out_specs=[col, pl.BlockSpec((length, 128), lambda p: (0, 0))],
        out_shape=[
            jax.ShapeDtypeStruct((length, width), bf16),
            jax.ShapeDtypeStruct((length, 128), f32),
        ],
        compiler_params=params(),
        cost_estimate=cost(4.2 * pairs),
        input_output_aliases={} if before is None else {6: 0},
        name="attend_fwd",
    )(q, k, v, q_mark, k_mark, keep_col, *([] if before is None else [before]))


def attend_bwd_body(
    q_ref, k_ref, v_ref, do_ref, lse_ref, qm_ref, km_ref, cos_ref, sin_ref, fg_ref, *rest,
):
    dq_ref, dk_ref, dv_ref, fo_ref, dk_acc, dv_acc = rest[-6:]
    pair = pl.program_id(0)
    length = q_ref.shape[0]
    blocks = length // QB
    most = key_blocks(length)
    row, col = [lax.broadcasted_iota(jnp.int32, (QB, QB), a) for a in (0, 1)]
    causal = jnp.where(row <= col, 0.0, NEG)
    marked = [pick(k_ref[...], h, km_ref[...]) for h in range(2)]
    k_t = k_ref[...].astype(f32).T.astype(bf16)
    dk_acc[...] = jnp.zeros_like(dk_acc)
    dv_acc[...] = jnp.zeros_like(dv_acc)

    work = [(i, h) for i in reversed(range(blocks)) for h in range(2)]

    def products(i, h):
        rows = slice(i * QB, (i + 1) * QB)
        keys = slice(max(0, i + 1 - most) * QB, (i + 1) * QB)
        qh = pick(q_ref[rows, :], h)
        dh = pick(do_ref[rows, :], h)
        qm = pick(q_ref[rows, :], h, qm_ref[rows, :])
        return qh, dh, nt(marked[h][keys, :], qm), nt(v_ref[keys, :], dh)

    ahead = products(*work[0])
    part_q = []
    for at, (i, h) in enumerate(work):
        rows = slice(i * QB, (i + 1) * QB)
        keys = slice(max(0, i + 1 - most) * QB, (i + 1) * QB)
        qh, dh, s, dp = ahead
        if at + 1 < len(work):
            ahead = products(*work[at + 1])
        lse = lse_ref[pl.ds(2 * pair + h, 1), rows]
        s = s + causal if i == 0 else jnp.concatenate([s[:-QB], s[-QB:] + causal], 0)
        p = jnp.exp(s - lse)
        delta = jnp.sum(p * dp, 0, keepdims=True)
        ds = (p * (dp - delta)).astype(bf16)
        dv_acc[keys, :] += nn(p.astype(bf16), dh)
        dk_acc[keys, :] += nn(ds, qh)
        part_q.append(nn(k_t[h * 64 : (h + 1) * 64, keys], ds))
        if h == 1:
            dq = jnp.concatenate(part_q, 0).T * 0.125
            part_q = []
            dq = dq * cos_ref[rows, :] + swap_halves(dq) * sin_ref[rows, :]
            dq_ref[rows, :] = dq.astype(bf16)
    dk = dk_acc[...]
    dk_ref[...] = (dk * cos_ref[...] + swap_halves(dk) * sin_ref[...]).astype(bf16)
    dv = dv_acc[...].astype(bf16).astype(f32) * 0.5
    dv_ref[...] = dv.astype(bf16)
    fo_ref[...] = fg_ref[...] + dv


def attend_bwd(q, k, v, do, lse_t, q_mark, k_mark, cos_w, sin_back, fgrad, first, pairs, before=None):
    length, width = q.shape
    col = pl.BlockSpec((length, 128), lambda p: (0, p + first))
    before = [] if before is None else list(before)

    def whole(a):
        return pl.BlockSpec(a.shape, lambda p: (0, 0))

    wide = jax.ShapeDtypeStruct((length, width), bf16)
    return pl.pallas_call(
        attend_bwd_body,
        grid=(pairs,),
        in_specs=[col] * 4 + [whole(lse_t), whole(q_mark), whole(k_mark), whole(cos_w), whole(sin_back), col]
        + [ANY] * len(before),
        out_specs=[col] * 4,
        out_shape=[wide, wide, wide, jax.ShapeDtypeStruct((length, width), f32)],
        scratch_shapes=[
            pltpu.VMEM((length, 128), f32),
            pltpu.VMEM((length, 128), f32),
        ],
        compiler_params=params(),
        cost_estimate=cost(5.5 * pairs),
        input_output_aliases={10 + i: i for i in range(len(before))},
        name="attend_bwd",
    )(q, k, v, do, lse_t, q_mark, k_mark, cos_w, sin_back, fgrad, *before)


def chosen_columns(ref, parity):
    blocks = ref.shape[1] // L
    return jnp.concatenate(
        [ref[:, pl.ds(pl.multiple_of((2 * p + parity) * L, L), L)] for p in range(blocks // 2)], 1
    )


def chosen_rows(ref, parity):
    return ref[:, parity].reshape(ref.shape[0] * G, ref.shape[3])


def wd_rows(wd, t):
    return jnp.concatenate([wd[c, pl.ds(8 * t, 8)].reshape(8 * G, L) for c in range(wd.shape[0])], 1)


def pair_at(w, t):
    rows = w.shape[1] * G
    return jnp.concatenate([w[2 * t].reshape(rows, L), w[2 * t + 1].reshape(rows, L)], 1)


def once(*dims):
    return pl.BlockSpec(dims, lambda i: (0,) * len(dims), pipeline_mode=pl.Buffered(1))


def ffn_body(groups, pos, x_ref, o_ref, gain_ref, df_hbm, *rest):
    count = [len(g.arrays) for g in groups]
    refs, rest = rest[: sum(count)], rest[sum(count) :]
    of = [refs[: count[0]], refs[count[0] :]]
    (hid_ref, dg_ref, du_ref, sg_ref, su_ref, sd_ref, r1_out, ht_out, ot_out,
     wo_out, wg_out, wu_out, wd_out,
     wo, wg, wu, wd, r1, h2, ht, ot, df, dfs, hts, sem) = rest
    step = pl.program_id(0)
    length = x_ref.shape[0]
    outs = ((r1, r1_out), (ht, ht_out), (ot, ot_out), (wo, wo_out), (wg, wg_out), (wu, wu_out), (wd, wd_out))

    @pl.when(step == 0)
    def _():
        groups[0].fetch(0, of[0], pos, wo, sem.at[0])
        groups[0].fetch(1, of[0], pos, wg, sem.at[1])
        groups[1].fetch(0, of[1], pos, wu, sem.at[2])
        pltpu.make_async_copy(df_hbm, df, sem.at[4]).start()
        groups[1].fetch(1, of[1], pos, wd, sem.at[3])
        other = 1 - lax.rem(pos[1], 2)
        wait_all(wo, sem.at[0])
        w = jnp.concatenate([two(wo, c) for c in range(wo.shape[0] // 2)], 1)
        for i in range(length // QB):
            rows = slice(i * QB, (i + 1) * QB)
            r = x_ref[rows, :].astype(f32) + nn(o_ref[rows, :], w)
            r1[rows, :] = r
            h = r * lax.rsqrt(jnp.mean(r * r, -1, keepdims=True) + EPS) * gain_ref[...]
            h2[rows, :] = h.astype(bf16)
            ht[:, :, :, rows] = h.T.astype(bf16).reshape(ht.shape[:3] + (QB,))
            ot[:, :, :, rows] = o_ref[rows, :].astype(f32).T.astype(bf16).reshape(ht.shape[:3] + (QB,))
        hts[...] = chosen_rows(ht, other)
        wait_all(df, sem.at[4])
        dfs[...] = chosen_columns(df, other)
        wait_all(wg, sem.at[1])
        wait_all(wu, sem.at[2])
        wait_all(wd, sem.at[3])
        for i, (a, b) in enumerate(outs):
            pltpu.make_async_copy(a, b, sem.at[5 + i]).start()

    @pl.when(step > 0)
    def _():
        t = step - 1
        wgt, wut, wdt = pair_at(wg, t), pair_at(wu, t), wd_rows(wd, t)
        for i in range(length // QB):
            rows = slice(i * QB, (i + 1) * QB)
            gate = nn(h2[rows, :], wgt)
            up = nn(h2[rows, :], wut)
            dhid = nt(df[rows, :], wdt)
            sigma = 0.5 + 0.5 * jnp.tanh(0.5 * gate)
            silu = gate * sigma
            hid_ref[rows, :] = (silu * up).astype(bf16)
            dg_ref[rows, :] = (dhid * up * (sigma + silu * (1.0 - sigma))).astype(bf16)
            du_ref[rows, :] = (dhid * silu).astype(bf16)
        gd = tn(hid_ref[...], dfs[...]).astype(bf16)
        for p in range(4):
            sd_ref[:, p] = gd[:, p * L : (p + 1) * L].reshape(8, G, L)
        for ref, grad in ((sg_ref, dg_ref), (su_ref, du_ref)):
            g = nn(hts[...], grad[...]).astype(bf16)
            for c in range(2):
                ref[:, :, c] = g[:, c * L : (c + 1) * L].reshape(4, 4, G, L)

    @pl.when(step == pl.num_programs(0) - 1)
    def _():
        for i, (a, b) in enumerate(outs):
            pltpu.make_async_copy(a, b, sem.at[5 + i]).wait()


def ffn(pos, x, o, df, gain, groups, hidden):
    length, width = x.shape
    tiles = hidden // (2 * L)

    def late(i):
        return jnp.maximum(i - 1, 0)

    col = pl.BlockSpec((length, 2 * L), lambda i: (0, late(i)))
    grad_cols = pl.BlockSpec((4, 4, 2, G, L), lambda i: (0, 0, late(i), 0, 0))
    grad_rows = pl.BlockSpec((8, 4, G, L), lambda i: (late(i), 0, 0, 0))
    ht_dims = (width // G // 2, 2, G, length)
    square, wide = (width // L, width // G, G, L), (hidden // L, width // G, G, L)
    tall = (width // L, hidden // G, G, L)
    kept = [((length, width), f32), (ht_dims, bf16), (ht_dims, bf16)]
    kept += [(square, bf16), (wide, bf16), (wide, bf16), (tall, bf16)]
    vmem = [pltpu.VMEM(*a) for a in kept]
    return pl.pallas_call(
        lambda *refs: ffn_body(groups, *refs),
        grid=(1 + tiles,),
        in_specs=[SMEM, once(length, width), once(length, width), once(1, width), ANY]
        + [s for g in groups for s in g.specs()],
        out_specs=[col, col, col, grad_cols, grad_cols, grad_rows] + [ANY] * 7,
        out_shape=[
            shape((length, hidden)),
            shape((length, hidden)),
            shape((length, hidden)),
            shape((4, 4, hidden // L, G, L)),
            shape((4, 4, hidden // L, G, L)),
            shape((hidden // G, 4, G, L)),
        ]
        + [shape(*a) for a in kept],
        scratch_shapes=vmem[3:]
        + [
            vmem[0],
            pltpu.VMEM((length, width), bf16),
            vmem[1],
            vmem[2],
            pltpu.VMEM((length, width), bf16),
            pltpu.VMEM((length, width // 2), bf16),
            pltpu.VMEM((width // 2, length), bf16),
            pltpu.SemaphoreType.DMA((12,)),
        ],
        compiler_params=params(),
        cost_estimate=cost(46),
        name="ffn",
    )(pos, x, o, gain, df, *[a for g in groups for a in g.arrays])


def ffn_back_body(gain_ref, keep_ref, r1_hbm, df_hbm, wo_hbm, dg_hbm, du_hbm, wg_hbm, wu_hbm,
                  dr_out, da_out, do_out, r1, df, wo, dg, du, wg, wu, acc, da, do, sem):
    length, width = r1.shape
    chunks = chunked(wg.shape[0], 6)
    loads = []
    for i, (low, size) in enumerate(chunks):
        cols = pl.ds(low * L, size * L)
        loads.append(
            [
                pltpu.make_async_copy(a.at[:, cols] if flat else a.at[pl.ds(low, size)],
                                      b.at[:, cols] if flat else b.at[pl.ds(low, size)], sem.at[i])
                for a, b, flat in ((dg_hbm, dg, 1), (wg_hbm, wg, 0), (du_hbm, du, 1), (wu_hbm, wu, 0))
            ]
        )
    last = [pltpu.make_async_copy(a, b, sem.at[len(chunks) + i]) for i, (a, b) in
            enumerate(((r1_hbm, r1), (df_hbm, df), (wo_hbm, wo)))]
    for copies in loads + [last]:
        for c in copies:
            c.start()
    for (low, size), copies in zip(chunks, loads):
        for c in copies:
            c.wait()
        both = jnp.concatenate([a[:, low * L : (low + size) * L] for a in (dg, du)], 1)
        for n in range(width // QB):
            rows = slice(n * QB // G, (n + 1) * QB // G)
            w = jnp.concatenate(
                [a[low + c, rows].reshape(QB, L) for a in (wg, wu) for c in range(size)], 1
            )
            part = nt(both, w)
            if low == 0:
                acc[:, n * QB : (n + 1) * QB] = part
            else:
                acc[:, n * QB : (n + 1) * QB] += part
    for c in last:
        c.wait()
    w = jnp.concatenate([two(wo, c) for c in range(wo.shape[0] // 2)], 1)
    out = []
    for i in range(length // QB):
        rows = slice(i * QB, (i + 1) * QB)
        r = r1[rows, :]
        rinv = lax.rsqrt(jnp.mean(r * r, -1, keepdims=True) + EPS)
        n2 = r * rinv
        dn = acc[rows, :] * gain_ref[...]
        dr = df[rows, :].astype(f32) + rinv * (dn - n2 * jnp.mean(dn * n2, -1, keepdims=True))
        acc[rows, :] = dr
        da[rows, :] = dr.astype(bf16)
        do[rows, :] = (nt(da[rows, :], w) * keep_ref[rows, :]).astype(bf16)
        for k, (a, b) in enumerate(((acc, dr_out), (da, da_out), (do, do_out))):
            c = pltpu.make_async_copy(
                a.at[pl.ds(i * QB, QB)], b.at[pl.ds(i * QB, QB)], sem.at[len(chunks) + 3 + 3 * i + k]
            )
            c.start()
            out.append(c)
    for c in out:
        c.wait()


def ffn_back(r1, df, keep_col, gain, dgate, dup, wo, wg, wu):
    length, width = r1.shape
    hidden = dgate.shape[1]
    vmem = pl.BlockSpec(memory_space=pltpu.VMEM)

    return pl.pallas_call(
        ffn_back_body,
        in_specs=[vmem, vmem] + [ANY] * 7,
        out_specs=[ANY] * 3,
        out_shape=[shape((length, width), f32), shape((length, width)), shape((length, width))],
        scratch_shapes=[like(a) for a in (r1, df, wo, dgate, dup, wg, wu, r1, df, df)]
        + [pltpu.SemaphoreType.DMA((7 + 3 * (length // QB),))],
        compiler_params=params(),
        cost_estimate=cost(22),
        name="ffn_back",
    )(gain, keep_col, r1, df, wo, dgate, dup, wg, wu)


def bits(pos):
    d = pos[1]
    return lax.rem(d, 2), lax.rem(d // 2, 2), lax.rem(d // 4, 2)


def sort_out(out, by_x, value, at, own):
    n = value.shape[1]
    for p in range(4):
        bit, other = (p % 2, p // 2) if by_x else (p // 2, p % 2)
        which = jnp.where(own == bit, 0, 1)
        out[which, other, pl.ds(at, n)] = value[p]


def ffn_grads_body(pos, ht_hbm, df_hbm, hid_hbm, dg_hbm, du_hbm, rg_hbm, ru_hbm, rd_hbm,
                   ka_out, ta_out, kb_out, tb_out,
                   ht, df, hid, dg, du, rg, ru, rd, out_a, out_b, sem):
    core, b1, b2 = bits(pos)
    blocks = rg.shape[2]
    chunks = chunked(blocks, 4)
    first = [pltpu.make_async_copy(ht_hbm.at[:, core], ht, sem.at[0])]
    for p in range(4):
        cols = pl.ds(pl.multiple_of((2 * p + core) * L, L), L)
        first.append(pltpu.make_async_copy(df_hbm.at[:, cols], df.at[:, pl.ds(p * L, L)], sem.at[1 + p]))
    at = 5
    loads = {}
    for name, a, b, ra, rb in (("g", dg_hbm, dg, rg_hbm, rg), ("u", du_hbm, du, ru_hbm, ru), ("d", hid_hbm, hid, rd_hbm, rd)):
        for low, size in chunks:
            cols = pl.ds(low * L, size * L)
            if name == "d":
                some = pl.ds(4 * low, 4 * size)
                pair = (ra.at[some], rb.at[some])
            else:
                some = pl.ds(low, size)
                pair = (ra.at[:, :, some], rb.at[:, :, some])
            loads[name, low] = [
                pltpu.make_async_copy(a.at[:, cols], b.at[:, cols], sem.at[at]),
                pltpu.make_async_copy(*pair, sem.at[at + 1]),
            ]
            at += 2
    for c in first:
        c.start()
    for copies in loads.values():
        for c in copies:
            c.start()
    for c in first:
        c.wait()
    left = ht[...].reshape(ht.shape[0] * G, ht.shape[2])
    targets = ((out_a, ka_out, ta_out), (out_b, kb_out, tb_out))
    sent = []

    def send(which, low, size):
        o, *refs = targets[which]
        some = pl.ds(low, size)
        for i, ref in enumerate(refs):
            sent.append(pltpu.make_async_copy(o.at[i, :, some], ref.at[:, some], sem.at[56 + len(sent)]))
            sent[-1].start()

    for name, grad, got, out, by_x, own in (("g", dg, rg, out_a, True, b1), ("u", du, ru, out_b, False, b2)):
        for low, size in chunks:
            for c in loads[name, low]:
                c.wait()
            g = nn(left, grad[:, low * L : (low + size) * L])
            for s in range(4):
                rows = g[s * 4 * G : (s + 1) * 4 * G].reshape(4, G, size * L)
                value = jnp.stack([rows[:, :, c * L : (c + 1) * L] for c in range(size)], 1)
                value = (value + got[s, :, low : low + size].astype(f32)).astype(bf16)
                sort_out(out, by_x, value, s * blocks + low, own)
        send(0 if by_x else 1, 0, 4 * blocks)
    right = df[...]
    for low, size in chunks:
        for c in loads["d", low]:
            c.wait()
        g = tn(hid[:, low * L : (low + size) * L], right)
        n = 4 * size
        value = jnp.stack([g[:, p * L : (p + 1) * L].reshape(n, G, L) for p in range(4)], 0)
        value = value + jnp.stack([rd[4 * low : 4 * low + n, p].astype(f32) for p in range(4)], 0)
        value = value.astype(bf16)
        edge = min(max(2 * blocks - 4 * low, 0), n)
        if edge:
            sort_out(out_a, True, value[:, :edge], 4 * blocks + 4 * low, b1)
        if edge < n:
            sort_out(out_b, False, value[:, edge:], 4 * blocks + 4 * low + edge - 2 * blocks, b2)
    send(0, 4 * blocks, 2 * blocks)
    send(1, 4 * blocks, 2 * blocks)
    for c in sent:
        c.wait()


def ffn_grads(pos, ht, df, hid, dgate, dup, got):
    length, width = df.shape
    hidden = hid.shape[1]
    half = shape((2, 6 * hidden // L, G, L))
    return pl.pallas_call(
        ffn_grads_body,
        in_specs=[SMEM] + [ANY] * 8,
        out_specs=[ANY] * 4,
        out_shape=[half] * 4,
        scratch_shapes=[
            pltpu.VMEM((ht.shape[0], G, length), bf16),
            pltpu.VMEM((length, width // 2), bf16),
        ]
        + [like(a) for a in (hid, dgate, dup, *got)]
        + [pltpu.VMEM((2,) + half.shape, bf16)] * 2
        + [pltpu.SemaphoreType.DMA((64,))],
        compiler_params=params(),
        cost_estimate=cost(17),
        name="ffn_grads",
    )(pos, ht, df, hid, dgate, dup, *got)


def ffn_out_body(r1_ref, hid_ref, wd, out_ref):
    out_ref[...] = (r1_ref[...] + nn(hid_ref[...], two(wd, 0))).astype(bf16)


def ffn_out(r1, hid, wd):
    length, width = r1.shape
    hidden = hid.shape[1]
    col = pl.BlockSpec((length, 2 * L), lambda i: (0, i))
    return pl.pallas_call(
        ffn_out_body,
        grid=(width // (2 * L),),
        in_specs=[col, once(length, hidden), pl.BlockSpec((2, hidden // G, G, L), lambda i: (i, 0, 0, 0))],
        out_specs=col,
        out_shape=shape((length, width)),
        compiler_params=params(),
        cost_estimate=cost(11),
        name="ffn_out",
    )(r1, hid, wd)


def square_body(keep, pos, ot_hbm, ht_hbm, *rest):
    grads_hbm, rest = rest[:4], rest[4:]
    if keep:
        got_hbm, ka_out, ta_out, kb_out, tb_out, ot, ht, da, dq, dk, dv, got, out_a, out_b, sem = rest
    else:
        out_hbm, ot, ht, da, dq, dk, dv, out, sem = rest
    core, b1, b2 = bits(pos)
    grads = (da, dq, dk, dv)
    mine = core if keep else 1 - core
    blocks = da.shape[1] // L
    loads = [pltpu.make_async_copy(a, b, sem.at[i]) for i, (a, b) in enumerate(zip(grads_hbm, grads))]
    lefts = [pltpu.make_async_copy(a.at[:, mine], b, sem.at[4 + i]) for i, (a, b) in enumerate(((ot_hbm, ot), (ht_hbm, ht)))]
    recv = []
    if keep:
        for i in range(4):
            some = pl.ds(i * blocks, blocks)
            recv.append(pltpu.make_async_copy(got_hbm.at[:, :, some], got.at[:, :, some], sem.at[6 + i]))
            recv[i].start()
    lefts[0].start()
    loads[0].start()
    lefts[1].start()
    for c in loads[1:]:
        c.start()
    sent = []

    def send(a, b):
        sent.append(pltpu.make_async_copy(a, b, sem.at[10 + len(sent)]))
        sent[-1].start()

    for i in range(4):
        if i < 2:
            lefts[i].wait()
        loads[i].wait()
        if keep:
            recv[i].wait()
        ref = (ot, ht, ht, ht)[i]
        left = ref[...].reshape(ref.shape[0] * G, ref.shape[2])
        for low, size in chunked(blocks, 4):
            g = nn(left, grads[i][:, low * L : (low + size) * L])
            for s in range(4):
                rows = g[s * 4 * G : (s + 1) * 4 * G].reshape(4, G, size * L)
                value = jnp.stack([rows[:, :, c * L : (c + 1) * L] for c in range(size)], 1)
                at = i * blocks + low
                if not keep:
                    out[s, :, at : at + size] = value.astype(bf16)
                    continue
                value = (value + got[s, :, at : at + size].astype(f32)).astype(bf16)
                at = s * 2 * blocks + (i % 2) * blocks + low
                sort_out(out_a if i < 2 else out_b, i < 2, value, at, b1 if i < 2 else b2)
        if not keep:
            some = pl.ds(i * blocks, blocks)
            send(out.at[:, :, some], out_hbm.at[:, :, some])
        elif i == 1:
            send(out_a.at[0], ka_out)
            send(out_a.at[1], ta_out)
        elif i == 3:
            send(out_b.at[0], kb_out)
            send(out_b.at[1], tb_out)
    for c in sent:
        c.wait()


def square_grads(pos, ot, ht, grads, got):
    length, width = grads[0].shape
    whole = shape((4, 4, 4 * width // L, G, L))
    half = shape((2, 8 * width // L, G, L))
    keep = got is not None
    left = pltpu.VMEM((ht.shape[0], G, length), bf16)
    return pl.pallas_call(
        lambda *refs: square_body(keep, *refs),
        in_specs=[SMEM] + [ANY] * (7 if keep else 6),
        out_specs=[ANY] * 4 if keep else ANY,
        out_shape=[half] * 4 if keep else whole,
        scratch_shapes=[left, left]
        + [like(a) for a in grads]
        + ([like(whole)] + [pltpu.VMEM((2,) + half.shape, bf16)] * 2 if keep else [like(whole)])
        + [pltpu.SemaphoreType.DMA((14,))],
        compiler_params=params(),
        cost_estimate=cost(10),
        name="square_keep" if keep else "square_send",
    )(pos, ot, ht, *grads, *([got] if keep else []))


def input_grad_body(x_ref, gain_ref, dq_hbm, dk_hbm, dv_hbm, wq_hbm, wk_hbm, wv_hbm, dr_hbm, out_hbm,
                    dq, dk, dv, wq, wk, wv, dr, acc, sem):
    length, width = x_ref.shape
    blocks = width // L
    pairs = ((dq_hbm, dq, wq_hbm, wq), (dk_hbm, dk, wk_hbm, wk), (dv_hbm, dv, wv_hbm, wv))
    loads = [
        (pltpu.make_async_copy(a, b, sem.at[2 * i]), pltpu.make_async_copy(c, d, sem.at[2 * i + 1]))
        for i, (a, b, c, d) in enumerate(pairs)
    ]
    get_dr = pltpu.make_async_copy(dr_hbm, dr, sem.at[6])
    for pair in loads:
        for c in pair:
            c.start()
    get_dr.start()
    for i, (_, grad, _, w) in enumerate(pairs):
        for c in loads[i]:
            c.wait()
        for n in range(width // QB):
            rows = slice(n * QB // G, (n + 1) * QB // G)
            part = nt(grad[...], jnp.concatenate([w[c, rows].reshape(QB, L) for c in range(blocks)], 1))
            if i == 0:
                acc[:, n * QB : (n + 1) * QB] = part
            else:
                acc[:, n * QB : (n + 1) * QB] += part
    get_dr.wait()
    out = []
    for i in range(length // QB):
        rows = slice(i * QB, (i + 1) * QB)
        x = x_ref[rows, :].astype(f32)
        rinv = lax.rsqrt(jnp.mean(x * x, -1, keepdims=True) + EPS)
        n1 = x * rinv
        dn = acc[rows, :] * gain_ref[...]
        acc[rows, :] = dr[rows, :] + rinv * (dn - n1 * jnp.mean(dn * n1, -1, keepdims=True))
        out.append(pltpu.make_async_copy(acc.at[pl.ds(i * QB, QB)], out_hbm.at[pl.ds(i * QB, QB)], sem.at[7 + i]))
        out[-1].start()
    for c in out:
        c.wait()


def input_grad(x, gain, dr1, dq, dk, dv, weights):
    length, width = x.shape
    vmem = pl.BlockSpec(memory_space=pltpu.VMEM)
    return pl.pallas_call(
        input_grad_body,
        in_specs=[vmem, vmem] + [ANY] * 7,
        out_specs=ANY,
        out_shape=shape((length, width), f32),
        scratch_shapes=[like(a) for a in (dq, dk, dv, *weights, dr1, dr1)]
        + [pltpu.SemaphoreType.DMA((7 + length // QB,))],
        compiler_params=params(),
        cost_estimate=cost(14),
        name="input_grad",
    )(x, gain, dq, dk, dv, *weights, dr1)


def place_body(tall, pos, *refs):
    pieces, outs = refs[:10], refs[10:]
    blocks = []
    for which, out in enumerate(outs[:-3] if tall else outs):
        blocks += [(which, c) for c in range(out.shape[1] // L)]
    if tall:
        blocks += [(len(outs) - 3, j) for j in range(outs[-3].shape[0] // G)] + [(None, 0)]
    d = pos[1]
    for array, mask, low, size in piece_sources(pieces[0].shape[1]):
        piece = d ^ mask
        rows = pl.ds(pl.multiple_of(piece * G, G), G)
        cols = pl.ds(pl.multiple_of(piece * L, L), L)
        for c in range(size):
            which, at = blocks[low + c]
            value = pieces[array][0, c].astype(f32)
            if which is None:
                outs[-1][piece] = value
            elif tall and which == len(outs) - 3:
                outs[which][at * G : (at + 1) * G, cols] = value
            else:
                outs[which][rows, at * L : (at + 1) * L] = value
    if tall:
        total = outs[-1][0]
        for piece in range(1, 8):
            total = total + outs[-1][piece]
        outs[-2][...] = total


def place(pos, arrays, widths, rows, tall=None):
    vmem = pl.BlockSpec(memory_space=pltpu.VMEM)
    outs = [shape((rows, w), f32) for w in widths]
    if tall is not None:
        outs += [shape(tall, f32), shape((G, L), f32)]
    return pl.pallas_call(
        lambda *refs: place_body(tall is not None, *refs),
        in_specs=[SMEM] + [vmem] * 10,
        out_specs=[vmem] * len(outs),
        out_shape=outs,
        scratch_shapes=[] if tall is None else [pltpu.VMEM((8, G, L), f32)],
        compiler_params=params(),
        cost_estimate=cost(5),
        name="place",
    )(pos, *arrays)


def layout(lengths, length):
    position = jnp.arange(length, dtype=jnp.int32)
    ends = jnp.cumsum(lengths).astype(jnp.int32)
    seg = jnp.sum((position[:, None] >= ends[None, :]).astype(jnp.int32), 1)
    onehot = seg[:, None] == jnp.arange(lengths.shape[0], dtype=jnp.int32)[None, :]
    first = jnp.sum(jnp.where(onehot, (ends - lengths)[None, :], 0), 1)
    rel = (position - first).astype(f32)
    inverse = 10000.0 ** (-jnp.arange(HEAD_DIM // 2, dtype=f32) * 2.0 / HEAD_DIM)
    angle = rel[:, None] * inverse[None, :]
    keep = (seg < lengths.shape[0] - 1).astype(f32)
    cos, sin = jnp.cos(angle), jnp.sin(angle)
    cos_w = jnp.concatenate([cos] * 4, 1)
    sin_w = jnp.concatenate([-sin, sin] * 2, 1)
    return cos_w, sin_w, marks(seg, lengths.shape[0]), keep[:, None]


def add(*terms):
    total = terms[0].astype(f32)
    for t in terms[1:]:
        total = total + t.astype(f32)
    return total


def halve(kept, got, bit):
    picked = []
    for at in (1 - bit, bit):
        parts = [lax.dynamic_index_in_dim(x, at, 0, keepdims=False) for x in (kept, got)]
        picked.append(add(*parts).astype(bf16))
    return picked


def in_parts(sums):
    parts = []
    for _ in range(3):
        part = lax.reduce_precision(sums, 8, 7)
        parts.append(part)
        sums = sums - part
    return jnp.pad(jnp.stack(parts).astype(bf16), ((0, G - 3), (0, L - 2)))


def from_parts(block):
    parts = block[..., :3, :2].astype(f32)
    return parts[..., 0, :] + parts[..., 1, :] + parts[..., 2, :]


def to_shards(total, z, extra=None):
    terms = [lax.dynamic_index_in_dim(total, z, 0, keepdims=False)]
    if extra is not None:
        terms[0] = jnp.concatenate([terms[0], extra[None]])
    for s in (1, 2, 3):
        away = lax.dynamic_index_in_dim(total, lax.rem(z + s, 4), 0, keepdims=False)
        if extra is not None:
            away = jnp.concatenate([away, extra[None]])
        terms.append(fsdp_shift(away, s))
    return terms


def sums_over_fsdp(terms, z):
    numbers = jnp.stack([from_parts(t[-1]) for t in terms])
    sums = jnp.zeros_like(numbers[0])
    for shard in range(4):
        sums = sums + lax.dynamic_index_in_dim(numbers, lax.rem(z + 4 - shard, 4), 0, keepdims=False)
    return sums


def back_over_dp(reduced):
    g = Gather.__new__(Gather)
    g.count, g.start = reduced.shape[0], reduced[None]
    g.x, g.y = dp_swap(g.start, 2), dp_swap(g.start, 4)
    return g


def unfold_rows(w):
    return w.transpose(0, 2, 1, 3).reshape(w.shape[0] * G, w.shape[1] * L)


def sum_whole(grad):
    part = lax.psum_scatter(grad.astype(bf16), "fsdp", scatter_dimension=0, tiled=True)
    return lax.psum(part, "dp").astype(f32)


def local(
    layer_in, first_values, first_values_grad, cotangent, doc_lengths, norm1_gain,
    w_query, w_key, w_value, w_out, norm2_gain, w_gate, w_up, w_down,
):
    rows, length, width = layer_in.shape
    hidden = w_gate.shape[1]
    dp, fsdp = lax.axis_size("dp"), lax.axis_size("fsdp")
    fast = fast_mesh(dp, fsdp, w_query.shape[0])
    z, d = lax.axis_index("fsdp"), lax.axis_index("dp")
    b1, b2 = lax.rem(d // 2, 2), lax.rem(d // 4, 2)
    x, v1 = layer_in[0], first_values[0]
    df = cotangent[0]
    gains = jnp.stack([norm1_gain, norm2_gain])
    c, h = width // L, hidden // L
    members = (
        ((w_query, w_key, w_value), ((c, True),) * 3),
        ((w_out, w_gate), ((c, True), (h, True))),
        ((w_up, w_down), ((h, True), (w_down.shape[0] // G, False))),
    )
    if fast:
        pos = jnp.stack([z, d]).astype(jnp.int32)
        extra = jnp.pad(gains.reshape(-1, L), ((0, G - gains.size // L), (0, 0)))
        g1 = Gather(cut(pos, *members[0], extra), True)
        far = jnp.stack([e[: gains.size // L].reshape(gains.shape) for e in g1.extras])
        mines = [cut(after(pos, g1.extras[0]), *m) for m in members[1:]]
        g1.near()
        g2 = Gather(after(mines[0], g1.start))
        g1.corner(g2.far[0], g2.far[2])
        g2.near(g1.c1, g1.c2)
        g3 = Gather(after(mines[1], g2.start))
        g1.core()
        g1.core_corner()
        groups = [Group(members[0][1], members[0][0], g1.arrays(), False)]
        whole_gains = jnp.concatenate(
            [lax.dynamic_index_in_dim(far, lax.rem(z + 4 - j, 4), 0, keepdims=False) for j in range(4)], 1
        )
    else:
        pos = jnp.zeros((2,), jnp.int32)

        def blocks(w, by_rows):
            full = lax.all_gather(w, "fsdp", axis=0, tiled=True)
            return row_pieces(full, full.shape[0] // G).transpose(1, 0, 2, 3) if by_rows else column_pieces(full, c)

        whole_gains = lax.all_gather(gains, "fsdp", axis=1, tiled=True)
        groups = [
            Group(tensors, [], [blocks(w, t[1]) for w, t in zip(weights, tensors)], True)
            for weights, tensors in members
        ]
    whole_gains = whole_gains.astype(f32)
    gain_1, gain_2 = whole_gains[:1], whole_gains[1:]
    cos_w, sin_w, mark, keep_col = layout(doc_lengths[0], length)

    q, k, vm, h1t, sums, wq, wk, wv = qkv(pos, x, v1, gain_1, cos_w, sin_w, groups[0])
    squares = jnp.sum(sums, (1, 2))
    entries = rows * length * width * dp * fsdp
    if fast:
        g2.corner(q)
        q = after(q, g2.x, g2.y)
    o, lse_1 = attend_fwd(q, k, vm, *mark, keep_col, 0, 3)
    if fast:
        g3.near(o)
        g2.core(o)
        o = after(o, g2.c1, g2.c2, g3.start)
    o, lse_2 = attend_fwd(q, k, vm, *mark, keep_col, 3, 5, o)
    if fast:
        g3.corner(o)
        g2.core_corner(o)
        g3.core(o)
        g3.core_corner()
        groups += [Group(members[i][1], members[i][0], g.arrays(), False) for i, g in ((1, g2), (2, g3))]
    hid, dgate, dup, sg, su, sd, r1, h2t, ot, wo, wg, wu, wd = ffn(pos, x, o, df, gain_2, groups[1:], hidden)
    got = [dp_swap(g, 1) if fast else jnp.zeros_like(g) for g in (sg, su, sd)]
    out = ffn_out(r1, hid, wd)
    ka, ta, kb, tb = ffn_grads(pos, h2t, df, hid, dgate, dup, after(got, out))
    if fast:
        na, nb = dp_swap(ta, 2), dp_swap(tb, 4)
        dgate = after(dgate, ta)
    dr1, da, do = ffn_back(r1, df, keep_col, gain_2, dgate, dup, wo, wg, wu)
    back = (*mark, cos_w, -sin_w, first_values_grad[0])
    results = attend_bwd(q, k, vm, do, lse_2.T, *back, 3, 5)
    if fast:
        na, nb = after((na, nb), results)
        ta, ka = halve(ka, na, b2)
        tb, kb = halve(kb, nb, b1)
        ma, mb = dp_swap(ta, 4), dp_swap(tb, 2)
        results = after(results, ta, tb)
    dq, dk, dv, first_out = attend_bwd(q, k, vm, do, lse_1.T, *back, 0, 3, results)
    grads = (da, dq, dk, dv)
    if fast:
        grads = after(grads, ma, mb)
    send = square_grads(pos, ot, h1t, grads, None)
    swapped = dp_swap(send, 1) if fast else jnp.zeros_like(send)
    if fast:
        ma, mb = after((ma, mb), send)
        total_a, total_b = add(ka, ma).astype(bf16), add(kb, mb).astype(bf16)
        n = 4 * hidden // L
        cols_a, cols_b = [t[:n].reshape(4, n // 4, G, L) for t in (total_a, total_b)]
        cols_d = jnp.concatenate([total_a[n:], total_b[n:]]).reshape(4, n // 4, G, L)
        wide_terms = to_shards(jnp.concatenate([cols_a, cols_b, cols_d], 1), z, in_parts(squares))
        swapped = after(swapped, wide_terms[0])
    ks, ts, kt, tt = square_grads(pos, ot, h1t, grads, swapped)
    if fast:
        ns, n_t = dp_swap(ts, 2), dp_swap(tt, 4)
    d_x = input_grad(after(x, ts), gain_1, dr1, dq, dk, dv, (wq, wk, wv))
    if fast:
        ns, n_t = after((ns, n_t), d_x)
        ts, ks = halve(ks, ns, b2)
        tt, kt = halve(kt, n_t, b1)
        ms, mt = dp_swap(ts, 4), dp_swap(tt, 2)
        ms, mt, wide_terms = after((ms, mt, wide_terms), ts)
        total_s, total_t = add(ks, ms).astype(bf16), add(kt, mt).astype(bf16)
        both = [t.reshape((4, -1) + t.shape[1:]) for t in (total_s, total_t)]
        last_terms = to_shards(jnp.concatenate(both, 1), z)
        wide_terms = after(wide_terms, *both)
        reduced = add(*[t[:-1] for t in wide_terms]).astype(bf16)
        wide = back_over_dp(jnp.concatenate([reduced, in_parts(sums_over_fsdp(wide_terms, z))[None]]))
        wide.corner()
        last = back_over_dp(after(add(*last_terms).astype(bf16), wide.c1, wide.c2))
        wide.core()
        wide.core_corner()
        last.corner(*wide.other)
        grad_wg, grad_wu, grad_wd, squares = place(
            pos, wide.arrays(), [hidden] * 2, w_query.shape[0], (w_down.shape[0], width)
        )
        squares = from_parts(squares)
        last.core()
        last.core_corner()
        grad_wo, grad_wq, grad_wk, grad_wv = place(pos, last.arrays(), [width] * 4, w_query.shape[0])
    else:
        squares = lax.psum(squares, ("dp", "fsdp"))
        n = 4 * hidden // L
        even_a, even_b = jnp.stack([ka, ta], 1), jnp.stack([kb, tb], 0)
        even_a, even_b = [e.reshape((4,) + ka.shape[1:]) for e in (even_a, even_b)]
        grad_wg, grad_wu = join(even_a[:, :n], sg), join(even_b[:, :n], su)
        even_d = jnp.concatenate([even_a[:, n:], even_b[:, n:]], 1).transpose(1, 0, 2, 3)
        grad_wd = jnp.stack([even_d, sd], 2).reshape(n, 8, G, L).transpose(0, 2, 1, 3).reshape(hidden, width)
        n = 2 * width // L
        even_s, even_t = jnp.stack([ks, ts], 1), jnp.stack([kt, tt], 0)
        firsts = join(even_s.reshape((4,) + ks.shape[1:]), send[:, :, :n])
        seconds = join(even_t.reshape((4,) + ks.shape[1:]), send[:, :, n:])
        grad_wo, grad_wq = firsts[:, :width], firsts[:, width:]
        grad_wk, grad_wv = seconds[:, :width], seconds[:, width:]
        grad_wo, grad_wq, grad_wk, grad_wv, grad_wg, grad_wu, grad_wd = [
            sum_whole(g) for g in (grad_wo, grad_wq, grad_wk, grad_wv, grad_wg, grad_wu, grad_wd)
        ]
    def along(*pairs):
        return sum(jnp.sum(w.astype(f32) * g, 1) for w, g in pairs)

    grad_g1 = along((w_query, grad_wq), (w_key, grad_wk), (w_value, grad_wv)) / norm1_gain.astype(f32)
    grad_g2 = along((w_gate, grad_wg), (w_up, grad_wu)) / norm2_gain.astype(f32)
    return (
        out[None], d_x[None], first_out[None], grad_g1, grad_wq, grad_wk, grad_wv, grad_wo, grad_g2,
        grad_wg, grad_wu, grad_wd, squares / entries,
    )


def join(even, odd):
    even = even.reshape((4, 4, -1) + even.shape[2:]).transpose(1, 0, 2, 3, 4)
    both = jnp.stack([even, odd], 2)
    return unfold_rows(both.reshape((32,) + odd.shape[2:]))


def solution(mesh):
    by_row = P(("dp", "fsdp"), None, None)
    shard = P("fsdp", None)
    return jax.shard_map(
        local,
        mesh=mesh,
        in_specs=(by_row,) * 4
        + (P(("dp", "fsdp"), None), P("fsdp"), shard, shard, shard, shard, P("fsdp"), shard, shard, shard),
        out_specs=(by_row,) * 3
        + (P("fsdp"), shard, shard, shard, shard, P("fsdp"), shard, shard, shard, P()),
        check_vma=False,
    )
```

```python
import jax
import jax.numpy as jnp
from jax import lax
from jax.experimental import pallas as pl
from jax.experimental.pallas import tpu as pltpu
from jax.sharding import PartitionSpec as P

HEADS = 16
HEAD_DIM = 64
EPS = 1e-06
NEG = -1e30
COST = 4e9
QB = 256
G = 32
L = 128
bf16 = jnp.bfloat16
f32 = jnp.float32
ANY = pl.BlockSpec(memory_space=pl.ANY)
SMEM = pl.BlockSpec(memory_space=pltpu.SMEM)


def params(mib=58):
    return pltpu.CompilerParams(vmem_limit_bytes=mib * 2**20)


def cost(us):
    return pl.CostEstimate(flops=int(us * COST), bytes_accessed=0, transcendentals=0)


def shape(dims, dtype=bf16):
    return jax.ShapeDtypeStruct(dims, dtype)


def nt(a, b):
    return lax.dot_general(a, b, (((1,), (1,)), ((), ())), preferred_element_type=f32)


def nn(a, b):
    return lax.dot_general(a, b, (((1,), (0,)), ((), ())), preferred_element_type=f32)


def tn(a, b):
    return lax.dot_general(a, b, (((0,), (0,)), ((), ())), preferred_element_type=f32)


def fast_mesh(dp, fsdp, shard_rows):
    return dp == 8 and fsdp == 4 and shard_rows == 8 * G


def row_pieces(w, count):
    return w.reshape(count, G, w.shape[1] // L, L).transpose(0, 2, 1, 3)


def column_pieces(w, count):
    return w.reshape(w.shape[0] // G, G, count, L).transpose(2, 0, 1, 3)


def dp_swap(x, bit):
    return lax.ppermute(x, "dp", [(i, i ^ bit) for i in range(lax.axis_size("dp"))])


def after(x, *first):
    return lax.optimization_barrier((x, first))[0]


def fsdp_shift(x, step):
    size = lax.axis_size("fsdp")
    return lax.ppermute(x, "fsdp", [(i, (i + step) % size) for i in range(size)])


class Gather:
    def __init__(self, sent, extra=False):
        self.count = sent.shape[0] - extra
        self.far = [fsdp_shift(sent, s) for s in (1, 2, 3)]
        self.extras = [x[self.count] for x in [sent] + self.far] if extra else None

    def near(self, *gate):
        self.start = jnp.stack([x[: self.count] for x in after(self.far, *gate)])
        self.x, self.y = dp_swap(self.start, 2), dp_swap(self.start, 4)

    def corner(self, *gate):
        cut = self.count // 2
        self.c1 = dp_swap(after(self.x[:, :cut], *gate), 4)
        self.c2 = dp_swap(after(self.y[:, cut:], *gate), 2)

    def core(self, *gate):
        self.other = [dp_swap(after(a, *gate), 1) for a in (self.start, self.x, self.y)]

    def core_corner(self, *gate):
        self.other += [dp_swap(after(a, *gate), 1) for a in (self.c1, self.c2)]

    def arrays(self):
        return [self.start, self.x, self.y, self.c1, self.c2] + self.other


def piece_sources(count):
    cut = count // 2
    found = []
    for core in range(2):
        for i, (mask, low, size) in enumerate(
            ((0, 0, count), (2, 0, count), (4, 0, count), (6, 0, cut), (6, cut, count - cut))
        ):
            found.append((5 * core + i, mask | core, low, size))
    return found


class Group:
    def __init__(self, tensors, owned, arrays, whole):
        self.tensors, self.whole, self.owned = tensors, whole, len(owned)
        self.arrays = list(owned) + list(arrays)

    def specs(self):
        return [ANY] * len(self.arrays)

    def fetch(self, index, refs, pos, scratch, sem):
        if self.whole:
            pltpu.make_async_copy(refs[index], scratch, sem).start()
            return
        z, d = pos[0], pos[1]
        at = sum(t[0] for t in self.tensors[:index])
        blocks, by_rows = self.tensors[index]

        def target(shard, piece, low, size):
            if by_rows:
                return scratch.at[pl.ds(low, size), shard * 8 + piece]
            return scratch.at[piece, pl.ds(shard * blocks + low, size)]

        own = refs[index]
        rows = own.shape[0]
        flat = scratch.reshape(scratch.shape[0], scratch.shape[1] * G, L)
        for c in range(scratch.shape[0]):
            pltpu.make_async_copy(
                own.at[:, pl.ds(c * L, L)], flat.at[c, pl.ds(pl.multiple_of(z * rows, G), rows)], sem
            ).start()
        for array, mask, low, size in piece_sources(sum(t[0] for t in self.tensors)):
            begin, end = max(at, low), min(at + blocks, low + size)
            if end <= begin:
                continue
            for s in range(3):
                pltpu.make_async_copy(
                    refs[self.owned + array].at[s, pl.ds(begin - low, end - begin)],
                    target(lax.rem(z + 3 - s, 4), d ^ mask, begin - at, end - begin),
                    sem,
                ).start()


def cut_body(tensors, gains, pos, *refs):
    count = len(tensors)
    weights, refs = refs[:count], refs[count:]
    if gains:
        gain_ref, refs = refs[0], refs[1:]
    out, stages, sem = refs[0], refs[1:-1], refs[-1]
    d = pos[1]
    copies = []
    for i, (blocks, by_rows) in enumerate(tensors):
        rows = pl.ds(pl.multiple_of(d * G, G), G)
        cols = pl.ds(pl.multiple_of(d * L, L), L)
        part = weights[i].at[rows] if by_rows else weights[i].at[:, cols]
        copies.append(pltpu.make_async_copy(part, stages[i], sem.at[i]))
    for c in copies:
        c.start()
    at = 0
    for i, (blocks, by_rows) in enumerate(tensors):
        copies[i].wait()
        if by_rows:
            for c in range(blocks):
                out[at + c] = stages[i][:, c * L : (c + 1) * L]
        else:
            out[at : at + blocks] = stages[i][...].reshape(blocks, G, L)
        at += blocks
    if gains:
        out[at] = gain_ref[...]


def cut(pos, weights, tensors, gains=None):
    vmem = pl.BlockSpec(memory_space=pltpu.VMEM)
    total = sum(t[0] for t in tensors) + (gains is not None)
    stages = [
        pltpu.VMEM((G, w.shape[1]) if by_rows else (w.shape[0], L), bf16) for w, (_, by_rows) in zip(weights, tensors)
    ]
    return pl.pallas_call(
        lambda *refs: cut_body(tensors, gains is not None, *refs),
        in_specs=[SMEM] + [ANY] * len(weights) + ([] if gains is None else [vmem]),
        out_specs=vmem,
        out_shape=shape((total, G, L)),
        scratch_shapes=stages + [pltpu.SemaphoreType.DMA((len(weights),))],
        compiler_params=params(),
        name="cut",
    )(pos, *weights, *([] if gains is None else [gains]))


def wait_all(scratch, sem):
    pltpu.make_async_copy(scratch, scratch, sem).wait()


def two(w, i):
    rows = w.shape[1] * w.shape[2]
    return jnp.concatenate([w[2 * i].reshape(rows, L), w[2 * i + 1].reshape(rows, L)], 1)


def swap_halves(t):
    lane = lax.broadcasted_iota(jnp.int32, t.shape, 1) % 64
    return jnp.where(lane < 32, pltpu.roll(t, 96, 1), pltpu.roll(t, 32, 1))


def chunked(blocks, size):
    return [(low, min(size, blocks - low)) for low in range(0, blocks, size)]


def beside(w, low, size):
    rows = w.shape[1] * G
    return jnp.concatenate([w[low + c].reshape(rows, L) for c in range(size)], 1)


def like(a):
    return pltpu.VMEM(a.shape, a.dtype)


def qkv_body(group, pos, gain_ref, cos_ref, sin_ref, x_ref, v1_hbm, *rest):
    count = len(group.arrays)
    w_refs = rest[:count]
    (q_out, k_out, v_out, ht_out, sums_ref, wq_out, wk_out, wv_out,
     v1, wq, wk, wv, h, ht, q, k, v, sem) = rest[count:]
    length, width = x_ref.shape
    blocks = width // L
    for i, w in enumerate((wq, wk, wv)):
        group.fetch(i, w_refs, pos, w, sem.at[i])
    get_v1 = pltpu.make_async_copy(v1_hbm, v1, sem.at[3])
    get_v1.start()
    for i in range(length // QB):
        rows = slice(i * QB, (i + 1) * QB)
        x = x_ref[rows, :].astype(f32)
        n = x * lax.rsqrt(jnp.mean(x * x, -1, keepdims=True) + EPS) * gain_ref[...]
        h[rows, :] = n.astype(bf16)
        ht[:, :, :, rows] = n.T.astype(bf16).reshape(ht.shape[:3] + (QB,))
    out = [pltpu.make_async_copy(ht, ht_out, sem.at[4])]
    out[0].start()
    cos, sin = cos_ref[...], sin_ref[...]
    at = 5

    def send(a, b):
        out.append(pltpu.make_async_copy(a, b, sem.at[at + len(out) - 1]))
        out[-1].start()

    sums_ref[...] = jnp.zeros_like(sums_ref)
    for i, (w, w_out, t, t_out) in enumerate(((wq, wq_out, q, q_out), (wk, wk_out, k, k_out), (wv, wv_out, v, v_out))):
        wait_all(w, sem.at[i])
        send(w, w_out)
        if i == 2:
            get_v1.wait()
        for low, size in chunked(blocks, 2):
            cols = slice(low * L, (low + size) * L)
            got = nn(h[...], beside(w, low, size))
            if i == 2:
                first = v1[:, cols].astype(f32)
                mixed = (0.5 * got + 0.5 * first).astype(bf16)
                v[:, cols] = mixed
                mixed = mixed.astype(f32)
                sums_ref[0] += jnp.sum((first * first).reshape(length // 8, 8, size * L), 0)
                sums_ref[1] += jnp.sum((mixed * mixed).reshape(length // 8, 8, size * L), 0)
                continue
            for c in range(size):
                part = got[:, c * L : (c + 1) * L]
                part = (part * cos + swap_halves(part) * sin).astype(bf16)
                if i == 0:
                    part = (part.astype(f32) * 0.125).astype(bf16)
                t[:, (low + c) * L : (low + c + 1) * L] = part
        send(t, t_out)
    for c in out:
        c.wait()


def qkv(pos, x, v1, gain, cos_w, sin_w, group):
    length, width = x.shape
    blocks = width // L
    vmem = pl.BlockSpec(memory_space=pltpu.VMEM)
    weight = shape((blocks, width // G, G, L))
    ht = shape((width // G // 2, 2, G, length))
    return pl.pallas_call(
        lambda *refs: qkv_body(group, *refs),
        in_specs=[SMEM, vmem, vmem, vmem, vmem, ANY] + group.specs(),
        out_specs=[ANY] * 4 + [vmem] + [ANY] * 3,
        out_shape=[shape((length, width))] * 3 + [ht, shape((2, 8, 2 * L), f32)] + [weight] * 3,
        scratch_shapes=[like(a) for a in (v1, weight, weight, weight, x, ht, x, x, x)]
        + [pltpu.SemaphoreType.DMA((12,))],
        compiler_params=params(),
        cost_estimate=cost(15),
        name="qkv",
    )(pos, gain, cos_w, sin_w, x, v1, *group.arrays)


def half_mask(rows, which):
    lane = lax.broadcasted_iota(jnp.int32, (rows, 128), 1)
    return (lane < 64) if which == 0 else (lane >= 64)


def pick(x, which, other=None):
    return jnp.where(half_mask(x.shape[0], which), x, jnp.zeros_like(x) if other is None else other)


def marks(seg, docs):
    lane = jnp.arange(128, dtype=jnp.int32)[None, :] % 64
    same = lane == seg[:, None]
    return jnp.where((lane < docs) & ~same, NEG, 0.0).astype(bf16), same.astype(bf16)


def key_blocks(length):
    return length // 2 // QB + 1


def attend_fwd_body(q_ref, k_ref, v_ref, qm_ref, km_ref, keep_ref, *rest):
    o_ref, lse_ref = rest[-2:]
    pair = pl.program_id(0)
    length = q_ref.shape[0]
    blocks = length // QB
    most = key_blocks(length)
    row, col = [lax.broadcasted_iota(jnp.int32, (QB, QB), a) for a in (0, 1)]
    causal = jnp.where(row >= col, 0.0, NEG)
    keys = [pick(k_ref[...], h, km_ref[...]) for h in range(2)]
    lane = lax.broadcasted_iota(jnp.int32, (QB, 128), 1)

    work = [(i, h) for i in range(blocks) for h in range(2)]

    def span(i):
        return slice(max(0, i + 1 - most) * QB, (i + 1) * QB)

    def scores(i, h):
        rows = slice(i * QB, (i + 1) * QB)
        return nt(pick(q_ref[rows, :], h, qm_ref[rows, :]), keys[h][span(i), :])

    ahead = scores(*work[0])
    outs, stats = {}, {}
    for at, (i, h) in enumerate(work):
        rows = slice(i * QB, (i + 1) * QB)
        s = ahead + causal if i == 0 else jnp.concatenate([ahead[:, :-QB], ahead[:, -QB:] + causal], 1)
        if at + 1 < len(work):
            ahead = scores(*work[at + 1])
        top = jnp.max(s, -1, keepdims=True)
        expo = jnp.exp(s - top)
        total = jnp.sum(expo, -1, keepdims=True)
        outs[h] = nn(expo.astype(bf16), v_ref[span(i), :]) / total
        stats[h] = top + jnp.log(total)
        if h == 1:
            old = jnp.where(lane == 2 * pair, stats[0], lse_ref[rows, :])
            lse_ref[rows, :] = jnp.where(lane == 2 * pair + 1, stats[1], old)
            o = jnp.where(lane < 64, outs[0], outs[1]) * keep_ref[rows, :]
            o_ref[rows, :] = o.astype(bf16)


def attend_fwd(q, k, v, q_mark, k_mark, keep_col, first, pairs, before=None):
    length, width = q.shape
    col = pl.BlockSpec((length, 128), lambda p: (0, p + first))
    return pl.pallas_call(
        attend_fwd_body,
        grid=(pairs,),
        in_specs=[
            col,
            col,
            col,
            pl.BlockSpec((length, 128), lambda p: (0, 0)),
            pl.BlockSpec((length, 128), lambda p: (0, 0)),
            pl.BlockSpec((length, 1), lambda p: (0, 0)),
        ]
        + ([] if before is None else [ANY]),
        out_specs=[col, pl.BlockSpec((length, 128), lambda p: (0, 0))],
        out_shape=[
            jax.ShapeDtypeStruct((length, width), bf16),
            jax.ShapeDtypeStruct((length, 128), f32),
        ],
        compiler_params=params(),
        cost_estimate=cost(4.2 * pairs),
        input_output_aliases={} if before is None else {6: 0},
        name="attend_fwd",
    )(q, k, v, q_mark, k_mark, keep_col, *([] if before is None else [before]))


def attend_bwd_body(
    q_ref, k_ref, v_ref, do_ref, lse_ref, qm_ref, km_ref, cos_ref, sin_ref, fg_ref, *rest,
):
    dq_ref, dk_ref, dv_ref, fo_ref, dk_acc, dv_acc = rest[-6:]
    pair = pl.program_id(0)
    length = q_ref.shape[0]
    blocks = length // QB
    most = key_blocks(length)
    row, col = [lax.broadcasted_iota(jnp.int32, (QB, QB), a) for a in (0, 1)]
    causal = jnp.where(row <= col, 0.0, NEG)
    marked = [pick(k_ref[...], h, km_ref[...]) for h in range(2)]
    k_t = k_ref[...].astype(f32).T.astype(bf16)
    dk_acc[...] = jnp.zeros_like(dk_acc)
    dv_acc[...] = jnp.zeros_like(dv_acc)

    work = [(i, h) for i in reversed(range(blocks)) for h in range(2)]

    def products(i, h):
        rows = slice(i * QB, (i + 1) * QB)
        keys = slice(max(0, i + 1 - most) * QB, (i + 1) * QB)
        qh = pick(q_ref[rows, :], h)
        dh = pick(do_ref[rows, :], h)
        qm = pick(q_ref[rows, :], h, qm_ref[rows, :])
        return qh, dh, nt(marked[h][keys, :], qm), nt(v_ref[keys, :], dh)

    ahead = products(*work[0])
    part_q = []
    for at, (i, h) in enumerate(work):
        rows = slice(i * QB, (i + 1) * QB)
        keys = slice(max(0, i + 1 - most) * QB, (i + 1) * QB)
        qh, dh, s, dp = ahead
        if at + 1 < len(work):
            ahead = products(*work[at + 1])
        lse = lse_ref[pl.ds(2 * pair + h, 1), rows]
        s = s + causal if i == 0 else jnp.concatenate([s[:-QB], s[-QB:] + causal], 0)
        p = jnp.exp(s - lse)
        delta = jnp.sum(p * dp, 0, keepdims=True)
        ds = (p * (dp - delta)).astype(bf16)
        dv_acc[keys, :] += nn(p.astype(bf16), dh)
        dk_acc[keys, :] += nn(ds, qh)
        part_q.append(nn(k_t[h * 64 : (h + 1) * 64, keys], ds))
        if h == 1:
            dq = jnp.concatenate(part_q, 0).T * 0.125
            part_q = []
            dq = dq * cos_ref[rows, :] + swap_halves(dq) * sin_ref[rows, :]
            dq_ref[rows, :] = dq.astype(bf16)
    dk = dk_acc[...]
    dk_ref[...] = (dk * cos_ref[...] + swap_halves(dk) * sin_ref[...]).astype(bf16)
    dv = dv_acc[...].astype(bf16).astype(f32) * 0.5
    dv_ref[...] = dv.astype(bf16)
    fo_ref[...] = fg_ref[...] + dv


def attend_bwd(q, k, v, do, lse_t, q_mark, k_mark, cos_w, sin_back, fgrad, first, pairs, before=None):
    length, width = q.shape
    col = pl.BlockSpec((length, 128), lambda p: (0, p + first))
    before = [] if before is None else list(before)

    def whole(a):
        return pl.BlockSpec(a.shape, lambda p: (0, 0))

    wide = jax.ShapeDtypeStruct((length, width), bf16)
    return pl.pallas_call(
        attend_bwd_body,
        grid=(pairs,),
        in_specs=[col] * 4 + [whole(lse_t), whole(q_mark), whole(k_mark), whole(cos_w), whole(sin_back), col]
        + [ANY] * len(before),
        out_specs=[col] * 4,
        out_shape=[wide, wide, wide, jax.ShapeDtypeStruct((length, width), f32)],
        scratch_shapes=[
            pltpu.VMEM((length, 128), f32),
            pltpu.VMEM((length, 128), f32),
        ],
        compiler_params=params(),
        cost_estimate=cost(5.5 * pairs),
        input_output_aliases={10 + i: i for i in range(len(before))},
        name="attend_bwd",
    )(q, k, v, do, lse_t, q_mark, k_mark, cos_w, sin_back, fgrad, *before)


def chosen_columns(ref, parity):
    blocks = ref.shape[1] // L
    return jnp.concatenate(
        [ref[:, pl.ds(pl.multiple_of((2 * p + parity) * L, L), L)] for p in range(blocks // 2)], 1
    )


def chosen_rows(ref, parity):
    return ref[:, parity].reshape(ref.shape[0] * G, ref.shape[3])


def wd_rows(wd, t):
    return jnp.concatenate([wd[c, pl.ds(8 * t, 8)].reshape(8 * G, L) for c in range(wd.shape[0])], 1)


def pair_at(w, t):
    rows = w.shape[1] * G
    return jnp.concatenate([w[2 * t].reshape(rows, L), w[2 * t + 1].reshape(rows, L)], 1)


def once(*dims):
    return pl.BlockSpec(dims, lambda i: (0,) * len(dims), pipeline_mode=pl.Buffered(1))


def ffn_body(groups, pos, x_ref, o_ref, gain_ref, df_hbm, *rest):
    count = [len(g.arrays) for g in groups]
    refs, rest = rest[: sum(count)], rest[sum(count) :]
    of = [refs[: count[0]], refs[count[0] :]]
    (hid_ref, dg_ref, du_ref, sg_ref, su_ref, sd_ref, r1_out, ht_out, ot_out,
     wo_out, wg_out, wu_out, wd_out,
     wo, wg, wu, wd, r1, h2, ht, ot, df, dfs, hts, sem) = rest
    step = pl.program_id(0)
    length = x_ref.shape[0]
    outs = ((r1, r1_out), (ht, ht_out), (ot, ot_out), (wo, wo_out), (wg, wg_out), (wu, wu_out), (wd, wd_out))

    @pl.when(step == 0)
    def _():
        groups[0].fetch(0, of[0], pos, wo, sem.at[0])
        groups[0].fetch(1, of[0], pos, wg, sem.at[1])
        groups[1].fetch(0, of[1], pos, wu, sem.at[2])
        pltpu.make_async_copy(df_hbm, df, sem.at[4]).start()
        groups[1].fetch(1, of[1], pos, wd, sem.at[3])
        other = 1 - lax.rem(pos[1], 2)
        wait_all(wo, sem.at[0])
        w = jnp.concatenate([two(wo, c) for c in range(wo.shape[0] // 2)], 1)
        for i in range(length // QB):
            rows = slice(i * QB, (i + 1) * QB)
            r = x_ref[rows, :].astype(f32) + nn(o_ref[rows, :], w)
            r1[rows, :] = r
            h = r * lax.rsqrt(jnp.mean(r * r, -1, keepdims=True) + EPS) * gain_ref[...]
            h2[rows, :] = h.astype(bf16)
            ht[:, :, :, rows] = h.T.astype(bf16).reshape(ht.shape[:3] + (QB,))
            ot[:, :, :, rows] = o_ref[rows, :].astype(f32).T.astype(bf16).reshape(ht.shape[:3] + (QB,))
        hts[...] = chosen_rows(ht, other)
        wait_all(df, sem.at[4])
        dfs[...] = chosen_columns(df, other)
        wait_all(wg, sem.at[1])
        wait_all(wu, sem.at[2])
        wait_all(wd, sem.at[3])
        for i, (a, b) in enumerate(outs):
            pltpu.make_async_copy(a, b, sem.at[5 + i]).start()

    @pl.when(step > 0)
    def _():
        t = step - 1
        wgt, wut, wdt = pair_at(wg, t), pair_at(wu, t), wd_rows(wd, t)
        for i in range(length // QB):
            rows = slice(i * QB, (i + 1) * QB)
            gate = nn(h2[rows, :], wgt)
            up = nn(h2[rows, :], wut)
            dhid = nt(df[rows, :], wdt)
            sigma = 0.5 + 0.5 * jnp.tanh(0.5 * gate)
            silu = gate * sigma
            hid_ref[rows, :] = (silu * up).astype(bf16)
            dg_ref[rows, :] = (dhid * up * (sigma + silu * (1.0 - sigma))).astype(bf16)
            du_ref[rows, :] = (dhid * silu).astype(bf16)
        gd = tn(hid_ref[...], dfs[...]).astype(bf16)
        for p in range(4):
            sd_ref[:, p] = gd[:, p * L : (p + 1) * L].reshape(8, G, L)
        for ref, grad in ((sg_ref, dg_ref), (su_ref, du_ref)):
            g = nn(hts[...], grad[...]).astype(bf16)
            for c in range(2):
                ref[:, :, c] = g[:, c * L : (c + 1) * L].reshape(4, 4, G, L)

    @pl.when(step == pl.num_programs(0) - 1)
    def _():
        for i, (a, b) in enumerate(outs):
            pltpu.make_async_copy(a, b, sem.at[5 + i]).wait()


def ffn(pos, x, o, df, gain, groups, hidden):
    length, width = x.shape
    tiles = hidden // (2 * L)

    def late(i):
        return jnp.maximum(i - 1, 0)

    col = pl.BlockSpec((length, 2 * L), lambda i: (0, late(i)))
    grad_cols = pl.BlockSpec((4, 4, 2, G, L), lambda i: (0, 0, late(i), 0, 0))
    grad_rows = pl.BlockSpec((8, 4, G, L), lambda i: (late(i), 0, 0, 0))
    ht_dims = (width // G // 2, 2, G, length)
    square, wide = (width // L, width // G, G, L), (hidden // L, width // G, G, L)
    tall = (width // L, hidden // G, G, L)
    kept = [((length, width), f32), (ht_dims, bf16), (ht_dims, bf16)]
    kept += [(square, bf16), (wide, bf16), (wide, bf16), (tall, bf16)]
    vmem = [pltpu.VMEM(*a) for a in kept]
    return pl.pallas_call(
        lambda *refs: ffn_body(groups, *refs),
        grid=(1 + tiles,),
        in_specs=[SMEM, once(length, width), once(length, width), once(1, width), ANY]
        + [s for g in groups for s in g.specs()],
        out_specs=[col, col, col, grad_cols, grad_cols, grad_rows] + [ANY] * 7,
        out_shape=[
            shape((length, hidden)),
            shape((length, hidden)),
            shape((length, hidden)),
            shape((4, 4, hidden // L, G, L)),
            shape((4, 4, hidden // L, G, L)),
            shape((hidden // G, 4, G, L)),
        ]
        + [shape(*a) for a in kept],
        scratch_shapes=vmem[3:]
        + [
            vmem[0],
            pltpu.VMEM((length, width), bf16),
            vmem[1],
            vmem[2],
            pltpu.VMEM((length, width), bf16),
            pltpu.VMEM((length, width // 2), bf16),
            pltpu.VMEM((width // 2, length), bf16),
            pltpu.SemaphoreType.DMA((12,)),
        ],
        compiler_params=params(),
        cost_estimate=cost(46),
        name="ffn",
    )(pos, x, o, gain, df, *[a for g in groups for a in g.arrays])


def ffn_back_body(gain_ref, keep_ref, r1_hbm, df_hbm, wo_hbm, dg_hbm, du_hbm, wg_hbm, wu_hbm,
                  dr_out, da_out, do_out, r1, df, wo, dg, du, wg, wu, acc, da, do, sem):
    length, width = r1.shape
    chunks = chunked(wg.shape[0], 6)
    loads = []
    for i, (low, size) in enumerate(chunks):
        cols = pl.ds(low * L, size * L)
        loads.append(
            [
                pltpu.make_async_copy(a.at[:, cols] if flat else a.at[pl.ds(low, size)],
                                      b.at[:, cols] if flat else b.at[pl.ds(low, size)], sem.at[i])
                for a, b, flat in ((dg_hbm, dg, 1), (wg_hbm, wg, 0), (du_hbm, du, 1), (wu_hbm, wu, 0))
            ]
        )
    last = [pltpu.make_async_copy(a, b, sem.at[len(chunks) + i]) for i, (a, b) in
            enumerate(((r1_hbm, r1), (df_hbm, df), (wo_hbm, wo)))]
    for copies in loads + [last]:
        for c in copies:
            c.start()
    for (low, size), copies in zip(chunks, loads):
        for c in copies:
            c.wait()
        both = jnp.concatenate([a[:, low * L : (low + size) * L] for a in (dg, du)], 1)
        for n in range(width // QB):
            rows = slice(n * QB // G, (n + 1) * QB // G)
            w = jnp.concatenate(
                [a[low + c, rows].reshape(QB, L) for a in (wg, wu) for c in range(size)], 1
            )
            part = nt(both, w)
            if low == 0:
                acc[:, n * QB : (n + 1) * QB] = part
            else:
                acc[:, n * QB : (n + 1) * QB] += part
    for c in last:
        c.wait()
    w = jnp.concatenate([two(wo, c) for c in range(wo.shape[0] // 2)], 1)
    out = []
    for i in range(length // QB):
        rows = slice(i * QB, (i + 1) * QB)
        r = r1[rows, :]
        rinv = lax.rsqrt(jnp.mean(r * r, -1, keepdims=True) + EPS)
        n2 = r * rinv
        dn = acc[rows, :] * gain_ref[...]
        dr = df[rows, :].astype(f32) + rinv * (dn - n2 * jnp.mean(dn * n2, -1, keepdims=True))
        acc[rows, :] = dr
        da[rows, :] = dr.astype(bf16)
        do[rows, :] = (nt(da[rows, :], w) * keep_ref[rows, :]).astype(bf16)
        for k, (a, b) in enumerate(((acc, dr_out), (da, da_out), (do, do_out))):
            c = pltpu.make_async_copy(
                a.at[pl.ds(i * QB, QB)], b.at[pl.ds(i * QB, QB)], sem.at[len(chunks) + 3 + 3 * i + k]
            )
            c.start()
            out.append(c)
    for c in out:
        c.wait()


def ffn_back(r1, df, keep_col, gain, dgate, dup, wo, wg, wu):
    length, width = r1.shape
    hidden = dgate.shape[1]
    vmem = pl.BlockSpec(memory_space=pltpu.VMEM)

    return pl.pallas_call(
        ffn_back_body,
        in_specs=[vmem, vmem] + [ANY] * 7,
        out_specs=[ANY] * 3,
        out_shape=[shape((length, width), f32), shape((length, width)), shape((length, width))],
        scratch_shapes=[like(a) for a in (r1, df, wo, dgate, dup, wg, wu, r1, df, df)]
        + [pltpu.SemaphoreType.DMA((7 + 3 * (length // QB),))],
        compiler_params=params(),
        cost_estimate=cost(22),
        name="ffn_back",
    )(gain, keep_col, r1, df, wo, dgate, dup, wg, wu)


def bits(pos):
    d = pos[1]
    return lax.rem(d, 2), lax.rem(d // 2, 2), lax.rem(d // 4, 2)


def sort_out(out, by_x, value, at, own):
    n = value.shape[1]
    for p in range(4):
        bit, other = (p % 2, p // 2) if by_x else (p // 2, p % 2)
        which = jnp.where(own == bit, 0, 1)
        out[which, other, pl.ds(at, n)] = value[p]


def ffn_grads_body(pos, ht_hbm, df_hbm, hid_hbm, dg_hbm, du_hbm, rg_hbm, ru_hbm, rd_hbm,
                   ka_out, ta_out, kb_out, tb_out,
                   ht, df, hid, dg, du, rg, ru, rd, out_a, out_b, sem):
    core, b1, b2 = bits(pos)
    blocks = rg.shape[2]
    chunks = chunked(blocks, 8)
    first = [pltpu.make_async_copy(ht_hbm.at[:, core], ht, sem.at[0])]
    for p in range(4):
        cols = pl.ds(pl.multiple_of((2 * p + core) * L, L), L)
        first.append(pltpu.make_async_copy(df_hbm.at[:, cols], df.at[:, pl.ds(p * L, L)], sem.at[1 + p]))
    at = 5
    loads = {}
    for name, a, b, ra, rb in (("g", dg_hbm, dg, rg_hbm, rg), ("u", du_hbm, du, ru_hbm, ru), ("d", hid_hbm, hid, rd_hbm, rd)):
        for low, size in chunks:
            cols = pl.ds(low * L, size * L)
            if name == "d":
                some = pl.ds(4 * low, 4 * size)
                pair = (ra.at[some], rb.at[some])
            else:
                some = pl.ds(low, size)
                pair = (ra.at[:, :, some], rb.at[:, :, some])
            loads[name, low] = [
                pltpu.make_async_copy(a.at[:, cols], b.at[:, cols], sem.at[at]),
                pltpu.make_async_copy(*pair, sem.at[at + 1]),
            ]
            at += 2
    for c in first:
        c.start()
    for copies in loads.values():
        for c in copies:
            c.start()
    for c in first:
        c.wait()
    left = ht[...].reshape(ht.shape[0] * G, ht.shape[2])
    targets = ((out_a, ka_out, ta_out), (out_b, kb_out, tb_out))
    sent = []

    def send(which, low, size):
        o, *refs = targets[which]
        some = pl.ds(low, size)
        for i, ref in enumerate(refs):
            sent.append(pltpu.make_async_copy(o.at[i, :, some], ref.at[:, some], sem.at[56 + len(sent)]))
            sent[-1].start()

    for name, grad, got, out, by_x, own in (("g", dg, rg, out_a, True, b1), ("u", du, ru, out_b, False, b2)):
        for low, size in chunks:
            for c in loads[name, low]:
                c.wait()
            g = nn(left, grad[:, low * L : (low + size) * L])
            for s in range(4):
                rows = g[s * 4 * G : (s + 1) * 4 * G].reshape(4, G, size * L)
                value = jnp.stack([rows[:, :, c * L : (c + 1) * L] for c in range(size)], 1)
                value = (value + got[s, :, low : low + size].astype(f32)).astype(bf16)
                sort_out(out, by_x, value, s * blocks + low, own)
        send(0 if by_x else 1, 0, 4 * blocks)
    right = df[...]
    for low, size in chunks:
        for c in loads["d", low]:
            c.wait()
        g = tn(hid[:, low * L : (low + size) * L], right)
        n = 4 * size
        value = jnp.stack([g[:, p * L : (p + 1) * L].reshape(n, G, L) for p in range(4)], 0)
        value = value + jnp.stack([rd[4 * low : 4 * low + n, p].astype(f32) for p in range(4)], 0)
        value = value.astype(bf16)
        edge = min(max(2 * blocks - 4 * low, 0), n)
        if edge:
            sort_out(out_a, True, value[:, :edge], 4 * blocks + 4 * low, b1)
        if edge < n:
            sort_out(out_b, False, value[:, edge:], 4 * blocks + 4 * low + edge - 2 * blocks, b2)
    send(0, 4 * blocks, 2 * blocks)
    send(1, 4 * blocks, 2 * blocks)
    for c in sent:
        c.wait()


def ffn_grads(pos, ht, df, hid, dgate, dup, got):
    length, width = df.shape
    hidden = hid.shape[1]
    half = shape((2, 6 * hidden // L, G, L))
    return pl.pallas_call(
        ffn_grads_body,
        in_specs=[SMEM] + [ANY] * 8,
        out_specs=[ANY] * 4,
        out_shape=[half] * 4,
        scratch_shapes=[
            pltpu.VMEM((ht.shape[0], G, length), bf16),
            pltpu.VMEM((length, width // 2), bf16),
        ]
        + [like(a) for a in (hid, dgate, dup, *got)]
        + [pltpu.VMEM((2,) + half.shape, bf16)] * 2
        + [pltpu.SemaphoreType.DMA((64,))],
        compiler_params=params(),
        cost_estimate=cost(17),
        name="ffn_grads",
    )(pos, ht, df, hid, dgate, dup, *got)


def ffn_out_body(r1_ref, hid_ref, wd, out_ref):
    out_ref[...] = (r1_ref[...] + nn(hid_ref[...], two(wd, 0))).astype(bf16)


def ffn_out(r1, hid, wd):
    length, width = r1.shape
    hidden = hid.shape[1]
    col = pl.BlockSpec((length, 2 * L), lambda i: (0, i))
    return pl.pallas_call(
        ffn_out_body,
        grid=(width // (2 * L),),
        in_specs=[col, once(length, hidden), pl.BlockSpec((2, hidden // G, G, L), lambda i: (i, 0, 0, 0))],
        out_specs=col,
        out_shape=shape((length, width)),
        compiler_params=params(),
        cost_estimate=cost(11),
        name="ffn_out",
    )(r1, hid, wd)


def square_body(keep, pos, ot_hbm, ht_hbm, *rest):
    grads_hbm, rest = rest[:4], rest[4:]
    if keep:
        got_hbm, ka_out, ta_out, kb_out, tb_out, ot, ht, da, dq, dk, dv, got, out_a, out_b, sem = rest
    else:
        out_hbm, ot, ht, da, dq, dk, dv, out, sem = rest
    core, b1, b2 = bits(pos)
    grads = (da, dq, dk, dv)
    mine = core if keep else 1 - core
    blocks = da.shape[1] // L
    loads = [pltpu.make_async_copy(a, b, sem.at[i]) for i, (a, b) in enumerate(zip(grads_hbm, grads))]
    lefts = [pltpu.make_async_copy(a.at[:, mine], b, sem.at[4 + i]) for i, (a, b) in enumerate(((ot_hbm, ot), (ht_hbm, ht)))]
    recv = []
    if keep:
        for i in range(4):
            some = pl.ds(i * blocks, blocks)
            recv.append(pltpu.make_async_copy(got_hbm.at[:, :, some], got.at[:, :, some], sem.at[6 + i]))
            recv[i].start()
    lefts[0].start()
    loads[0].start()
    lefts[1].start()
    for c in loads[1:]:
        c.start()
    sent = []

    def send(a, b):
        sent.append(pltpu.make_async_copy(a, b, sem.at[10 + len(sent)]))
        sent[-1].start()

    for i in range(4):
        if i < 2:
            lefts[i].wait()
        loads[i].wait()
        if keep:
            recv[i].wait()
        ref = (ot, ht, ht, ht)[i]
        left = ref[...].reshape(ref.shape[0] * G, ref.shape[2])
        for low, size in chunked(blocks, 4):
            g = nn(left, grads[i][:, low * L : (low + size) * L])
            for s in range(4):
                rows = g[s * 4 * G : (s + 1) * 4 * G].reshape(4, G, size * L)
                value = jnp.stack([rows[:, :, c * L : (c + 1) * L] for c in range(size)], 1)
                at = i * blocks + low
                if not keep:
                    out[s, :, at : at + size] = value.astype(bf16)
                    continue
                value = (value + got[s, :, at : at + size].astype(f32)).astype(bf16)
                at = s * 2 * blocks + (i % 2) * blocks + low
                sort_out(out_a if i < 2 else out_b, i < 2, value, at, b1 if i < 2 else b2)
        if not keep:
            some = pl.ds(i * blocks, blocks)
            send(out.at[:, :, some], out_hbm.at[:, :, some])
        elif i == 1:
            send(out_a.at[0], ka_out)
            send(out_a.at[1], ta_out)
        elif i == 3:
            send(out_b.at[0], kb_out)
            send(out_b.at[1], tb_out)
    for c in sent:
        c.wait()


def square_grads(pos, ot, ht, grads, got):
    length, width = grads[0].shape
    whole = shape((4, 4, 4 * width // L, G, L))
    half = shape((2, 8 * width // L, G, L))
    keep = got is not None
    left = pltpu.VMEM((ht.shape[0], G, length), bf16)
    return pl.pallas_call(
        lambda *refs: square_body(keep, *refs),
        in_specs=[SMEM] + [ANY] * (7 if keep else 6),
        out_specs=[ANY] * 4 if keep else ANY,
        out_shape=[half] * 4 if keep else whole,
        scratch_shapes=[left, left]
        + [like(a) for a in grads]
        + ([like(whole)] + [pltpu.VMEM((2,) + half.shape, bf16)] * 2 if keep else [like(whole)])
        + [pltpu.SemaphoreType.DMA((14,))],
        compiler_params=params(),
        cost_estimate=cost(10),
        name="square_keep" if keep else "square_send",
    )(pos, ot, ht, *grads, *([got] if keep else []))


def input_grad_body(x_ref, gain_ref, dq_hbm, dk_hbm, dv_hbm, wq_hbm, wk_hbm, wv_hbm, dr_hbm, out_hbm,
                    dq, dk, dv, wq, wk, wv, dr, acc, sem):
    length, width = x_ref.shape
    blocks = width // L
    pairs = ((dq_hbm, dq, wq_hbm, wq), (dk_hbm, dk, wk_hbm, wk), (dv_hbm, dv, wv_hbm, wv))
    loads = [
        (pltpu.make_async_copy(a, b, sem.at[2 * i]), pltpu.make_async_copy(c, d, sem.at[2 * i + 1]))
        for i, (a, b, c, d) in enumerate(pairs)
    ]
    get_dr = pltpu.make_async_copy(dr_hbm, dr, sem.at[6])
    for pair in loads:
        for c in pair:
            c.start()
    get_dr.start()
    for i, (_, grad, _, w) in enumerate(pairs):
        for c in loads[i]:
            c.wait()
        for n in range(width // QB):
            rows = slice(n * QB // G, (n + 1) * QB // G)
            part = nt(grad[...], jnp.concatenate([w[c, rows].reshape(QB, L) for c in range(blocks)], 1))
            if i == 0:
                acc[:, n * QB : (n + 1) * QB] = part
            else:
                acc[:, n * QB : (n + 1) * QB] += part
    get_dr.wait()
    out = []
    for i in range(length // QB):
        rows = slice(i * QB, (i + 1) * QB)
        x = x_ref[rows, :].astype(f32)
        rinv = lax.rsqrt(jnp.mean(x * x, -1, keepdims=True) + EPS)
        n1 = x * rinv
        dn = acc[rows, :] * gain_ref[...]
        acc[rows, :] = dr[rows, :] + rinv * (dn - n1 * jnp.mean(dn * n1, -1, keepdims=True))
        out.append(pltpu.make_async_copy(acc.at[pl.ds(i * QB, QB)], out_hbm.at[pl.ds(i * QB, QB)], sem.at[7 + i]))
        out[-1].start()
    for c in out:
        c.wait()


def input_grad(x, gain, dr1, dq, dk, dv, weights):
    length, width = x.shape
    vmem = pl.BlockSpec(memory_space=pltpu.VMEM)
    return pl.pallas_call(
        input_grad_body,
        in_specs=[vmem, vmem] + [ANY] * 7,
        out_specs=ANY,
        out_shape=shape((length, width), f32),
        scratch_shapes=[like(a) for a in (dq, dk, dv, *weights, dr1, dr1)]
        + [pltpu.SemaphoreType.DMA((7 + length // QB,))],
        compiler_params=params(),
        cost_estimate=cost(14),
        name="input_grad",
    )(x, gain, dq, dk, dv, *weights, dr1)


def place_body(tall, pos, *refs):
    pieces, outs = refs[:10], refs[10:]
    blocks = []
    for which, out in enumerate(outs[:-3] if tall else outs):
        blocks += [(which, c) for c in range(out.shape[1] // L)]
    if tall:
        blocks += [(len(outs) - 3, j) for j in range(outs[-3].shape[0] // G)] + [(None, 0)]
    d = pos[1]
    for array, mask, low, size in piece_sources(pieces[0].shape[1]):
        piece = d ^ mask
        rows = pl.ds(pl.multiple_of(piece * G, G), G)
        cols = pl.ds(pl.multiple_of(piece * L, L), L)
        for c in range(size):
            which, at = blocks[low + c]
            value = pieces[array][0, c].astype(f32)
            if which is None:
                outs[-1][piece] = value
            elif tall and which == len(outs) - 3:
                outs[which][at * G : (at + 1) * G, cols] = value
            else:
                outs[which][rows, at * L : (at + 1) * L] = value
    if tall:
        total = outs[-1][0]
        for piece in range(1, 8):
            total = total + outs[-1][piece]
        outs[-2][...] = total


def place(pos, arrays, widths, rows, tall=None):
    vmem = pl.BlockSpec(memory_space=pltpu.VMEM)
    outs = [shape((rows, w), f32) for w in widths]
    if tall is not None:
        outs += [shape(tall, f32), shape((G, L), f32)]
    return pl.pallas_call(
        lambda *refs: place_body(tall is not None, *refs),
        in_specs=[SMEM] + [vmem] * 10,
        out_specs=[vmem] * len(outs),
        out_shape=outs,
        scratch_shapes=[] if tall is None else [pltpu.VMEM((8, G, L), f32)],
        compiler_params=params(),
        cost_estimate=cost(5),
        name="place",
    )(pos, *arrays)


def layout(lengths, length):
    position = jnp.arange(length, dtype=jnp.int32)
    ends = jnp.cumsum(lengths).astype(jnp.int32)
    seg = jnp.sum((position[:, None] >= ends[None, :]).astype(jnp.int32), 1)
    onehot = seg[:, None] == jnp.arange(lengths.shape[0], dtype=jnp.int32)[None, :]
    first = jnp.sum(jnp.where(onehot, (ends - lengths)[None, :], 0), 1)
    rel = (position - first).astype(f32)
    inverse = 10000.0 ** (-jnp.arange(HEAD_DIM // 2, dtype=f32) * 2.0 / HEAD_DIM)
    angle = rel[:, None] * inverse[None, :]
    keep = (seg < lengths.shape[0] - 1).astype(f32)
    cos, sin = jnp.cos(angle), jnp.sin(angle)
    cos_w = jnp.concatenate([cos] * 4, 1)
    sin_w = jnp.concatenate([-sin, sin] * 2, 1)
    return cos_w, sin_w, marks(seg, lengths.shape[0]), keep[:, None]


def add(*terms):
    total = terms[0].astype(f32)
    for t in terms[1:]:
        total = total + t.astype(f32)
    return total


def halve(kept, got, bit):
    picked = []
    for at in (1 - bit, bit):
        parts = [lax.dynamic_index_in_dim(x, at, 0, keepdims=False) for x in (kept, got)]
        picked.append(add(*parts).astype(bf16))
    return picked


def in_parts(sums):
    parts = []
    for _ in range(3):
        part = lax.reduce_precision(sums, 8, 7)
        parts.append(part)
        sums = sums - part
    return jnp.pad(jnp.stack(parts).astype(bf16), ((0, G - 3), (0, L - 2)))


def from_parts(block):
    parts = block[..., :3, :2].astype(f32)
    return parts[..., 0, :] + parts[..., 1, :] + parts[..., 2, :]


def to_shards(total, z, extra=None):
    terms = [lax.dynamic_index_in_dim(total, z, 0, keepdims=False)]
    if extra is not None:
        terms[0] = jnp.concatenate([terms[0], extra[None]])
    for s in (1, 2, 3):
        away = lax.dynamic_index_in_dim(total, lax.rem(z + s, 4), 0, keepdims=False)
        if extra is not None:
            away = jnp.concatenate([away, extra[None]])
        terms.append(fsdp_shift(away, s))
    return terms


def sums_over_fsdp(terms, z):
    numbers = jnp.stack([from_parts(t[-1]) for t in terms])
    sums = jnp.zeros_like(numbers[0])
    for shard in range(4):
        sums = sums + lax.dynamic_index_in_dim(numbers, lax.rem(z + 4 - shard, 4), 0, keepdims=False)
    return sums


def back_over_dp(reduced):
    g = Gather.__new__(Gather)
    g.count, g.start = reduced.shape[0], reduced[None]
    g.x, g.y = dp_swap(g.start, 2), dp_swap(g.start, 4)
    return g


def unfold_rows(w):
    return w.transpose(0, 2, 1, 3).reshape(w.shape[0] * G, w.shape[1] * L)


def sum_whole(grad):
    part = lax.psum_scatter(grad.astype(bf16), "fsdp", scatter_dimension=0, tiled=True)
    return lax.psum(part, "dp").astype(f32)


def local(
    layer_in, first_values, first_values_grad, cotangent, doc_lengths, norm1_gain,
    w_query, w_key, w_value, w_out, norm2_gain, w_gate, w_up, w_down,
):
    rows, length, width = layer_in.shape
    hidden = w_gate.shape[1]
    dp, fsdp = lax.axis_size("dp"), lax.axis_size("fsdp")
    fast = fast_mesh(dp, fsdp, w_query.shape[0])
    z, d = lax.axis_index("fsdp"), lax.axis_index("dp")
    b1, b2 = lax.rem(d // 2, 2), lax.rem(d // 4, 2)
    x, v1 = layer_in[0], first_values[0]
    df = cotangent[0]
    gains = jnp.stack([norm1_gain, norm2_gain])
    c, h = width // L, hidden // L
    members = (
        ((w_query, w_key, w_value), ((c, True),) * 3),
        ((w_out, w_gate), ((c, True), (h, True))),
        ((w_up, w_down), ((h, True), (w_down.shape[0] // G, False))),
    )
    if fast:
        pos = jnp.stack([z, d]).astype(jnp.int32)
        extra = jnp.pad(gains.reshape(-1, L), ((0, G - gains.size // L), (0, 0)))
        g1 = Gather(cut(pos, *members[0], extra), True)
        far = jnp.stack([e[: gains.size // L].reshape(gains.shape) for e in g1.extras])
        mines = [cut(after(pos, g1.extras[0]), *m) for m in members[1:]]
        g1.near()
        g2 = Gather(after(mines[0], g1.start))
        g1.corner(g2.far[0], g2.far[2])
        g2.near(g1.c1, g1.c2)
        g3 = Gather(after(mines[1], g2.start))
        g1.core()
        g1.core_corner()
        groups = [Group(members[0][1], members[0][0], g1.arrays(), False)]
        whole_gains = jnp.concatenate(
            [lax.dynamic_index_in_dim(far, lax.rem(z + 4 - j, 4), 0, keepdims=False) for j in range(4)], 1
        )
    else:
        pos = jnp.zeros((2,), jnp.int32)

        def blocks(w, by_rows):
            full = lax.all_gather(w, "fsdp", axis=0, tiled=True)
            return row_pieces(full, full.shape[0] // G).transpose(1, 0, 2, 3) if by_rows else column_pieces(full, c)

        whole_gains = lax.all_gather(gains, "fsdp", axis=1, tiled=True)
        groups = [
            Group(tensors, [], [blocks(w, t[1]) for w, t in zip(weights, tensors)], True)
            for weights, tensors in members
        ]
    whole_gains = whole_gains.astype(f32)
    gain_1, gain_2 = whole_gains[:1], whole_gains[1:]
    cos_w, sin_w, mark, keep_col = layout(doc_lengths[0], length)

    q, k, vm, h1t, sums, wq, wk, wv = qkv(pos, x, v1, gain_1, cos_w, sin_w, groups[0])
    squares = jnp.sum(sums, (1, 2))
    entries = rows * length * width * dp * fsdp
    if fast:
        g2.corner(q)
        q = after(q, g2.x, g2.y)
    o, lse_1 = attend_fwd(q, k, vm, *mark, keep_col, 0, 3)
    if fast:
        g3.near(o)
        g2.core(o)
        o = after(o, g2.c1, g2.c2, g3.start)
    o, lse_2 = attend_fwd(q, k, vm, *mark, keep_col, 3, 5, o)
    if fast:
        g3.corner(o)
        g2.core_corner(o)
        g3.core(o)
        g3.core_corner()
        groups += [Group(members[i][1], members[i][0], g.arrays(), False) for i, g in ((1, g2), (2, g3))]
    hid, dgate, dup, sg, su, sd, r1, h2t, ot, wo, wg, wu, wd = ffn(pos, x, o, df, gain_2, groups[1:], hidden)
    got = [dp_swap(g, 1) if fast else jnp.zeros_like(g) for g in (sg, su, sd)]
    out = ffn_out(r1, hid, wd)
    ka, ta, kb, tb = ffn_grads(pos, h2t, df, hid, dgate, dup, after(got, out))
    if fast:
        na, nb = dp_swap(ta, 2), dp_swap(tb, 4)
        dgate = after(dgate, ta)
    dr1, da, do = ffn_back(r1, df, keep_col, gain_2, dgate, dup, wo, wg, wu)
    back = (*mark, cos_w, -sin_w, first_values_grad[0])
    results = attend_bwd(q, k, vm, do, lse_2.T, *back, 3, 5)
    if fast:
        na, nb = after((na, nb), results)
        ta, ka = halve(ka, na, b2)
        tb, kb = halve(kb, nb, b1)
        ma, mb = dp_swap(ta, 4), dp_swap(tb, 2)
        results = after(results, ta, tb)
    dq, dk, dv, first_out = attend_bwd(q, k, vm, do, lse_1.T, *back, 0, 3, results)
    grads = (da, dq, dk, dv)
    if fast:
        grads = after(grads, ma, mb)
    send = square_grads(pos, ot, h1t, grads, None)
    swapped = dp_swap(send, 1) if fast else jnp.zeros_like(send)
    if fast:
        ma, mb = after((ma, mb), send)
        total_a, total_b = add(ka, ma).astype(bf16), add(kb, mb).astype(bf16)
        n = 4 * hidden // L
        cols_a, cols_b = [t[:n].reshape(4, n // 4, G, L) for t in (total_a, total_b)]
        cols_d = jnp.concatenate([total_a[n:], total_b[n:]]).reshape(4, n // 4, G, L)
        wide_terms = to_shards(jnp.concatenate([cols_a, cols_b, cols_d], 1), z, in_parts(squares))
        swapped = after(swapped, wide_terms[0])
    ks, ts, kt, tt = square_grads(pos, ot, h1t, grads, swapped)
    if fast:
        ns, n_t = dp_swap(ts, 2), dp_swap(tt, 4)
    d_x = input_grad(after(x, ts), gain_1, dr1, dq, dk, dv, (wq, wk, wv))
    if fast:
        ns, n_t = after((ns, n_t), d_x)
        ts, ks = halve(ks, ns, b2)
        tt, kt = halve(kt, n_t, b1)
        ms, mt = dp_swap(ts, 4), dp_swap(tt, 2)
        ms, mt, wide_terms = after((ms, mt, wide_terms), ts)
        total_s, total_t = add(ks, ms).astype(bf16), add(kt, mt).astype(bf16)
        both = [t.reshape((4, -1) + t.shape[1:]) for t in (total_s, total_t)]
        last_terms = to_shards(jnp.concatenate(both, 1), z)
        wide_terms = after(wide_terms, *both)
        reduced = add(*[t[:-1] for t in wide_terms]).astype(bf16)
        wide = back_over_dp(jnp.concatenate([reduced, in_parts(sums_over_fsdp(wide_terms, z))[None]]))
        wide.corner()
        last = back_over_dp(after(add(*last_terms).astype(bf16), wide.c1, wide.c2))
        wide.core()
        wide.core_corner()
        last.corner(*wide.other)
        grad_wg, grad_wu, grad_wd, squares = place(
            pos, wide.arrays(), [hidden] * 2, w_query.shape[0], (w_down.shape[0], width)
        )
        squares = from_parts(squares)
        last.core()
        last.core_corner()
        grad_wo, grad_wq, grad_wk, grad_wv = place(pos, last.arrays(), [width] * 4, w_query.shape[0])
    else:
        squares = lax.psum(squares, ("dp", "fsdp"))
        n = 4 * hidden // L
        even_a, even_b = jnp.stack([ka, ta], 1), jnp.stack([kb, tb], 0)
        even_a, even_b = [e.reshape((4,) + ka.shape[1:]) for e in (even_a, even_b)]
        grad_wg, grad_wu = join(even_a[:, :n], sg), join(even_b[:, :n], su)
        even_d = jnp.concatenate([even_a[:, n:], even_b[:, n:]], 1).transpose(1, 0, 2, 3)
        grad_wd = jnp.stack([even_d, sd], 2).reshape(n, 8, G, L).transpose(0, 2, 1, 3).reshape(hidden, width)
        n = 2 * width // L
        even_s, even_t = jnp.stack([ks, ts], 1), jnp.stack([kt, tt], 0)
        firsts = join(even_s.reshape((4,) + ks.shape[1:]), send[:, :, :n])
        seconds = join(even_t.reshape((4,) + ks.shape[1:]), send[:, :, n:])
        grad_wo, grad_wq = firsts[:, :width], firsts[:, width:]
        grad_wk, grad_wv = seconds[:, :width], seconds[:, width:]
        grad_wo, grad_wq, grad_wk, grad_wv, grad_wg, grad_wu, grad_wd = [
            sum_whole(g) for g in (grad_wo, grad_wq, grad_wk, grad_wv, grad_wg, grad_wu, grad_wd)
        ]
    def along(*pairs):
        return sum(jnp.sum(w.astype(f32) * g, 1) for w, g in pairs)

    grad_g1 = along((w_query, grad_wq), (w_key, grad_wk), (w_value, grad_wv)) / norm1_gain.astype(f32)
    grad_g2 = along((w_gate, grad_wg), (w_up, grad_wu)) / norm2_gain.astype(f32)
    return (
        out[None], d_x[None], first_out[None], grad_g1, grad_wq, grad_wk, grad_wv, grad_wo, grad_g2,
        grad_wg, grad_wu, grad_wd, squares / entries,
    )


def join(even, odd):
    even = even.reshape((4, 4, -1) + even.shape[2:]).transpose(1, 0, 2, 3, 4)
    both = jnp.stack([even, odd], 2)
    return unfold_rows(both.reshape((32,) + odd.shape[2:]))


def solution(mesh):
    by_row = P(("dp", "fsdp"), None, None)
    shard = P("fsdp", None)
    return jax.shard_map(
        local,
        mesh=mesh,
        in_specs=(by_row,) * 4
        + (P(("dp", "fsdp"), None), P("fsdp"), shard, shard, shard, shard, P("fsdp"), shard, shard, shard),
        out_specs=(by_row,) * 3
        + (P("fsdp"), shard, shard, shard, shard, P("fsdp"), shard, shard, shard, P()),
        check_vma=False,
    )
```
